32 devices in a mesh: dp: 8 (over z, y), seq: 4 (over x, core).
Axes of the slice: x: 2, y: 2, z: 4, core: 2. Of those that a mesh axis runs over, the one named last changes fastest.
Arguments:
- table_master: float32 [5000, 256], P(None, 'dp'), may hold values from -0.375 to 0.375
- inward_master: float32 [6, 256, 256], P(None, 'dp'), may hold values from -0.375 to 0.375
- outward_master: float32 [2, 256, 256], P(None, 'dp'), may hold values from -2 to 2
- expand_master: float32 [256, 2048], P('dp'), may hold values from -0.375 to 0.375
- shrink_master: float32 [2048, 256], P('dp'), may hold values from -0.125 to 0.125
- norms_master: float32 [6, 256], P(None, 'dp'), may hold values from -1.2 to 5, as said below
- table_first: float32 [5000, 256], P(None, 'dp'), may hold values from -1 to 1
- inward_first: float32 [6, 256, 256], P(None, 'dp'), may hold values from -1 to 1
- outward_first: float32 [2, 256, 256], P(None, 'dp'), may hold values from -1 to 1
- expand_first: float32 [256, 2048], P('dp'), may hold values from -0.25 to 0.25
- shrink_first: float32 [2048, 256], P('dp'), may hold values from -1 to 1
- norms_first: float32 [6, 256], P(None, 'dp'), may hold values from -1 to 1
- table_second: float32 [5000, 256], P(None, 'dp'), may hold values from 0.015765134 to 0.12612107
- inward_second: float32 [6, 256, 256], P(None, 'dp'), may hold values from 0.015765134 to 0.12612107
- outward_second: float32 [2, 256, 256], P(None, 'dp'), may hold values from 0.015765134 to 0.12612107
- expand_second: float32 [256, 2048], P('dp'), may hold values from 0.0009853209 to 0.007882567
- shrink_second: float32 [2048, 256], P('dp'), may hold values from 0.015765134 to 0.12612107
- norms_second: float32 [6, 256], P(None, 'dp'), may hold values from 0.015765134 to 0.12612107
- memory: bfloat16 [256, 712, 256], P('dp', 'seq'), may hold values from -6 to 6
- token_ids: int32 [256, 128], P(('dp', 'seq')), may hold values from 0 to 4999
- dec_segments: int32 [256, 128], P(('dp', 'seq')), may hold values from 0 to 3, never falling along the last dimension, each value on 1 to 48 neighbouring positions
- mem_segments: int32 [256, 712], P(('dp', 'seq')), may hold values from 0 to 3, never falling along the last dimension, each value on 1 to 267 neighbouring positions
- cotangent: bfloat16 [256, 128, 256], P(('dp', 'seq')), may hold values from -6 to 6
Outputs:
- block_out: bfloat16 [256, 128, 256], P(('dp', 'seq'))
- memory_grad: bfloat16 [256, 712, 256], P('dp', 'seq')
- grad_norm: float32 [], replicated
- table_grad: float32 [5000, 256], P(None, 'dp')
- table_moment: float32 [5000, 256], P(None, 'dp')
- table_square: float32 [5000, 256], P(None, 'dp')
- table_weight: float32 [5000, 256], P(None, 'dp')
- table_copy: bfloat16 [5000, 256], P(None, 'dp')
- inward_grad: float32 [6, 256, 256], P(None, 'dp')
- inward_moment: float32 [6, 256, 256], P(None, 'dp')
- inward_square: float32 [6, 256, 256], P(None, 'dp')
- inward_weight: float32 [6, 256, 256], P(None, 'dp')
- inward_copy: bfloat16 [6, 256, 256], P(None, 'dp')
- outward_grad: float32 [2, 256, 256], P(None, 'dp')
- outward_moment: float32 [2, 256, 256], P(None, 'dp')
- outward_square: float32 [2, 256, 256], P(None, 'dp')
- outward_weight: float32 [2, 256, 256], P(None, 'dp')
- outward_copy: bfloat16 [2, 256, 256], P(None, 'dp')
- expand_grad: float32 [256, 2048], P('dp')
- expand_moment: float32 [256, 2048], P('dp')
- expand_square: float32 [256, 2048], P('dp')
- expand_weight: float32 [256, 2048], P('dp')
- expand_copy: bfloat16 [256, 2048], P('dp')
- shrink_grad: float32 [2048, 256], P('dp')
- shrink_moment: float32 [2048, 256], P('dp')
- shrink_square: float32 [2048, 256], P('dp')
- shrink_weight: float32 [2048, 256], P('dp')
- shrink_copy: bfloat16 [2048, 256], P('dp')
- norms_grad: float32 [6, 256], P(None, 'dp')
- norms_moment: float32 [6, 256], P(None, 'dp')
- norms_square: float32 [6, 256], P(None, 'dp')
- norms_weight: float32 [6, 256], P(None, 'dp')
- norms_copy: bfloat16 [6, 256], P(None, 'dp')
The draws below stay inside these ranges and needn't reach their ends.
Inputs may be any that keep to these rules, and one draw needn't show every extreme that they name: `dec_segments`: numbers never fall along a row and each of the 4 numbers occurs in every row. `mem_segments`: numbers never fall along a row and each of the 4 numbers occurs in every row; utterance j of a memory row belongs to utterance j of the decoder row of the same index. `norms_master`: rows 0, 2, 4 are positive gains, rows 1, 3, 5 shifts.
All inputs are finite; a program needn't handle non-finite values.
Results may differ from the reference program's by a relative error of at most 0.014.
The reference program's roundings to bfloat16 on the way count: a program that leaves them out, or rounds other values in their place, can miss the bound.
Values may be sent and summed in bfloat16 or wider, within the bound.
No kernel may reach another device: no remote copies, remote signals or barrier semaphores. Data moves between devices by JAX's collectives and lax.ppermute only.
A program may use at most 128 MiB of HBM per device.

```python
import math
import jax
import jax.numpy as jnp
import numpy as np
from jax import lax

D = 256
HEADS = 4
FF = 2048
VOCAB = 5000
DLEN = 128
FRAMES = 712
DSEGS = 4
STEP = 5
ROWS = 256
NPARAM = 2854400


def draw_norms_master(key, part):
    column = jnp.arange(D, dtype=jnp.float32) / D
    first_key, second_key = jax.random.split(jax.random.fold_in(key, 11))
    spread = jax.random.uniform(first_key, (3, D), jnp.float32, 0.6, 1.4)
    ramp = 0.6 + 1.2 * column
    gains = spread * ramp[None, :]
    shifts = jnp.clip(0.3 * jax.random.normal(second_key, (3, D), jnp.float32), -1.2, 1.2)
    return jnp.stack([gains, shifts], 1).reshape(6, D).astype(jnp.float32)


def set_ends(values, rng, low, high):
    spot = [jax.random.randint(jax.random.fold_in(rng, axis), (), 0, length) for axis, length in enumerate(values.shape)]
    widest = values.shape.index(max(values.shape))
    next_to = spot[:widest] + [(spot[widest] + 1) % values.shape[widest]] + spot[widest + 1:]
    return values.at[tuple(spot)].set(low).at[tuple(next_to)].set(high)


def shard_levels(stream_key, dims, shards, smallest, top_value):
    def one(axis_at, shards_of):
        heights = jax.random.uniform(jax.random.fold_in(jax.random.fold_in(stream_key, 6), axis_at), (shards_of,), jnp.float32, smallest / len(shards), top_value / len(shards))
        return jnp.repeat(jnp.exp(heights), dims[axis_at] // shards_of).reshape((-1,) + (1,) * (len(dims) - axis_at - 1))

    factor_of = one(*shards[0])
    for cut in shards[1:]:
        factor_of = factor_of * one(*cut)
    return factor_of


def cumulative_ranks(count, lean):
    loads = [(1 << 20) // math.isqrt(grade ** lean) + 1 for grade in range(1, count + 1)]
    scale = 1 + sum(loads) // (1 << 30)
    return np.cumsum(np.array([max(1, weight // scale) for weight in loads]))


def ranked_ids(stream_key, shape, count, skew):
    listing = cumulative_ranks(count, skew)
    pick = jax.random.randint(jax.random.fold_in(stream_key, 1), shape, 0, int(listing[count - 1]))
    rank = jnp.searchsorted(jnp.asarray(listing, jnp.int32), pick, side="right")
    return jax.random.permutation(jax.random.fold_in(stream_key, 2), count)[rank].astype(jnp.int32)


def length_profile(number_of, total, reach, skew):
    loads = [(1 << 20) // math.isqrt(grade ** skew) + 1 for grade in range(2, number_of + 1)]
    surplus, counts = total - reach - (number_of - 1), [1] * (number_of - 1)
    while surplus > 0:
        free = [i for i in range(number_of - 1) if counts[i] < reach]
        whole, budget = sum([loads[i] for i in free]), surplus
        for i in free:
            addition = min(reach - counts[i], max(1, budget * loads[i] // whole), surplus)
            counts[i] = counts[i] + addition
            surplus = surplus - addition
    return np.array([reach] + counts)


def uneven_parts(rng, count, total, limit, skew):
    if count == 2:
        one = jax.random.randint(rng, (), max(1, total - limit), min(limit, total - 1) + 1)
        return jnp.stack([one, total - one])
    lengths = jnp.asarray(length_profile(count, total, limit, skew), jnp.int32)
    pairs = (count - 1) // 2
    giver, receiver = lengths[1:1 + 2 * pairs:2], lengths[2:2 + 2 * pairs:2]
    room = jnp.minimum(giver - 1, limit - receiver)
    shifted = jax.random.randint(jax.random.fold_in(rng, 1), (pairs,), 0, 1 << 20) % (room + 1)
    lengths = lengths.at[1:1 + 2 * pairs:2].set(giver - shifted).at[2:2 + 2 * pairs:2].set(receiver + shifted)
    return lengths[jax.random.permutation(jax.random.fold_in(rng, 2), count)]


def normal_values(rng, dims, scale, bound, pieces=(), kind=jnp.bfloat16):
    level = shard_levels(rng, dims, pieces, -0.22, 0.18) if pieces else 1.0
    values = jax.random.normal(rng, dims, jnp.float32) * scale * level
    return jnp.minimum(jnp.maximum(values, -bound), bound).astype(kind)


def setup_inputs(seed: int = 0) -> dict:
    key_of = jax.random.split(jax.random.key(seed), 24)
    table_master = normal_values(key_of[0], (VOCAB, D), D ** -0.5, 0.375, ((1, 8),), jnp.float32)
    inward_master = normal_values(key_of[1], (6, D, D), D ** -0.5, 0.375, ((1, 8),), jnp.float32)
    outward_master = normal_values(key_of[2], (2, D, D), (D // 32) ** -0.5, 2.0, ((1, 8),), jnp.float32)
    expand_master = normal_values(key_of[3], (D, FF), D ** -0.5, 0.375, ((0, 8),), jnp.float32)
    shrink_master = normal_values(key_of[4], (FF, D), FF ** -0.5, 0.125, ((0, 8),), jnp.float32)
    norms_master = draw_norms_master(jax.random.fold_in(key_of[23], 71), 0)
    table_first = normal_values(key_of[6], (VOCAB, D), (300 / NPARAM ** 0.5), 1.0, ((1, 8),), jnp.float32)
    inward_first = normal_values(key_of[7], (6, D, D), (300 / NPARAM ** 0.5), 1.0, ((1, 8),), jnp.float32)
    outward_first = normal_values(key_of[8], (2, D, D), (300 / NPARAM ** 0.5), 1.0, ((1, 8),), jnp.float32)
    expand_first = normal_values(key_of[9], (D, FF), (75 / NPARAM ** 0.5), 0.25, ((0, 8),), jnp.float32)
    shrink_first = normal_values(key_of[10], (FF, D), (300 / NPARAM ** 0.5), 1.0, ((0, 8),), jnp.float32)
    norms_first = normal_values(key_of[11], (6, D), (300 / NPARAM ** 0.5), 1.0, ((1, 8),), jnp.float32)
    table_second = jnp.clip(jnp.exp(math.log(0.12612107) - 2.0794415 * jax.random.uniform(key_of[12], (VOCAB, D), jnp.float32) ** shard_levels(key_of[12], (VOCAB, D), ((1, 8),), -0.2, 0.2)), 0.015765134, 0.12612107)
    inward_second = jnp.clip(jnp.exp(math.log(0.12612107) - 2.0794415 * jax.random.uniform(key_of[13], (6, D, D), jnp.float32) ** shard_levels(key_of[13], (6, D, D), ((1, 8),), -0.2, 0.2)), 0.015765134, 0.12612107)
    outward_second = jnp.clip(jnp.exp(math.log(0.12612107) - 2.0794415 * jax.random.uniform(key_of[14], (2, D, D), jnp.float32) ** shard_levels(key_of[14], (2, D, D), ((1, 8),), -0.2, 0.2)), 0.015765134, 0.12612107)
    expand_second = jnp.clip(jnp.exp(math.log(0.007882567) - 2.0794415 * jax.random.uniform(key_of[15], (D, FF), jnp.float32) ** shard_levels(key_of[15], (D, FF), ((0, 8),), -0.2, 0.2)), 0.0009853209, 0.007882567)
    shrink_second = jnp.clip(jnp.exp(math.log(0.12612107) - 2.0794415 * jax.random.uniform(key_of[16], (FF, D), jnp.float32) ** shard_levels(key_of[16], (FF, D), ((0, 8),), -0.2, 0.2)), 0.015765134, 0.12612107)
    norms_second = jnp.clip(jnp.exp(math.log(0.12612107) - 2.0794415 * jax.random.uniform(key_of[17], (6, D), jnp.float32) ** shard_levels(key_of[17], (6, D), ((1, 8),), -0.2, 0.2)), 0.015765134, 0.12612107)
    memory = normal_values(key_of[18], (ROWS, FRAMES, D), 1.0, 6.0, ((0, 8), (1, 4)))
    token_ids = set_ends(ranked_ids(key_of[19], (ROWS, DLEN), VOCAB, 2), jax.random.fold_in(key_of[19], 3), 0, VOCAB - 1).astype(jnp.int32)
    dec_segments = jax.vmap(lambda own: jnp.searchsorted(jnp.cumsum(uneven_parts(own, DSEGS, DLEN, DLEN // DSEGS + DLEN // (2 * DSEGS), 0)), jnp.arange(DLEN), side="right"))(jax.random.split(key_of[20], ROWS)).reshape((ROWS, DLEN)).astype(jnp.int32)
    mem_segments = jax.vmap(lambda own: jnp.searchsorted(jnp.cumsum(uneven_parts(own, DSEGS, FRAMES, FRAMES // DSEGS + FRAMES // (2 * DSEGS), 0)), jnp.arange(FRAMES), side="right"))(jax.random.split(key_of[21], ROWS)).reshape((ROWS, FRAMES)).astype(jnp.int32)
    cotangent = normal_values(key_of[22], (ROWS, DLEN, D), 1.0, 6.0, ((0, 32),))
    return {"table_master": table_master, "inward_master": inward_master, "outward_master": outward_master, "expand_master": expand_master, "shrink_master": shrink_master, "norms_master": norms_master, "table_first": table_first, "inward_first": inward_first, "outward_first": outward_first, "expand_first": expand_first, "shrink_first": shrink_first, "norms_first": norms_first, "table_second": table_second, "inward_second": inward_second, "outward_second": outward_second, "expand_second": expand_second, "shrink_second": shrink_second, "norms_second": norms_second, "memory": memory, "token_ids": token_ids, "dec_segments": dec_segments, "mem_segments": mem_segments, "cotangent": cotangent}


EPS = 1e-05
NEG = -1e+30
CLIP = 300.0
RATE = 0.05
NORM_RATE = 0.3
BETA_ONE = 0.5
BETA_TWO = 0.5
DECAY = 0.01
ADAM_EPS = 1e-08
HIGH = lax.Precision.HIGHEST

@jax.custom_vjp
def low(v):
    return lax.optimization_barrier(v.astype(jnp.bfloat16)).astype(jnp.float32)

@jax.custom_vjp
def low_back(v):
    return v

def low_keep(v):
    return (low(v), None)

def low_pass(kept, grad):
    return (grad,)

def back_keep(v):
    return (v, None)

def back_low(kept, grad):
    return (low(grad),)
low.defvjp(low_keep, low_pass)
low_back.defvjp(back_keep, back_low)

def both_ways(values):
    return low_back(low(values))

def layer_norm(stream, gain, shift):
    center = stream - lax.optimization_barrier(jnp.mean(stream, -1, keepdims=True))
    spread = lax.optimization_barrier(jnp.mean(center * center, -1, keepdims=True))
    return center * lax.rsqrt(spread + EPS) * gain + shift

def gelu_tanh(values):
    return jax.nn.gelu(values, approximate=True)

def positions(segment):
    index = jnp.arange(segment.shape[1], dtype=jnp.int32)[None, :]
    starts = jnp.concatenate([jnp.ones((segment.shape[0], 1), bool), segment[:, 1:] != segment[:, :-1]], 1)
    first = lax.cummax(jnp.where(starts, index, jnp.zeros_like(index)), axis=1)
    return (index - first).astype(jnp.float32)

def encode(place, width):
    halves = jnp.arange(width // 2, dtype=jnp.float32)
    freq = jnp.exp(halves * (-2.0 * math.log(10000.0) / width))
    angle = place[..., None] * freq
    return jnp.stack([jnp.sin(angle), jnp.cos(angle)], -1).reshape(place.shape + (width,))

def split_heads(values):
    return values.reshape(values.shape[0], values.shape[1], HEADS, values.shape[2] // HEADS)

def join_heads(values):
    return values.reshape(values.shape[0], values.shape[1], -1)

def attend(query, keys, values, mask):
    scores = jnp.einsum('rqhe,rkhe->rhqk', query, keys, precision=HIGH)
    scores = low_back(scores)
    scores = jnp.where(mask[:, None], scores, NEG)
    probs = low(jax.nn.softmax(scores, axis=-1))
    return jnp.einsum('rhqk,rkhe->rqhe', probs, values, precision=HIGH)

def forward(params, memory, token_ids, dec_segments, mem_segments):
    table, inward, outward, expand, shrink, norms = [low(weight) for weight in params]
    length = token_ids.shape[1]
    scale = (D // HEADS) ** (-0.5)
    stream0 = D ** 0.5 * low_back(jnp.take(table, token_ids, axis=0)) + encode(positions(dec_segments), D)
    place = jnp.arange(length)
    self_mask = (dec_segments[:, :, None] == dec_segments[:, None, :]) & (place[:, None] >= place[None, :])[None]
    cross_mask = dec_segments[:, :, None] == mem_segments[:, None, :]
    hidden1 = low(layer_norm(stream0, norms[0], norms[1]))
    query = split_heads(both_ways(jnp.matmul(hidden1, inward[0], precision=HIGH) * scale))
    keys = split_heads(both_ways(jnp.matmul(hidden1, inward[1], precision=HIGH)))
    values = split_heads(both_ways(jnp.matmul(hidden1, inward[2], precision=HIGH)))
    context1 = both_ways(join_heads(attend(query, keys, values, self_mask)))
    stream1 = stream0 + low_back(jnp.matmul(context1, outward[0], precision=HIGH))
    hidden2 = low(layer_norm(stream1, norms[2], norms[3]))
    frames = low_back(memory)
    cross_query = split_heads(both_ways(jnp.matmul(hidden2, inward[3], precision=HIGH) * scale))
    cross_keys = split_heads(both_ways(jnp.matmul(frames, inward[4], precision=HIGH)))
    cross_values = split_heads(both_ways(jnp.matmul(frames, inward[5], precision=HIGH)))
    context2 = both_ways(join_heads(attend(cross_query, cross_keys, cross_values, cross_mask)))
    stream2 = stream1 + low_back(jnp.matmul(context2, outward[1], precision=HIGH))
    hidden3 = low(layer_norm(stream2, norms[4], norms[5]))
    before = low_back(jnp.matmul(hidden3, expand, precision=HIGH))
    active = low(gelu_tanh(before))
    return stream2 + low_back(jnp.matmul(active, shrink, precision=HIGH))

def adam_update(master, first, second, gradient, factor, rate):
    clipped = gradient * factor
    moment = BETA_ONE * first + (1 - BETA_ONE) * clipped
    square = BETA_TWO * second + (1 - BETA_TWO) * clipped * clipped
    corrected = moment / (1 - BETA_ONE ** STEP)
    spread = jnp.sqrt(square / (1 - BETA_TWO ** STEP))
    weight = master - rate * (corrected / (spread + ADAM_EPS) + DECAY * master)
    return (clipped, moment, square, weight, weight.astype(jnp.bfloat16))

def reference(table_master, inward_master, outward_master, expand_master, shrink_master, norms_master, table_first, inward_first, outward_first, expand_first, shrink_first, norms_first, table_second, inward_second, outward_second, expand_second, shrink_second, norms_second, memory, token_ids, dec_segments, mem_segments, cotangent):
    params = (table_master, inward_master, outward_master, expand_master, shrink_master, norms_master)
    firsts = (table_first, inward_first, outward_first, expand_first, shrink_first, norms_first)
    seconds = (table_second, inward_second, outward_second, expand_second, shrink_second, norms_second)
    rates = (RATE, RATE, RATE, RATE, RATE, NORM_RATE)
    group = math.gcd(ROWS, 32)
    blocks = ROWS // group

    def one_group(totals, items):
        frames, idents, dsegs, msegs, upstream = items

        def local(weights, mem_values):
            return forward(weights, mem_values, idents, dsegs, msegs)
        result, pull = jax.vjp(local, params, frames.astype(jnp.float32))
        dparams, dframes = pull(upstream.astype(jnp.float32))
        totals = jax.tree.map(lambda left, right: left + right, totals, dparams)
        return (totals, (result.astype(jnp.bfloat16), dframes.astype(jnp.bfloat16)))
    items = (memory.reshape(blocks, group, FRAMES, D), token_ids.reshape(blocks, group, DLEN), dec_segments.reshape(blocks, group, DLEN), mem_segments.reshape(blocks, group, FRAMES), cotangent.reshape(blocks, group, DLEN, D))
    zeros = tuple((jnp.zeros_like(weight) for weight in params))
    grads, (outputs, dframes) = lax.scan(one_group, zeros, items)
    total = jnp.float32(0.0)
    for gradient in grads:
        total = total + jnp.sum(gradient * gradient)
    grad_norm = jnp.sqrt(total)
    factor = CLIP / jnp.maximum(grad_norm, CLIP)
    results = []
    for master, first, second, gradient, rate in zip(params, firsts, seconds, grads, rates):
        results.extend(adam_update(master, first, second, gradient, factor, rate))
    return (outputs.reshape(ROWS, DLEN, D), dframes.reshape(ROWS, FRAMES, D), grad_norm, results[0], results[1], results[2], results[3], results[4], results[5], results[6], results[7], results[8], results[9], results[10], results[11], results[12], results[13], results[14], results[15], results[16], results[17], results[18], results[19], results[20], results[21], results[22], results[23], results[24], results[25], results[26], results[27], results[28], results[29])
```

```python
import functools
import math

import jax
import jax.numpy as jnp
from jax import lax
from jax.experimental import pallas as pl
from jax.experimental.pallas import tpu as pltpu
from jax.sharding import PartitionSpec as P

HEADS = 4
STEP = 5
EPS = 1e-05
NEG = -1e30
CLIP = 300.0
RATE = 0.05
NORM_RATE = 0.3
BETA_ONE = 0.5
BETA_TWO = 0.5
DECAY = 0.01
ADAM_EPS = 1e-08
BF = jnp.bfloat16
F32 = jnp.float32
VMEM_LIMIT = 56 * 1024 * 1024
BASE = 256
LANES = 128


def dot(left, right):
    return jnp.dot(left, right, preferred_element_type=F32)


def dot_nt(left, right):
    return lax.dot_general(left, right, (((1,), (1,)), ((), ())), preferred_element_type=F32)


def dot_tn(left, right):
    return lax.dot_general(left, right, (((0,), (0,)), ((), ())), preferred_element_type=F32)


def norm_parts(stream):
    center = stream - jnp.mean(stream, -1, keepdims=True)
    inverse = lax.rsqrt(jnp.mean(center * center, -1, keepdims=True) + EPS)
    return center * inverse, inverse


def norm_back(upstream, unit, inverse, gain):
    scaled = upstream * gain
    grad = inverse * (
        scaled
        - jnp.mean(scaled, -1, keepdims=True)
        - unit * jnp.mean(scaled * unit, -1, keepdims=True)
    )
    both = jnp.concatenate(
        [jnp.sum(upstream * unit, 0, keepdims=True), jnp.sum(upstream, 0, keepdims=True)], 0
    )
    return grad, both


def head_columns(flipped):
    width, length = flipped.shape
    wide = jnp.concatenate([flipped] * HEADS, 1)
    row = lax.broadcasted_iota(jnp.int32, wide.shape, 0) // (width // HEADS)
    column = lax.broadcasted_iota(jnp.int32, wide.shape, 1) // length
    return jnp.where(row == column, wide, jnp.zeros_like(wide))


def head_rows(values):
    length, width = values.shape
    tall = jnp.concatenate([values] * HEADS, 0)
    row = lax.broadcasted_iota(jnp.int32, tall.shape, 0) // length
    column = lax.broadcasted_iota(jnp.int32, tall.shape, 1) // (width // HEADS)
    return jnp.where(row == column, tall, jnp.zeros_like(tall))


def own_blocks(wide, length):
    part = wide.shape[0] // HEADS
    return jnp.concatenate(
        [
            wide[h * part : (h + 1) * part, h * length : (h + 1) * length]
            for h in range(HEADS)
        ],
        0,
    )


def lanes_store(ref, at, rows, values):
    for i in range(values.shape[1] // LANES):
        ref[at // LANES + i, rows, :] = values[:, i * LANES : (i + 1) * LANES]


def lanes_load(ref, at, rows, width):
    return jnp.concatenate(
        [ref[at // LANES + i, rows, :].astype(BF) for i in range(width // LANES)], 1
    )


def flip(values):
    return values.T


def scores_of(keys, columns, low, high):
    scores = dot(keys, columns)
    place = lax.broadcasted_iota(jnp.int32, scores.shape, 0)
    return jnp.where((place >= low) & (place < high), scores, NEG)


def spread(bounds):
    return jnp.concatenate([bounds] * HEADS, 1)


def softmax_columns(scores):
    peak = jnp.max(scores, 0, keepdims=True)
    expo = jnp.exp(scores - peak)
    total = jnp.sum(expo, 0, keepdims=True)
    return expo * (1.0 / total), peak + jnp.log(total)


def attention_back(keys, values, query, dcontext, low, high, logsum):
    length = query.shape[0]
    query_columns = head_columns(flip(query))
    grad_rows = head_rows(dcontext)
    probs = jnp.exp(scores_of(keys, query_columns, low, high) - logsum)
    dvalues = dot(probs.astype(BF), grad_rows)
    dprobs = dot_nt(values, grad_rows)
    inner = jnp.sum(dprobs * probs, 0, keepdims=True)
    dscores = (probs * (dprobs - inner)).astype(BF)
    dkeys = dot(dscores, head_rows(query))
    dquery = flip(own_blocks(dot_tn(keys, dscores), length))
    return dquery, dkeys, dvalues


def full_spec(shape):
    return pl.BlockSpec(shape, lambda *_: (0,) * len(shape))


def shape_of(shape, kind):
    return jax.ShapeDtypeStruct(shape, kind)


def params(steps=1):
    return pltpu.CompilerParams(
        vmem_limit_bytes=VMEM_LIMIT, dimension_semantics=("arbitrary",) * steps
    )


def cost(flops, data):
    return pl.CostEstimate(flops=int(flops), bytes_accessed=int(data), transcendentals=0)


def lookup_kernel(ids_ref, table_ref, out_ref, split_ref):
    width = table_ref.shape[0]
    blocks = split_ref.shape[0] // width

    @pl.when(pl.program_id(0) == 0)
    def _():
        for b in range(blocks):
            split_ref[b * width : (b + 1) * width, :] = table_ref[:, b * BASE : (b + 1) * BASE]

    ids = ids_ref[0]
    lead = ids >> 8
    rest = ids & (BASE - 1)
    onehot = (
        lax.broadcasted_iota(jnp.int32, (BASE, ids.shape[1]), 0) == rest
    ).astype(F32).astype(BF)
    found = dot(split_ref[...].astype(BF), onehot)
    total = jnp.zeros((width, ids.shape[1]), F32)
    for b in range(blocks):
        total = jnp.where(lead == b, found[b * width : (b + 1) * width, :], total)
    out_ref[0] = total.astype(BF)


def lookup(ids, table):
    count, _, tokens = ids.shape
    width, padded = table.shape
    blocks = padded // BASE
    return pl.pallas_call(
        lookup_kernel,
        grid=(count,),
        in_specs=[
            pl.BlockSpec((1, 1, tokens), lambda i: (i, 0, 0)),
            full_spec((width, padded)),
        ],
        out_specs=pl.BlockSpec((1, width, tokens), lambda i: (i, 0, 0)),
        out_shape=shape_of((count, width, tokens), BF),
        scratch_shapes=[pltpu.VMEM((blocks * width, BASE), F32)],
        compiler_params=params(),
        cost_estimate=cost(
            2 * blocks * width * BASE * tokens * count, 4 * width * padded + 2 * count * width * tokens
        ),
        name="lookup",
    )(ids, table)


def table_grad_kernel(ids_ref, grads_ref, out_ref, total_ref):
    width = grads_ref.shape[1]
    blocks = total_ref.shape[0] // width
    ids = ids_ref[0]
    lead = ids >> 8
    rest = ids & (BASE - 1)
    onehot = (
        lax.broadcasted_iota(jnp.int32, (BASE, ids.shape[1]), 0) == rest
    ).astype(F32).astype(BF)
    grads = grads_ref[0].astype(F32)
    spreads = jnp.concatenate(
        [jnp.where(lead == b, grads, 0.0) for b in range(blocks)], 0
    ).astype(BF)
    part = dot_nt(spreads, onehot)
    step = pl.program_id(0)

    @pl.when(step == 0)
    def _():
        total_ref[...] = part

    @pl.when(step > 0)
    def _():
        total_ref[...] += part

    @pl.when(step == pl.num_programs(0) - 1)
    def _():
        for b in range(blocks):
            out_ref[:, b * BASE : (b + 1) * BASE] = total_ref[b * width : (b + 1) * width, :]


def table_grad(ids, grads, padded):
    count, width, tokens = grads.shape
    blocks = padded // BASE
    return pl.pallas_call(
        table_grad_kernel,
        grid=(count,),
        in_specs=[
            pl.BlockSpec((1, 1, tokens), lambda i: (i, 0, 0)),
            pl.BlockSpec((1, width, tokens), lambda i: (i, 0, 0)),
        ],
        out_specs=full_spec((width, padded)),
        out_shape=shape_of((width, padded), F32),
        scratch_shapes=[pltpu.VMEM((blocks * width, BASE), F32)],
        compiler_params=params(),
        cost_estimate=cost(
            2 * blocks * width * BASE * tokens * count, 4 * width * padded + 2 * count * width * tokens
        ),
        name="table_grad",
    )(ids, grads)


def self_forward_kernel(
    emb_ref, place_ref, low_ref, inward_ref, outward_ref, norms_ref,
    x0_ref, x1_ref, n1_ref, q_ref, k_ref, v_ref, c1_ref, n2_ref, qc_ref, lse_ref,
):
    rows, length = low_ref.shape
    width = x0_ref.shape[1]
    scale = (width // HEADS) ** (-0.5)
    x0 = math.sqrt(width) * flip(emb_ref[...].astype(F32)) + place_ref[...]
    x0_ref[...] = x0
    unit, _ = norm_parts(x0)
    n1 = (unit * norms_ref[0:1, :] + norms_ref[1:2, :]).astype(BF)
    n1_ref[...] = n1
    q_ref[...] = (dot(n1, inward_ref[0]) * scale).astype(BF)
    k_ref[...] = dot(n1, inward_ref[1]).astype(BF)
    v_ref[...] = dot(n1, inward_ref[2]).astype(BF)
    high = spread(lax.broadcasted_iota(jnp.int32, (1, length), 1) + 1)
    for r in range(rows):
        span = slice(r * length, (r + 1) * length)
        scores = scores_of(
            k_ref[span, :], head_columns(flip(q_ref[span, :])), spread(low_ref[r : r + 1, :]), high
        )
        probs, logsum = softmax_columns(scores)
        lse_ref[r : r + 1, :] = logsum
        c1_ref[span, :] = flip(
            own_blocks(dot_tn(v_ref[span, :], probs.astype(BF)), length)
        ).astype(BF)
    x1 = x0 + dot(c1_ref[...], outward_ref[...])
    x1_ref[...] = x1
    unit, _ = norm_parts(x1)
    n2 = (unit * norms_ref[2:3, :] + norms_ref[3:4, :]).astype(BF)
    n2_ref[...] = n2
    qc_ref[...] = (dot(n2, inward_ref[3]) * scale).astype(BF)


def self_forward(emb, place, low, inward, outward, norms):
    rows, length = low.shape
    tokens, width = place.shape
    wide = shape_of((tokens, width), F32)
    thin = shape_of((tokens, width), BF)
    return pl.pallas_call(
        self_forward_kernel,
        in_specs=[
            full_spec(emb.shape), full_spec(place.shape), full_spec(low.shape),
            full_spec(inward.shape), full_spec(outward.shape), full_spec(norms.shape),
        ],
        grid=(1,),
        out_specs=[full_spec((tokens, width))] * 9 + [full_spec((rows, HEADS * length))],
        out_shape=[wide, wide, thin, thin, thin, thin, thin, thin, thin,
                   shape_of((rows, HEADS * length), F32)],
        compiler_params=params(),
        cost_estimate=cost(2 * tokens * width * width * 8, 8 * tokens * width * 4),
        name="self_forward",
    )(emb, place, low, inward, outward, norms)


def cross_forward_kernel(
    rows, pieces, memory_ref, inward_ref, qc_ref, low_ref, high_ref,
    c2_ref, kc_ref, vc_ref, lse_ref, kv_ref,
):
    row = pl.program_id(0)
    total, width = memory_ref.shape
    frames = total // rows
    length = qc_ref.shape[0]

    @pl.when(row == 0)
    def _():
        part = total // pieces
        for i in range(pieces):
            span = slice(i * part, (i + 1) * part)
            block = memory_ref[span, :]
            lanes_store(kv_ref, 0, span, dot(block, inward_ref[0]))
            lanes_store(kv_ref, width, span, dot(block, inward_ref[1]))

    own = pl.ds(row, frames, stride=rows)
    keys = lanes_load(kv_ref, 0, own, width)
    values = lanes_load(kv_ref, width, own, width)
    kc_ref[0] = keys
    vc_ref[0] = values
    scores = scores_of(
        keys, head_columns(flip(qc_ref[...])), spread(low_ref[0]), spread(high_ref[0])
    )
    probs, logsum = softmax_columns(scores)
    lse_ref[0] = logsum
    c2_ref[...] = flip(own_blocks(dot_tn(values, probs.astype(BF)), length)).astype(BF)


def pieces_of(total):
    return max(p for p in (1, 2, 4) if total % (16 * p) == 0)


def cross_forward(memory, inward, query, low, high):
    rows, _, length = low.shape
    total, width = memory.shape
    frames = total // rows
    bound = pl.BlockSpec((1, 1, length), lambda i: (i, 0, 0))
    block = pl.BlockSpec((length, width), lambda i: (i, 0))
    held = pl.BlockSpec((1, frames, width), lambda i: (i, 0, 0))
    return pl.pallas_call(
        functools.partial(cross_forward_kernel, rows, pieces_of(total)),
        grid=(rows,),
        in_specs=[full_spec(memory.shape), full_spec(inward.shape), block, bound, bound],
        out_specs=[block, held, held, pl.BlockSpec((1, 1, HEADS * length), lambda i: (i, 0, 0))],
        out_shape=[
            shape_of((rows * length, width), BF),
            shape_of((rows, frames, width), BF),
            shape_of((rows, frames, width), BF),
            shape_of((rows, 1, HEADS * length), F32),
        ],
        scratch_shapes=[pltpu.VMEM((2 * width // LANES, total, LANES), F32)],
        compiler_params=params(),
        cost_estimate=cost(
            2 * total * width * 2 * width + 4 * total * length * HEADS * width, 6 * total * width
        ),
        name="cross_forward",
    )(memory, inward, query, low, high)


def feed_kernel(
    x1_ref, c2_ref, outward_ref, norms_ref, expand_ref, shrink_ref, cot_ref,
    out_ref, dx2_ref, gexp_ref, gshr_ref, gnorm_ref, total_ref, dn_ref,
):
    parts = gexp_ref.shape[0]
    chunk = expand_ref.shape[1] // parts
    x2 = x1_ref[...] + dot(c2_ref[...], outward_ref[...])
    unit, inverse = norm_parts(x2)
    gain = norms_ref[4:5, :]
    n3 = (unit * gain + norms_ref[5:6, :]).astype(BF)
    n3_flipped = flip(n3)
    cot = cot_ref[...]
    cot_flipped = flip(cot)
    total_ref[...] = x2
    first = math.sqrt(2.0 / math.pi)
    for j in range(parts):
        span = slice(j * chunk, (j + 1) * chunk)
        before = dot(n3, expand_ref[:, span])
        square = before * before
        tanh = jnp.tanh(before * (first + (first * 0.044715) * square))
        half = 0.5 * before
        wing = 0.5 + 0.5 * tanh
        active = (before * wing).astype(BF)
        slope = wing + half * (1.0 - tanh * tanh) * (first + (3.0 * first * 0.044715) * square)
        grad = (dot_nt(cot, shrink_ref[span, :]) * slope).astype(BF)
        total_ref[...] += dot(active, shrink_ref[span, :])
        gexp_ref[j] = dot(n3_flipped, grad).astype(BF)
        gshr_ref[span, :] = flip(dot(cot_flipped, active)).astype(BF)
        back = dot_nt(grad, expand_ref[:, span])
        if j == 0:
            dn_ref[...] = back
        else:
            dn_ref[...] += back
    out_ref[...] = total_ref[...].astype(BF)
    grad, both = norm_back(dn_ref[...], unit, inverse, gain)
    dx2_ref[...] = cot.astype(F32) + grad
    gnorm_ref[...] = both


def feed(x1, c2, outward, norms, expand, shrink, cot):
    tokens, width = x1.shape
    hidden = expand.shape[1]
    parts = 4
    return pl.pallas_call(
        feed_kernel,
        grid=(1,),
        in_specs=[full_spec(a.shape) for a in (x1, c2, outward, norms, expand, shrink, cot)],
        out_specs=[
            full_spec((tokens, width)), full_spec((tokens, width)),
            full_spec((parts, width, hidden // parts)), full_spec((hidden, width)),
            full_spec((2, width)),
        ],
        out_shape=[
            shape_of((tokens, width), BF), shape_of((tokens, width), F32),
            shape_of((parts, width, hidden // parts), BF), shape_of((hidden, width), BF),
            shape_of((2, width), F32),
        ],
        scratch_shapes=[pltpu.VMEM((tokens, width), F32), pltpu.VMEM((tokens, width), F32)],
        compiler_params=params(),
        cost_estimate=cost(12 * tokens * width * hidden, 12 * width * hidden),
        name="feed",
    )(x1, c2, outward, norms, expand, shrink, cot)


def cross_backward_kernel(
    rows, pieces, dx2_ref, c2_ref, outward_ref, qc_ref, kc_ref, vc_ref, lse_ref, low_ref, high_ref,
    n2_ref, x1_ref, inward_ref, memory_ref, norms_ref,
    frame_ref, dx1_ref, gweight_ref, gnorm_ref, dc_ref, dq_ref, dkv_ref,
):
    row = pl.program_id(0)
    total, width = memory_ref.shape
    frames = total // rows
    length = qc_ref.shape[0]
    scale = (width // HEADS) ** (-0.5)

    @pl.when(row == 0)
    def _():
        rounded = dx2_ref[...].astype(BF)
        gweight_ref[3] = dot_tn(c2_ref[...], rounded)
        dc_ref[...] = dot_nt(rounded, outward_ref[...]).astype(BF)

    span = pl.ds(pl.multiple_of(row * length, length), length)
    dquery, dkeys, dvalues = attention_back(
        kc_ref[0], vc_ref[0], qc_ref[...], dc_ref[span, :],
        spread(low_ref[0]), spread(high_ref[0]), lse_ref[0],
    )
    dq_ref[span, :] = dquery.astype(BF)
    own = pl.ds(row, frames, stride=rows)
    lanes_store(dkv_ref, 0, own, dkeys)
    lanes_store(dkv_ref, width, own, dvalues)

    @pl.when(row == rows - 1)
    def _():
        part = total // pieces
        for i in range(pieces):
            block = slice(i * part, (i + 1) * part)
            memory = memory_ref[block, :]
            dk = lanes_load(dkv_ref, 0, block, width)
            dv = lanes_load(dkv_ref, width, block, width)
            frame_ref[block, :] = (dot_nt(dk, inward_ref[1]) + dot_nt(dv, inward_ref[2])).astype(BF)
            flipped = flip(memory)
            if i == 0:
                gweight_ref[1] = dot(flipped, dk)
                gweight_ref[2] = dot(flipped, dv)
            else:
                gweight_ref[1] += dot(flipped, dk)
                gweight_ref[2] += dot(flipped, dv)
        dq = dq_ref[...]
        gweight_ref[0] = dot_tn(n2_ref[...], dq) * scale
        unit, inverse = norm_parts(x1_ref[...])
        grad, both = norm_back(
            dot_nt(dq, inward_ref[0]) * scale, unit, inverse, norms_ref[2:3, :]
        )
        dx1_ref[...] = dx2_ref[...] + grad
        gnorm_ref[...] = both


def cross_backward(dx2, c2, outward, query, keys, values, logsum, low, high, n2, x1, inward, memory, norms):
    rows, _, length = low.shape
    total, width = memory.shape
    frames = total // rows
    tokens = rows * length
    bound = pl.BlockSpec((1, 1, length), lambda i: (i, 0, 0))
    block = pl.BlockSpec((length, width), lambda i: (i, 0))
    held = pl.BlockSpec((1, frames, width), lambda i: (i, 0, 0))
    return pl.pallas_call(
        functools.partial(cross_backward_kernel, rows, pieces_of(total)),
        grid=(rows,),
        in_specs=[
            full_spec(dx2.shape), full_spec(c2.shape), full_spec(outward.shape), block, held, held,
            pl.BlockSpec((1, 1, HEADS * length), lambda i: (i, 0, 0)), bound, bound,
            full_spec(n2.shape), full_spec(x1.shape), full_spec(inward.shape),
            full_spec(memory.shape), full_spec(norms.shape),
        ],
        out_specs=[
            full_spec((total, width)), full_spec((tokens, width)),
            full_spec((4, width, width)), full_spec((2, width)),
        ],
        out_shape=[
            shape_of((total, width), BF), shape_of((tokens, width), F32),
            shape_of((4, width, width), F32), shape_of((2, width), F32),
        ],
        scratch_shapes=[
            pltpu.VMEM((tokens, width), BF), pltpu.VMEM((tokens, width), BF),
            pltpu.VMEM((2 * width // LANES, total, LANES), F32),
        ],
        compiler_params=params(),
        cost_estimate=cost(
            2 * total * width * 4 * width + 10 * total * length * HEADS * width, 8 * total * width
        ),
        name="cross_backward",
    )(dx2, c2, outward, query, keys, values, logsum, low, high, n2, x1, inward, memory, norms)


def self_backward_kernel(
    dx1_ref, c1_ref, outward_ref, q_ref, k_ref, v_ref, lse_ref, low_ref, n1_ref, x0_ref,
    inward_ref, norms_ref, dt_ref, gweight_ref, gnorm_ref, dc_ref, dq_ref, dk_ref, dv_ref,
):
    rows, length = low_ref.shape
    width = x0_ref.shape[1]
    scale = (width // HEADS) ** (-0.5)
    dx1 = dx1_ref[...]
    rounded = dx1.astype(BF)
    gweight_ref[3] = dot_tn(c1_ref[...], rounded)
    dc_ref[...] = dot_nt(rounded, outward_ref[...]).astype(BF)
    high = spread(lax.broadcasted_iota(jnp.int32, (1, length), 1) + 1)
    for r in range(rows):
        span = slice(r * length, (r + 1) * length)
        dquery, dkeys, dvalues = attention_back(
            k_ref[span, :], v_ref[span, :], q_ref[span, :], dc_ref[span, :],
            spread(low_ref[r : r + 1, :]), high, lse_ref[r : r + 1, :],
        )
        dq_ref[span, :] = dquery.astype(BF)
        dk_ref[span, :] = dkeys.astype(BF)
        dv_ref[span, :] = dvalues.astype(BF)
    flipped = flip(n1_ref[...])
    gweight_ref[0] = dot(flipped, dq_ref[...]) * scale
    gweight_ref[1] = dot(flipped, dk_ref[...])
    gweight_ref[2] = dot(flipped, dv_ref[...])
    upstream = (
        dot_nt(dq_ref[...], inward_ref[0]) * scale
        + dot_nt(dk_ref[...], inward_ref[1])
        + dot_nt(dv_ref[...], inward_ref[2])
    )
    unit, inverse = norm_parts(x0_ref[...])
    grad, both = norm_back(upstream, unit, inverse, norms_ref[0:1, :])
    gnorm_ref[...] = both
    dt_ref[...] = flip(math.sqrt(width) * (dx1 + grad)).astype(BF)


def self_backward(dx1, c1, outward, query, keys, values, logsum, low, n1, x0, inward, norms):
    tokens, width = dx1.shape
    ins = (dx1, c1, outward, query, keys, values, logsum, low, n1, x0, inward, norms)
    return pl.pallas_call(
        self_backward_kernel,
        grid=(1,),
        in_specs=[full_spec(a.shape) for a in ins],
        out_specs=[full_spec((width, tokens)), full_spec((4, width, width)), full_spec((2, width))],
        out_shape=[
            shape_of((width, tokens), BF), shape_of((4, width, width), F32),
            shape_of((2, width), F32),
        ],
        scratch_shapes=[pltpu.VMEM((tokens, width), BF)] * 4,
        compiler_params=params(),
        cost_estimate=cost(2 * tokens * width * width * 12, 8 * tokens * width * 4),
        name="self_backward",
    )(*ins)


def bits_of(count):
    return count.bit_length() - 1


def swap(values, axis, bit, count):
    return lax.ppermute(values, axis, [(i, i ^ (1 << bit)) for i in range(count)])


def side(axis, bit):
    return (lax.axis_index(axis) >> bit) & 1


def halve(values, dim, axis, bit, count):
    mine = side(axis, bit)
    keep = lax.dynamic_index_in_dim(values, mine, dim, keepdims=False)
    send = lax.dynamic_index_in_dim(values, 1 - mine, dim, keepdims=False).astype(BF)
    return keep.astype(F32) + swap(send, axis, bit, count).astype(F32)


def both_halves(values, dim, axis, bit, count):
    other = swap(values, axis, bit, count)
    mine = side(axis, bit) == 0
    return jnp.stack([jnp.where(mine, values, other), jnp.where(mine, other, values)], dim)


def scatter_sum(values, sizes, order):
    names = [(axis, bit) for axis, count in sizes for bit in reversed(range(bits_of(count)))]
    values = values.reshape((2,) * len(names) + values.shape[2:])
    counts = dict(sizes)
    for step in order:
        at = names.index(step)
        names.pop(at)
        values = halve(values, at, step[0], step[1], counts[step[0]])
    return values


def encode(place, width):
    halves = jnp.arange(width // 2, dtype=F32)
    freq = jnp.exp(halves * (-2.0 * math.log(10000.0) / width))
    angle = place[..., None] * freq
    return jnp.stack([jnp.sin(angle), jnp.cos(angle)], -1).reshape(place.shape + (width,))


def adam_update(master, first, second, gradient, factor, rate):
    clipped = gradient * factor
    moment = BETA_ONE * first + (1 - BETA_ONE) * clipped
    square = BETA_TWO * second + (1 - BETA_TWO) * clipped * clipped
    corrected = moment / (1 - BETA_ONE**STEP)
    spread_of = jnp.sqrt(square / (1 - BETA_TWO**STEP))
    weight = master - rate * (corrected / (spread_of + ADAM_EPS) + DECAY * master)
    return (clipped, moment, square, weight, weight.astype(BF))


def body(n, m, *args):
    masters, firsts, seconds = args[0:6], args[6:12], args[12:18]
    memory, token_ids, dec_segments, mem_segments, cotangent = args[18:23]
    table_master, inward_master, outward_master, expand_master, shrink_master, norms_master = masters
    rates = (RATE, RATE, RATE, RATE, RATE, NORM_RATE)
    rows, length = token_ids.shape
    tokens = rows * length
    vocab, share = table_master.shape
    width = inward_master.shape[2]
    hidden = expand_master.shape[1]
    part = inward_master.shape[1]
    frames = mem_segments.shape[1]
    padded = -(-vocab // (2 * BASE)) * 2 * BASE

    ids = lax.all_to_all(
        jnp.broadcast_to(token_ids[None], (n, rows, length)), "dp", 0, 0
    ).reshape(n, 1, tokens)

    norm_block = jnp.pad(
        norms_master.reshape(1, 1, 6 * share), ((0, 0), (0, part - 1), (0, width - 6 * share))
    )
    blocks = jnp.concatenate([inward_master, outward_master, norm_block], 0).astype(BF)
    gathered = lax.all_gather(blocks, "dp", axis=1, tiled=True)
    expand = lax.all_gather(expand_master.astype(BF), "dp", axis=0, tiled=True)
    shrink = lax.all_gather(shrink_master.astype(BF), "dp", axis=0, tiled=True)
    inward, outward = gathered[0:6], gathered[6:8]
    norms = (
        gathered[8].reshape(n, part, width)[:, 0, : 6 * share]
        .reshape(n, 6, share).transpose(1, 0, 2).reshape(6, width).astype(F32)
    )

    flipped = memory.transpose(1, 0, 2).reshape(frames // m, m, rows, width)
    mem_rows = lax.all_to_all(flipped, "seq", 1, 0).reshape(frames * rows, width)

    table_flipped = jnp.pad(table_master.T, ((0, -share % 8), (0, padded - vocab)))
    found = lookup(ids, table_flipped)[:, :share]
    emb = lax.all_to_all(found, "dp", 0, 0).reshape(width, tokens)

    starts = jnp.sum(dec_segments[:, None, :] < dec_segments[:, :, None], -1).astype(jnp.int32)
    place = encode((jnp.arange(length)[None] - starts).astype(F32), width).reshape(tokens, width)
    low = jnp.sum(mem_segments[:, None, :] < dec_segments[:, :, None], -1).astype(jnp.int32)
    high = jnp.sum(mem_segments[:, None, :] <= dec_segments[:, :, None], -1).astype(jnp.int32)
    low, high = low[:, None, :], high[:, None, :]

    x0, x1, n1, q, k, v, c1, n2, qc, lse1 = self_forward(
        emb, place, starts, inward[0:4], outward[0], norms
    )
    c2, kc, vc, lse2 = cross_forward(mem_rows, inward[4:6], qc, low, high)
    block_out, dx2, gexp, gshr, gnorm3 = feed(
        x1, c2, outward[1], norms, expand, shrink, cotangent.reshape(tokens, width)
    )
    sizes = (("seq", m), ("dp", n))
    seq_steps = [("seq", b) for b in range(bits_of(m))]
    dp_steps = [("dp", b) for b in range(bits_of(n))]

    gshr = gshr.reshape(n, m, hidden // (m * n), width).transpose(1, 0, 2, 3)
    gexp = (
        gexp.reshape(m, n, part, hidden // (m * width), width)
        .transpose(0, 1, 3, 2, 4).reshape(m, n, -1, width)
    )
    ff_sum = scatter_sum(jnp.concatenate([gshr, gexp], 2), sizes, seq_steps + dp_steps)

    frame, dx1, gcross, gnorm2 = cross_backward(
        dx2, c2, outward[1], qc, kc, vc, lse2, low, high, n2, x1, inward[3:6], mem_rows, norms
    )
    returned = (
        lax.all_to_all(frame.reshape(m, frames // m, rows, width), "seq", 0, 1)
        .reshape(frames // m, m * rows, width).transpose(1, 0, 2)
    )
    dt, gself, gnorm1 = self_backward(
        dx1, c1, outward[0], q, k, v, lse1, starts, n1, x0, inward[0:3], norms
    )
    gnorm = jnp.concatenate([gnorm1, gnorm2, gnorm3], 0)

    arrived = lax.all_to_all(dt.reshape(n, share, tokens), "dp", 0, 0)
    arrived = jnp.pad(arrived, ((0, 0), (0, -share % 8), (0, 0)))
    gtable = table_grad(ids, arrived, padded)[:share]

    gnorm = jnp.pad(
        gnorm.reshape(6, n, share).transpose(1, 0, 2).reshape(1, n, 1, 6 * share),
        ((0, m - 1), (0, 0), (0, 7), (0, width - 6 * share)),
    )
    late = jnp.concatenate(
        [gcross.reshape(m, n, part, width), gself.reshape(m, n, part, width), gnorm], 2
    )
    late_sum = scatter_sum(late, sizes, seq_steps[:1] + dp_steps + seq_steps[1:])

    half = padded // 2
    gtable = halve(gtable.reshape(share, 2, half), 1, "seq", 0, m).astype(BF)
    gtable = gtable.astype(F32) + swap(gtable, "seq", 1, m).astype(F32)

    squares = (
        jnp.sum(ff_sum * ff_sum) + jnp.sum(late_sum * late_sum) + 0.5 * jnp.sum(gtable * gtable)
    )
    squares = lax.all_to_all(
        jnp.broadcast_to(squares, (n * m, 8, LANES)), ("dp", "seq"), 0, 0
    )
    grad_norm = jnp.sqrt(jnp.sum(squares[:, 0, 0]))
    factor = CLIP / jnp.maximum(grad_norm, CLIP)

    gtable = both_halves(gtable, 1, "seq", 0, m).reshape(share, padded)[:, :vocab].T
    dense = jnp.concatenate([ff_sum, late_sum], 0)
    dense = both_halves(dense, 0, "seq", 1, m)
    dense = both_halves(dense, 1, "seq", 0, m).reshape((m,) + ff_sum.shape[:0] + (-1, width))
    cut = hidden // (m * n)
    at = ff_sum.shape[0]
    gshrink = dense[:, :cut].reshape(-1, width)
    gexpand = (
        dense[:, cut:at].reshape(m, hidden // (m * width), part, width)
        .transpose(2, 0, 1, 3).reshape(part, hidden)
    )
    gcross, gself = dense[:, at : at + part], dense[:, at + part : at + 2 * part]
    ginward = jnp.concatenate([gself[:3], gcross[:3]], 0)
    goutward = jnp.stack([gself[3], gcross[3]])
    gnorms = dense[0, at + 2 * part, : 6 * share].reshape(6, share)

    results = []
    grads = (gtable, ginward, goutward, gexpand, gshrink, gnorms)
    for master, first, second, gradient, rate in zip(masters, firsts, seconds, grads, rates):
        results.extend(adam_update(master, first, second, gradient, factor, rate))
    return (block_out.reshape(rows, length, width), returned, grad_norm, *results)


def solution(mesh):
    n, m = mesh.shape["dp"], mesh.shape["seq"]
    state = (
        P(None, "dp"), P(None, "dp", None), P(None, "dp", None),
        P("dp", None), P("dp", None), P(None, "dp"),
    )
    flat = P(("dp", "seq"), None)
    deep = P(("dp", "seq"), None, None)
    in_specs = state * 3 + (P("dp", "seq", None), flat, flat, flat, deep)
    out_specs = (deep, P("dp", "seq", None), P()) + tuple(s for s in state for _ in range(5))
    return jax.shard_map(
        functools.partial(body, n, m), mesh=mesh, in_specs=in_specs, out_specs=out_specs, check_vma=False
    )
```

```python
import functools
import math

import jax
import jax.numpy as jnp
from jax import lax
from jax.experimental import pallas as pl
from jax.experimental.pallas import tpu as pltpu
from jax.sharding import PartitionSpec as P

HEADS = 4
STEP = 5
EPS = 1e-05
NEG = -1e30
CLIP = 300.0
RATE = 0.05
NORM_RATE = 0.3
BETA_ONE = 0.5
BETA_TWO = 0.5
DECAY = 0.01
ADAM_EPS = 1e-08
BF = jnp.bfloat16
F32 = jnp.float32
VMEM_LIMIT = 56 * 1024 * 1024
BASE = 256
LANES = 128


def dot(left, right):
    return jnp.dot(left, right, preferred_element_type=F32)


def dot_nt(left, right):
    return lax.dot_general(left, right, (((1,), (1,)), ((), ())), preferred_element_type=F32)


def dot_tn(left, right):
    return lax.dot_general(left, right, (((0,), (0,)), ((), ())), preferred_element_type=F32)


def norm_parts(stream):
    center = stream - jnp.mean(stream, -1, keepdims=True)
    inverse = lax.rsqrt(jnp.mean(center * center, -1, keepdims=True) + EPS)
    return center * inverse, inverse


def norm_back(upstream, unit, inverse, gain):
    scaled = upstream * gain
    grad = inverse * (
        scaled
        - jnp.mean(scaled, -1, keepdims=True)
        - unit * jnp.mean(scaled * unit, -1, keepdims=True)
    )
    both = jnp.concatenate(
        [jnp.sum(upstream * unit, 0, keepdims=True), jnp.sum(upstream, 0, keepdims=True)], 0
    )
    return grad, both


def head_columns(flipped):
    width, length = flipped.shape
    wide = jnp.concatenate([flipped] * HEADS, 1)
    row = lax.broadcasted_iota(jnp.int32, wide.shape, 0) // (width // HEADS)
    column = lax.broadcasted_iota(jnp.int32, wide.shape, 1) // length
    return jnp.where(row == column, wide, jnp.zeros_like(wide))


def head_rows(values):
    length, width = values.shape
    tall = jnp.concatenate([values] * HEADS, 0)
    row = lax.broadcasted_iota(jnp.int32, tall.shape, 0) // length
    column = lax.broadcasted_iota(jnp.int32, tall.shape, 1) // (width // HEADS)
    return jnp.where(row == column, tall, jnp.zeros_like(tall))


def own_blocks(wide, length):
    part = wide.shape[0] // HEADS
    return jnp.concatenate(
        [
            wide[h * part : (h + 1) * part, h * length : (h + 1) * length]
            for h in range(HEADS)
        ],
        0,
    )


def lanes_store(ref, at, rows, values):
    for i in range(values.shape[1] // LANES):
        ref[at // LANES + i, rows, :] = values[:, i * LANES : (i + 1) * LANES]


def lanes_load(ref, at, rows, width):
    return jnp.concatenate(
        [ref[at // LANES + i, rows, :].astype(BF) for i in range(width // LANES)], 1
    )


def flip(values):
    return values.T


def scores_of(keys, columns, low, high):
    scores = dot(keys, columns)
    place = lax.broadcasted_iota(jnp.int32, scores.shape, 0)
    return jnp.where((place >= low) & (place < high), scores, NEG)


def spread(bounds):
    return jnp.concatenate([bounds] * HEADS, 1)


def counts(segments, tokens):
    low = jnp.zeros(tokens.shape, jnp.int32)
    high = jnp.zeros(tokens.shape, jnp.int32)
    values = segments.astype(F32)
    for s in range(4):
        below = jnp.sum((values < s).astype(F32), 1, keepdims=True).astype(jnp.int32)
        upto = jnp.sum((values < s + 1).astype(F32), 1, keepdims=True).astype(jnp.int32)
        low = jnp.where(tokens == s, below, low)
        high = jnp.where(tokens == s, upto, high)
    return low, high


def softmax_columns(scores):
    peak = jnp.max(scores, 0, keepdims=True)
    expo = jnp.exp(scores - peak)
    total = jnp.sum(expo, 0, keepdims=True)
    return expo * (1.0 / total), peak + jnp.log(total)


def attention_back(keys, values, query, dcontext, low, high, logsum):
    length = query.shape[0]
    query_columns = head_columns(flip(query))
    grad_rows = head_rows(dcontext)
    probs = jnp.exp(scores_of(keys, query_columns, low, high) - logsum)
    dvalues = dot(probs.astype(BF), grad_rows)
    dprobs = dot_nt(values, grad_rows)
    inner = jnp.sum(dprobs * probs, 0, keepdims=True)
    dscores = (probs * (dprobs - inner)).astype(BF)
    dkeys = dot(dscores, head_rows(query))
    dquery = flip(own_blocks(dot_tn(keys, dscores), length))
    return dquery, dkeys, dvalues


def matrix(ref, i):
    block = ref[:, i]
    return block.reshape(block.shape[0] * block.shape[1], block.shape[2])


def norm_rows(ref):
    return jnp.sum(ref[:, 0].astype(F32), 0)


def stack_spec(stack, count, at):
    groups, _, rows, width = stack.shape
    return pl.BlockSpec((groups, count, rows, width), lambda *_: (0, at // count, 0, 0))


def full_spec(shape):
    return pl.BlockSpec(shape, lambda *_: (0,) * len(shape))


def shape_of(shape, kind):
    return jax.ShapeDtypeStruct(shape, kind)


def params(steps=1):
    return pltpu.CompilerParams(
        vmem_limit_bytes=VMEM_LIMIT, dimension_semantics=("arbitrary",) * steps
    )


def cost(flops, data):
    return pl.CostEstimate(flops=int(flops), bytes_accessed=int(data), transcendentals=0)


def lookup_kernel(ids_ref, table_ref, out_ref, split_ref):
    width = table_ref.shape[0]
    blocks = split_ref.shape[0] // width

    @pl.when(pl.program_id(0) == 0)
    def _():
        for b in range(blocks):
            split_ref[b * width : (b + 1) * width, :] = table_ref[:, b * BASE : (b + 1) * BASE]

    ids = ids_ref[0]
    lead = ids >> 8
    rest = ids & (BASE - 1)
    onehot = (
        lax.broadcasted_iota(jnp.int32, (BASE, ids.shape[1]), 0) == rest
    ).astype(F32).astype(BF)
    found = dot(split_ref[...].astype(BF), onehot)
    total = jnp.zeros((width, ids.shape[1]), F32)
    for b in range(blocks):
        total = jnp.where(lead == b, found[b * width : (b + 1) * width, :], total)
    out_ref[0] = total.astype(BF)


def lookup(ids, table):
    count, _, tokens = ids.shape
    width, padded = table.shape
    blocks = padded // BASE
    return pl.pallas_call(
        lookup_kernel,
        grid=(count,),
        in_specs=[
            pl.BlockSpec((1, 1, tokens), lambda i: (i, 0, 0)),
            full_spec((width, padded)),
        ],
        out_specs=pl.BlockSpec((1, width, tokens), lambda i: (i, 0, 0)),
        out_shape=shape_of((count, width, tokens), BF),
        scratch_shapes=[pltpu.VMEM((blocks * width, BASE), F32)],
        compiler_params=params(),
        cost_estimate=cost(
            2 * blocks * width * BASE * tokens * count, 4 * width * padded + 2 * count * width * tokens
        ),
        name="lookup",
    )(ids, table)


def table_grad_kernel(ids_ref, grads_ref, out_ref, square_ref, total_ref):
    count, width, _ = grads_ref.shape
    blocks = total_ref.shape[0] // width
    ids = jnp.concatenate([ids_ref[i] for i in range(count)], 1)
    grads = jnp.concatenate([grads_ref[i].astype(F32) for i in range(count)], 1)
    lead = ids >> 8
    rest = ids & (BASE - 1)
    onehot = (
        lax.broadcasted_iota(jnp.int32, (BASE, ids.shape[1]), 0) == rest
    ).astype(F32).astype(BF)
    spreads = jnp.concatenate(
        [jnp.where(lead == b, grads, 0.0) for b in range(blocks)], 0
    ).astype(BF)
    part = dot_nt(spreads, onehot)
    step = pl.program_id(0)

    @pl.when(step == 0)
    def _():
        total_ref[...] = part

    @pl.when(step > 0)
    def _():
        total_ref[...] += part

    @pl.when(step == pl.num_programs(0) - 1)
    def _():
        total = jnp.zeros(square_ref.shape, F32)
        for b in range(blocks):
            value = total_ref[b * width : (b + 1) * width, :]
            out_ref[:, b * BASE : (b + 1) * BASE] = value
            for i in range(0, width, 8):
                for j in range(0, BASE, LANES):
                    piece = value[i : i + 8, j : j + LANES]
                    total = total + piece * piece
        square_ref[...] = total


def table_grad(ids, grads, padded):
    count, width, tokens = grads.shape
    blocks = padded // BASE
    group = 4
    return pl.pallas_call(
        table_grad_kernel,
        grid=(count // group,),
        in_specs=[
            pl.BlockSpec((group, 1, tokens), lambda i: (i, 0, 0)),
            pl.BlockSpec((group, width, tokens), lambda i: (i, 0, 0)),
        ],
        out_specs=[full_spec((width, padded)), full_spec((8, LANES))],
        out_shape=[shape_of((width, padded), F32), shape_of((8, LANES), F32)],
        scratch_shapes=[pltpu.VMEM((blocks * width, BASE), F32)],
        compiler_params=params(),
        cost_estimate=cost(
            2 * blocks * width * BASE * tokens * count, 4 * width * padded + 2 * count * width * tokens
        ),
        name="table_grad",
    )(ids, grads)


def self_forward_kernel(
    emb_ref, waves_ref, segments_ref, inward_ref, outward_ref, norms_ref,
    x0_ref, x1_ref, n1_ref, q_ref, k_ref, v_ref, c1_ref, n2_ref, qc_ref, lse_ref,
):
    rows, length = segments_ref.shape
    width = x0_ref.shape[1]
    scale = (width // HEADS) ** (-0.5)
    segments = segments_ref[...]
    low, _ = counts(segments, segments)
    index = lax.broadcasted_iota(jnp.int32, (1, length), 1)
    places = jnp.concatenate([index - low[r : r + 1, :] for r in range(rows)], 1)
    onehot = (
        lax.broadcasted_iota(jnp.int32, (length, rows * length), 0) == places
    ).astype(F32).astype(BF)
    rest = waves_ref[...]
    place = jnp.zeros(x0_ref.shape, F32)
    for _ in range(3):
        term = rest.astype(BF)
        rest = rest - term.astype(F32)
        place = place + dot_tn(onehot, term)
    x0 = math.sqrt(width) * flip(emb_ref[...].astype(F32)) + place
    x0_ref[...] = x0
    norms = norm_rows(norms_ref)
    unit, _ = norm_parts(x0)
    n1 = (unit * norms[0:1, :] + norms[1:2, :]).astype(BF)
    n1_ref[...] = n1
    q_ref[...] = (dot(n1, matrix(inward_ref, 0)) * scale).astype(BF)
    k_ref[...] = dot(n1, matrix(inward_ref, 1)).astype(BF)
    v_ref[...] = dot(n1, matrix(inward_ref, 2)).astype(BF)
    high = spread(lax.broadcasted_iota(jnp.int32, (1, length), 1) + 1)
    for r in range(rows):
        span = slice(r * length, (r + 1) * length)
        scores = scores_of(
            k_ref[span, :], head_columns(flip(q_ref[span, :])), spread(low[r : r + 1, :]), high
        )
        probs, logsum = softmax_columns(scores)
        lse_ref[r : r + 1, :] = logsum
        c1_ref[span, :] = flip(
            own_blocks(dot_tn(v_ref[span, :], probs.astype(BF)), length)
        ).astype(BF)
    x1 = x0 + dot(c1_ref[...], matrix(outward_ref, 0))
    x1_ref[...] = x1
    unit, _ = norm_parts(x1)
    n2 = (unit * norms[2:3, :] + norms[3:4, :]).astype(BF)
    n2_ref[...] = n2
    qc_ref[...] = (dot(n2, matrix(inward_ref, 3)) * scale).astype(BF)


def self_forward(emb, waves, segments, stack):
    rows, length = segments.shape
    width, tokens = emb.shape
    wide = shape_of((tokens, width), F32)
    thin = shape_of((tokens, width), BF)
    return pl.pallas_call(
        self_forward_kernel,
        in_specs=[
            full_spec(emb.shape), full_spec(waves.shape), full_spec(segments.shape),
            stack_spec(stack, 4, 0), stack_spec(stack, 1, 6), stack_spec(stack, 1, 8),
        ],
        grid=(1,),
        out_specs=[full_spec((tokens, width))] * 9 + [full_spec((rows, HEADS * length))],
        out_shape=[wide, wide, thin, thin, thin, thin, thin, thin, thin,
                   shape_of((rows, HEADS * length), F32)],
        compiler_params=params(),
        cost_estimate=cost(2 * tokens * width * width * 8, 8 * tokens * width * 4),
        name="self_forward",
    )(emb, waves, segments, stack, stack, stack)


def cross_forward_kernel(
    rows, here_ref, *refs,
):
    *memory_refs, inward_ref, qc_ref, tokens_ref, frames_ref = refs[:-5]
    c2_ref, kc_ref, vc_ref, lse_ref, kv_ref = refs[-5:]
    row = pl.program_id(0)
    part, width = memory_refs[0].shape
    frames = part * len(memory_refs) // rows
    length = qc_ref.shape[0]

    @pl.when(row == 0)
    def _():
        for i, ref in enumerate(memory_refs):
            span = pl.ds(pl.multiple_of((here_ref[0] ^ i) * part, 16), part)
            lanes_store(kv_ref, 0, span, dot(ref[...], matrix(inward_ref, 0)))
            lanes_store(kv_ref, width, span, dot(ref[...], matrix(inward_ref, 1)))

    own = pl.ds(row, frames, stride=rows)
    keys = lanes_load(kv_ref, 0, own, width)
    values = lanes_load(kv_ref, width, own, width)
    kc_ref[0] = keys
    vc_ref[0] = values
    low, high = counts(frames_ref[pl.ds(row, 1), :], tokens_ref[pl.ds(row, 1), :])
    scores = scores_of(keys, head_columns(flip(qc_ref[...])), spread(low), spread(high))
    probs, logsum = softmax_columns(scores)
    lse_ref[0] = logsum
    c2_ref[...] = flip(own_blocks(dot_tn(values, probs.astype(BF)), length)).astype(BF)


def cross_forward(here, memory, stack, query, tokens, frame_segments):
    rows, length = tokens.shape
    part, width = memory[0].shape
    total = part * len(memory)
    frames = total // rows
    block = pl.BlockSpec((length, width), lambda i: (i, 0))
    held = pl.BlockSpec((1, frames, width), lambda i: (i, 0, 0))
    return pl.pallas_call(
        functools.partial(cross_forward_kernel, rows),
        grid=(rows,),
        in_specs=[
            pl.BlockSpec(memory_space=pltpu.SMEM), *[full_spec(a.shape) for a in memory],
            stack_spec(stack, 2, 4), block, full_spec(tokens.shape),
            full_spec(frame_segments.shape),
        ],
        out_specs=[block, held, held, pl.BlockSpec((1, 1, HEADS * length), lambda i: (i, 0, 0))],
        out_shape=[
            shape_of((rows * length, width), BF),
            shape_of((rows, frames, width), BF),
            shape_of((rows, frames, width), BF),
            shape_of((rows, 1, HEADS * length), F32),
        ],
        scratch_shapes=[pltpu.VMEM((2 * width // LANES, total, LANES), F32)],
        compiler_params=params(),
        cost_estimate=cost(
            2 * total * width * 2 * width + 4 * total * length * HEADS * width, 6 * total * width
        ),
        name="cross_forward",
    )(here, *memory, stack, query, tokens, frame_segments)


def feed_kernel(
    packed, x1_ref, c2_ref, outward_ref, norms_ref, expand_ref, shrink_ref, cot_ref,
    out_ref, dx2_ref, gff_ref, gnorm_ref, total_ref, dn_ref,
):
    parts, owners = gff_ref.shape[0], gff_ref.shape[1]
    blocks = expand_ref.shape[1] // parts
    groups = shrink_ref.shape[0] // parts
    norms = norm_rows(norms_ref)
    x2 = x1_ref[...] + dot(c2_ref[...], matrix(outward_ref, 0))
    width = x2.shape[1]
    unit, inverse = norm_parts(x2)
    gain = norms[4:5, :]
    n3 = (unit * gain + norms[5:6, :]).astype(BF)
    n3_flipped = flip(n3)
    cot = cot_ref[...]
    cot_flipped = flip(cot)
    total_ref[...] = x2
    first = math.sqrt(2.0 / math.pi)
    for j in range(parts):
        expand = jnp.concatenate([matrix(expand_ref, j * blocks + b) for b in range(blocks)], 1)
        shrink = shrink_ref[j * groups : (j + 1) * groups].reshape(-1, width)
        chunk = shrink.shape[0]
        before = dot(n3, expand)
        square = before * before
        tanh = jnp.tanh(before * (first + (first * 0.044715) * square))
        half = 0.5 * before
        wing = 0.5 + 0.5 * tanh
        active = (before * wing).astype(BF)
        slope = wing + half * (1.0 - tanh * tanh) * (first + (3.0 * first * 0.044715) * square)
        grad = (dot_nt(cot, shrink) * slope).astype(BF)
        total_ref[...] += dot(active, shrink)
        gexp = dot(n3_flipped, grad).astype(BF)
        gshr = flip(dot(cot_flipped, active)).astype(BF)
        share = chunk * parts // (parts * owners)
        if packed:
            rows = width // owners
            for o in range(chunk // (share * parts)):
                for q in range(parts):
                    at = (o * parts + q) * share
                    owner = j * (chunk // (share * parts)) + o
                    gff_ref[q, owner, 0:share, :] = gshr[at : at + share, :]
            for b in range(chunk // width):
                for o in range(owners):
                    gff_ref[j, o, share + b * rows : share + (b + 1) * rows, :] = gexp[
                        o * rows : (o + 1) * rows, b * width : (b + 1) * width
                    ]
        else:
            gff_ref[j, 0, 0:chunk, :] = gshr
            for b in range(chunk // width):
                gff_ref[j, 0, chunk + b * width : chunk + (b + 1) * width, :] = gexp[
                    :, b * width : (b + 1) * width
                ]
        back = dot_nt(grad, expand)
        if j == 0:
            dn_ref[...] = back
        else:
            dn_ref[...] += back
    out_ref[...] = total_ref[...].astype(BF)
    grad, both = norm_back(dn_ref[...], unit, inverse, gain)
    dx2_ref[...] = cot.astype(F32) + grad
    gnorm_ref[...] = both


def feed(x1, c2, stack, wide, cot, parts, owners):
    tokens, width = x1.shape
    groups, blocks, rows, _ = wide.shape
    blocks //= 2
    hidden = groups * blocks * rows
    packed = width // owners % 16 == 0 and hidden // (parts * owners) % 16 == 0
    shape = (parts, owners if packed else 1, 2 * hidden // (parts * (owners if packed else 1)), width)
    result = pl.pallas_call(
        functools.partial(feed_kernel, packed),
        grid=(1,),
        in_specs=[
            full_spec(x1.shape), full_spec(c2.shape), stack_spec(stack, 1, 7),
            stack_spec(stack, 1, 8), stack_spec(wide, blocks, 0), stack_spec(wide, blocks, blocks),
            full_spec(cot.shape),
        ],
        out_specs=[
            full_spec((tokens, width)), full_spec((tokens, width)), full_spec(shape),
            full_spec((2, width)),
        ],
        out_shape=[
            shape_of((tokens, width), BF), shape_of((tokens, width), F32), shape_of(shape, BF),
            shape_of((2, width), F32),
        ],
        scratch_shapes=[pltpu.VMEM((tokens, width), F32), pltpu.VMEM((tokens, width), F32)],
        compiler_params=params(),
        cost_estimate=cost(12 * tokens * width * hidden, 12 * width * hidden),
        name="feed",
    )(x1, c2, stack, stack, wide, wide, cot)
    out, dx2, gff, gnorm = result
    if not packed:
        chunk = hidden // parts
        gshr = gff[:, 0, :chunk].reshape(owners, parts, hidden // (parts * owners), width)
        gexp = gff[:, 0, chunk:].reshape(parts, chunk // width, owners, width // owners, width)
        gff = jnp.concatenate(
            [
                gshr.transpose(1, 0, 2, 3),
                gexp.transpose(0, 2, 1, 3, 4).reshape(parts, owners, -1, width),
            ],
            2,
        )
    return out, dx2, gff, gnorm


def cross_backward_kernel(
    rows, count, here_ref, dx2_ref, c2_ref, outward_ref, qc_ref, kc_ref, vc_ref, lse_ref, tokens_ref,
    frames_ref, n2_ref, x1_ref, inward_ref, norms_ref, *refs,
):
    memory_refs, frame_refs = refs[:count], refs[count : 2 * count]
    dx1_ref, gweight_ref, gnorm_ref, dc_ref, dq_ref, dkv_ref = refs[2 * count :]
    row = pl.program_id(0)
    part, width = memory_refs[0].shape
    frames = part * count // rows
    length = qc_ref.shape[0]
    scale = (width // HEADS) ** (-0.5)

    @pl.when(row == 0)
    def _():
        rounded = dx2_ref[...].astype(BF)
        gweight_ref[3] = dot_tn(c2_ref[...], rounded)
        dc_ref[...] = dot_nt(rounded, matrix(outward_ref, 0)).astype(BF)

    span = pl.ds(pl.multiple_of(row * length, length), length)
    low, high = counts(frames_ref[pl.ds(row, 1), :], tokens_ref[pl.ds(row, 1), :])
    dquery, dkeys, dvalues = attention_back(
        kc_ref[0], vc_ref[0], qc_ref[...], dc_ref[span, :], spread(low), spread(high), lse_ref[0]
    )
    dq_ref[span, :] = dquery.astype(BF)
    own = pl.ds(row, frames, stride=rows)
    lanes_store(dkv_ref, 0, own, dkeys)
    lanes_store(dkv_ref, width, own, dvalues)

    @pl.when(row == rows - 1)
    def _():
        key_weight, value_weight = matrix(inward_ref, 1), matrix(inward_ref, 2)
        for i in range(count):
            block = pl.ds(pl.multiple_of((here_ref[0] ^ i) * part, 16), part)
            dk = lanes_load(dkv_ref, 0, block, width)
            dv = lanes_load(dkv_ref, width, block, width)
            frame_refs[i][...] = (dot_nt(dk, key_weight) + dot_nt(dv, value_weight)).astype(BF)
            flipped = flip(memory_refs[i][...])
            if i == 0:
                gweight_ref[1] = dot(flipped, dk)
                gweight_ref[2] = dot(flipped, dv)
            else:
                gweight_ref[1] += dot(flipped, dk)
                gweight_ref[2] += dot(flipped, dv)
        dq = dq_ref[...]
        gweight_ref[0] = dot_tn(n2_ref[...], dq) * scale
        unit, inverse = norm_parts(x1_ref[...])
        grad, both = norm_back(
            dot_nt(dq, matrix(inward_ref, 0)) * scale, unit, inverse, norm_rows(norms_ref)[2:3, :]
        )
        dx1_ref[...] = dx2_ref[...] + grad
        gnorm_ref[...] = both


def cross_backward(
    here, dx2, c2, query, keys, values, logsum, segments, frame_segments, n2, x1, stack, memory
):
    rows, length = segments.shape
    part, width = memory[0].shape
    count = len(memory)
    total = part * count
    frames = total // rows
    tokens = rows * length
    block = pl.BlockSpec((length, width), lambda i: (i, 0))
    held = pl.BlockSpec((1, frames, width), lambda i: (i, 0, 0))
    return pl.pallas_call(
        functools.partial(cross_backward_kernel, rows, count),
        grid=(rows,),
        in_specs=[
            pl.BlockSpec(memory_space=pltpu.SMEM), full_spec(dx2.shape), full_spec(c2.shape),
            stack_spec(stack, 1, 7), block, held, held,
            pl.BlockSpec((1, 1, HEADS * length), lambda i: (i, 0, 0)), full_spec(segments.shape),
            full_spec(frame_segments.shape), full_spec(n2.shape), full_spec(x1.shape), stack_spec(stack, 3, 3),
            stack_spec(stack, 1, 8), *[full_spec(a.shape) for a in memory],
        ],
        out_specs=[
            *[full_spec(a.shape) for a in memory], full_spec((tokens, width)),
            full_spec((4, width, width)), full_spec((2, width)),
        ],
        out_shape=[
            *[shape_of(a.shape, BF) for a in memory], shape_of((tokens, width), F32),
            shape_of((4, width, width), F32), shape_of((2, width), F32),
        ],
        scratch_shapes=[
            pltpu.VMEM((tokens, width), BF), pltpu.VMEM((tokens, width), BF),
            pltpu.VMEM((2 * width // LANES, total, LANES), F32),
        ],
        compiler_params=params(),
        cost_estimate=cost(
            2 * total * width * 4 * width + 10 * total * length * HEADS * width, 8 * total * width
        ),
        name="cross_backward",
    )(
        here, dx2, c2, stack, query, keys, values, logsum, segments, frame_segments, n2, x1, stack,
        stack, *memory
    )


def self_backward_kernel(
    dx1_ref, c1_ref, outward_ref, q_ref, k_ref, v_ref, lse_ref, segments_ref, n1_ref, x0_ref,
    inward_ref, norms_ref, dt_ref, gweight_ref, gnorm_ref, dc_ref, dq_ref, dk_ref, dv_ref,
):
    rows, length = segments_ref.shape
    width = x0_ref.shape[1]
    scale = (width // HEADS) ** (-0.5)
    low, _ = counts(segments_ref[...], segments_ref[...])
    dx1 = dx1_ref[...]
    rounded = dx1.astype(BF)
    gweight_ref[3] = dot_tn(c1_ref[...], rounded)
    dc_ref[...] = dot_nt(rounded, matrix(outward_ref, 0)).astype(BF)
    high = spread(lax.broadcasted_iota(jnp.int32, (1, length), 1) + 1)
    for r in range(rows):
        span = slice(r * length, (r + 1) * length)
        dquery, dkeys, dvalues = attention_back(
            k_ref[span, :], v_ref[span, :], q_ref[span, :], dc_ref[span, :],
            spread(low[r : r + 1, :]), high, lse_ref[r : r + 1, :],
        )
        dq_ref[span, :] = dquery.astype(BF)
        dk_ref[span, :] = dkeys.astype(BF)
        dv_ref[span, :] = dvalues.astype(BF)
    flipped = flip(n1_ref[...])
    gweight_ref[0] = dot(flipped, dq_ref[...]) * scale
    gweight_ref[1] = dot(flipped, dk_ref[...])
    gweight_ref[2] = dot(flipped, dv_ref[...])
    upstream = (
        dot_nt(dq_ref[...], matrix(inward_ref, 0)) * scale
        + dot_nt(dk_ref[...], matrix(inward_ref, 1))
        + dot_nt(dv_ref[...], matrix(inward_ref, 2))
    )
    unit, inverse = norm_parts(x0_ref[...])
    grad, both = norm_back(upstream, unit, inverse, norm_rows(norms_ref)[0:1, :])
    gnorm_ref[...] = both
    dt_ref[...] = flip(math.sqrt(width) * (dx1 + grad)).astype(BF)


def self_backward(dx1, c1, query, keys, values, logsum, segments, n1, x0, stack):
    tokens, width = dx1.shape
    ins = (dx1, c1, query, keys, values, logsum, segments, n1, x0)
    specs = [full_spec(a.shape) for a in ins]
    return pl.pallas_call(
        self_backward_kernel,
        grid=(1,),
        in_specs=specs[:2] + [stack_spec(stack, 1, 6)] + specs[2:]
        + [stack_spec(stack, 3, 0), stack_spec(stack, 1, 8)],
        out_specs=[full_spec((width, tokens)), full_spec((4, width, width)), full_spec((2, width))],
        out_shape=[
            shape_of((width, tokens), BF), shape_of((4, width, width), F32),
            shape_of((2, width), F32),
        ],
        scratch_shapes=[pltpu.VMEM((tokens, width), BF)] * 4,
        compiler_params=params(),
        cost_estimate=cost(2 * tokens * width * width * 12, 8 * tokens * width * 4),
        name="self_backward",
    )(*ins[:2], stack, *ins[2:], stack, stack)


def bits_of(count):
    return count.bit_length() - 1


def swap(values, axis, bit, count):
    return lax.ppermute(values, axis, [(i, i ^ (1 << bit)) for i in range(count)])


def side(axis, bit):
    return (lax.axis_index(axis) >> bit) & 1


def halve(values, dim, axis, bit, count):
    mine = side(axis, bit)
    keep = lax.dynamic_index_in_dim(values, mine, dim, keepdims=False)
    send = lax.dynamic_index_in_dim(values, 1 - mine, dim, keepdims=False).astype(BF)
    return keep.astype(F32) + swap(send, axis, bit, count).astype(F32)


def both_halves(values, dim, axis, bit, count):
    other = swap(values, axis, bit, count)
    mine = side(axis, bit) == 0
    return jnp.stack([jnp.where(mine, values, other), jnp.where(mine, other, values)], dim)


def quarter_sum(values, m):
    here = lax.axis_index("seq")
    pieces = [lax.dynamic_index_in_dim(values, here ^ i, 0, keepdims=False) for i in range(m)]
    pieces = [
        (lax.ppermute(a.astype(BF), "seq", [(p, p ^ i) for p in range(m)]) if i else a).astype(F32)
        for i, a in enumerate(pieces)
    ]
    return functools.reduce(jnp.add, pieces)


def gather_all(values, axis, bits, count):
    size, low_bit = 1 << len(bits), bits[0]
    mine = (lax.axis_index(axis) >> low_bit) & (size - 1)
    pieces = jnp.stack(
        [values]
        + [
            lax.ppermute(values, axis, [(p, p ^ (i << low_bit)) for p in range(count)])
            for i in range(1, size)
        ]
    )
    return jnp.stack(
        [lax.dynamic_index_in_dim(pieces, mine ^ i, 0, keepdims=False) for i in range(size)]
    )


tie = lax.optimization_barrier


def mark_kernel(source_ref, small_ref, out_ref):
    del source_ref
    out_ref[...] = small_ref[...]


def mark(source, small, *later):
    small = pl.pallas_call(
        mark_kernel,
        in_specs=[pl.BlockSpec(memory_space=pl.ANY), pl.BlockSpec(memory_space=pltpu.VMEM)],
        out_specs=pl.BlockSpec(memory_space=pltpu.VMEM),
        out_shape=shape_of(small.shape, small.dtype),
        compiler_params=pltpu.CompilerParams(vmem_limit_bytes=1024 * 1024),
        cost_estimate=cost(0, 100e6),
        name="mark",
    )(source, small)
    return tie((small, *later))


def regroup(values, rows):
    groups, count, part, width = values.shape
    return (
        values.transpose(1, 0, 2, 3).reshape(count, groups * part // rows, rows, width)
        .transpose(1, 0, 2, 3)
    )


def own_half(values, dim):
    half = values.shape[dim] // 2
    return lax.dynamic_slice_in_dim(values, side("seq", 0) * half, half, dim)


def encode(place, width):
    halves = jnp.arange(width // 2, dtype=F32)
    freq = jnp.exp(halves * (-2.0 * math.log(10000.0) / width))
    angle = place[..., None] * freq
    return jnp.stack([jnp.sin(angle), jnp.cos(angle)], -1).reshape(place.shape + (width,))


def assemble_kernel(here_ref, *refs):
    pieces, out_ref, sem = refs[:-2], refs[-2], refs[-1]
    copies = [
        pltpu.make_async_copy(ref, out_ref.at[:, here_ref[0] ^ i], sem.at[i])
        for i, ref in enumerate(pieces)
    ]
    for copy in copies:
        copy.start()
    for copy in copies:
        copy.wait()


def assemble(here, pieces):
    frames, rows, width = pieces[0].shape
    count = len(pieces)
    return pl.pallas_call(
        assemble_kernel,
        in_specs=[pl.BlockSpec(memory_space=pltpu.SMEM)]
        + [pl.BlockSpec(memory_space=pl.ANY)] * count,
        out_specs=pl.BlockSpec(memory_space=pl.ANY),
        out_shape=shape_of((frames, count, rows, width), pieces[0].dtype),
        scratch_shapes=[pltpu.SemaphoreType.DMA((count,))],
        compiler_params=pltpu.CompilerParams(vmem_limit_bytes=1024 * 1024),
        cost_estimate=cost(0, 4 * count * frames * rows * width),
        name="assemble",
    )(here, *pieces)


def square_kernel(part_ref, dense_ref, out_ref):
    dense = dense_ref[...]
    dense = dense * dense
    total = part_ref[...]
    for i in range(dense.shape[0] // 8):
        for j in range(dense.shape[1] // LANES):
            total = total + dense[i * 8 : (i + 1) * 8, j * LANES : (j + 1) * LANES]
    for i in range(out_ref.shape[0]):
        out_ref[i] = total


def square_blocks(part, dense, count):
    return pl.pallas_call(
        square_kernel,
        grid=(1,),
        in_specs=[full_spec(part.shape), full_spec(dense.shape)],
        out_specs=full_spec((count, 8, LANES)),
        out_shape=shape_of((count, 8, LANES), F32),
        compiler_params=params(),
        cost_estimate=cost(dense.size, 4 * dense.size),
        name="square_blocks",
    )(part, dense)


def adam_kernel(squares_ref, gtable_ref, dense_ref, *refs):
    masters, firsts, seconds = refs[0:6], refs[6:12], refs[12:18]
    norm_ref, outs = refs[18], refs[19:]
    total = jnp.sum(jnp.sum(squares_ref[...], 0), keepdims=True)
    norm = jnp.sqrt(total)
    norm_ref[...] = norm
    factor = CLIP / jnp.maximum(norm, CLIP)
    parts, _, width = dense_ref.shape
    share = masters[5].shape[1]
    part = masters[1].shape[1]
    hidden = masters[3].shape[1]
    cut = masters[4].shape[0] // parts
    late = dense_ref.shape[1] - 2 * part - 8

    def update(i, at, gradient, rate):
        first_m = 1.0 / (1 - BETA_ONE**STEP)
        first_s = 1.0 / (1 - BETA_TWO**STEP)
        clipped = gradient * factor
        moment = BETA_ONE * firsts[i][at] + (1 - BETA_ONE) * clipped
        square = BETA_TWO * seconds[i][at] + (1 - BETA_TWO) * clipped * clipped
        master = masters[i][at]
        weight = master - rate * (
            (moment * first_m) / (jnp.sqrt(square * first_s) + ADAM_EPS) + DECAY * master
        )
        for ref, value in zip(outs[5 * i : 5 * i + 5], (clipped, moment, square, weight, weight)):
            ref[at] = value.astype(ref.dtype)

    everything = (slice(None), slice(None))
    update(0, everything, gtable_ref[:, 0 : masters[0].shape[1]], RATE)
    for i in range(parts):
        for a in range(2):
            gradient = dense_ref[i, late + a * part : late + (a + 1) * part, :]
            if i < 3:
                update(1, (3 - 3 * a + i, slice(None), slice(None)), gradient, RATE)
            else:
                update(2, (1 - a, slice(None), slice(None)), gradient, RATE)
        blocks = hidden // (parts * width)
        for b in range(blocks):
            at = (i * blocks + b) * width
            update(
                3, (slice(None), slice(at, at + width)),
                dense_ref[i, cut + b * part : cut + (b + 1) * part, :], RATE,
            )
        update(4, (slice(i * cut, (i + 1) * cut), slice(None)), dense_ref[i, 0:cut, :], RATE)
    update(5, everything, dense_ref[0, late + 2 * part : late + 2 * part + 6, 0:share], NORM_RATE)


def adam(squares, gtable, dense, state):
    shapes = [shape_of((1, 1), F32)] + [
        shape_of(a.shape, kind) for a in state[:6] for kind in (F32, F32, F32, F32, BF)
    ]
    ins = (squares, gtable, dense, *state)
    norm, *results = pl.pallas_call(
        adam_kernel,
        grid=(1,),
        in_specs=[full_spec(a.shape) for a in ins],
        out_specs=[full_spec(a.shape) for a in shapes],
        out_shape=shapes,
        compiler_params=params(),
        cost_estimate=cost(0, 34 * sum(a.size for a in state[:6])),
        name="adam",
    )(*ins)
    return norm, results


def body(n, m, *args):
    masters, firsts, seconds = args[0:6], args[6:12], args[12:18]
    memory, token_ids, dec_segments, mem_segments, cotangent = args[18:23]
    table_master, inward_master, outward_master, expand_master, shrink_master, norms_master = masters
    rates = (RATE, RATE, RATE, RATE, RATE, NORM_RATE)
    rows, length = token_ids.shape
    tokens = rows * length
    vocab, share = table_master.shape
    width = inward_master.shape[2]
    hidden = expand_master.shape[1]
    part = inward_master.shape[1]
    frames = mem_segments.shape[1]
    padded = -(-vocab // (2 * BASE)) * 2 * BASE

    copies = jnp.broadcast_to(token_ids[None], (n * m, rows, length))
    ids = lax.all_to_all(copies, ("dp", "seq"), 0, 0).reshape(n * m, 1, tokens)
    norms_now, inward_now, outward_now, memory = mark(
        copies, norms_master, inward_master, outward_master, memory
    )

    here = lax.axis_index("seq")
    flipped = memory.transpose(1, 0, 2).reshape(frames // m, m, rows, width)
    mem_rows = [lax.dynamic_index_in_dim(flipped, here ^ i, 1, keepdims=False) for i in range(m)]
    mem_rows = [
        (lax.ppermute(a, "seq", [(p, p ^ i) for p in range(m)]) if i else a).reshape(-1, width)
        for i, a in enumerate(mem_rows)
    ]
    line_ids = lax.dynamic_index_in_dim(
        ids.reshape(n, m, 1, tokens), here, 1, keepdims=False
    )
    here = here.reshape(1).astype(jnp.int32)

    norm_block = lax.dynamic_update_slice(
        jnp.zeros((1, max(part, 16), width), F32), norms_now[None],
        (0, 0, lax.axis_index("dp") * share),
    )
    blocks = own_half(jnp.concatenate([inward_now, outward_now], 0), 1)
    if part == 32:
        blocks = jnp.concatenate([blocks, own_half(norm_block, 1)], 0)
    upper = list(range(1, bits_of(n)))
    narrow = gather_all(blocks.astype(BF), "dp", upper[:2], n)
    table_flipped = jnp.pad(table_master.T, ((0, -share % 8), (0, padded - vocab)))

    found = lookup(line_ids, table_flipped)[:, :share]
    narrow = both_halves(narrow, 1, "dp", 0, n)
    found, narrow = tie((found, narrow))
    emb = lax.all_to_all(found, "dp", 0, 0).reshape(width, tokens)
    if upper[2:]:
        narrow = gather_all(narrow, "dp", upper[2:], n)
        narrow = narrow.reshape((-1,) + narrow.shape[2:])
    narrow = both_halves(narrow, 2, "seq", 0, m)

    wide = jnp.concatenate(
        [
            own_half(expand_master, 0).reshape(part // 2, hidden // width, width).transpose(1, 0, 2),
            own_half(shrink_master, 0).reshape(hidden // width, part // 2, width),
        ],
        0,
    )
    wide = gather_all(wide.astype(BF), "dp", upper[:2], n)
    if upper[2:]:
        wide = gather_all(wide, "dp", upper[2:], n)
        wide = wide.reshape((-1,) + wide.shape[2:])

    waves = encode(jnp.arange(length).astype(F32), width)
    emb, narrow = tie((emb, narrow))
    stack = narrow.reshape((2 * n,) + narrow.shape[3:])
    if part != 32:
        norms = lax.psum(norm_block[:, :16].astype(BF).astype(F32), "dp").astype(BF)
        stack = regroup(stack, 16)
        norms = jnp.pad(norms[None], ((0, stack.shape[0] - 1), (0, 0), (0, 0), (0, 0)))
        stack = jnp.concatenate([stack, norms], 1)

    x0, x1, n1, q, k, v, c1, n2, qc, lse1 = self_forward(emb, waves, dec_segments, stack)
    qc, wide = tie((qc, wide))
    wide = both_halves(wide, 1, "dp", 0, n)
    c2, kc, vc, lse2 = cross_forward(here, mem_rows, stack, qc, dec_segments, mem_segments)
    c2, wide = tie((c2, wide))
    wide = both_halves(wide, 2, "seq", 0, m)
    wide = wide.reshape((2 * n,) + wide.shape[3:])
    if part != 32:
        count = hidden // width
        shrink = wide[:, count:].reshape(width // 16, count, 16, width)
        wide = jnp.concatenate([regroup(wide[:, :count], 16), shrink], 1)
    block_out, dx2, gff, gnorm3 = feed(
        x1, c2, stack, wide, cotangent.reshape(tokens, width), m, n
    )
    *frame, dx1, gcross, gnorm2 = cross_backward(
        here, dx2, c2, qc, kc, vc, lse2, dec_segments, mem_segments, n2, x1, stack, mem_rows
    )
    gff = quarter_sum(gff, m)
    dx1, gff = tie((dx1, gff))
    frame = [
        lax.ppermute(a, "seq", [(p, p ^ i) for p in range(m)]) if i else a
        for i, a in enumerate(frame)
    ]
    dt, gself, gnorm1 = self_backward(dx1, c1, q, k, v, lse1, dec_segments, n1, x0, stack)
    gff = gff.reshape((2,) * bits_of(n) + gff.shape[1:])
    gff = halve(gff, bits_of(n) - 1, "dp", 0, n)
    dt, gff = tie((dt, gff))

    few = share // m
    arrived = lax.all_to_all(dt.reshape(n * m, few, tokens), ("dp", "seq"), 0, 0)
    arrived = jnp.pad(arrived, ((0, 0), (0, -few % 8), (0, 0)))

    gnorm1, gcross, gself = mark(dt, gnorm1, gcross, gself)
    gnorm = jnp.concatenate([gnorm1, gnorm2, gnorm3], 0)
    gnorm = jnp.pad(
        gnorm.reshape(6, n, share).transpose(1, 0, 2)[:, None],
        ((0, 0), (0, m - 1), (0, 2), (0, width - share)),
    )
    late = jnp.concatenate(
        [
            a.reshape(m, n, part, width).transpose(1, 0, 2, 3) for a in (gcross, gself)
        ] + [gnorm], 2,
    )
    block = late.shape[2]
    late = late.reshape((2,) * bits_of(n) + (m * block, width))
    late = halve(late, bits_of(n) - 1, "dp", 0, n)
    arrived, late, gff = tie((arrived, late, gff))
    gtable, squares = table_grad(ids, arrived, padded)
    at = gff.shape[-2]
    joint = jnp.concatenate([gff, late], -2)
    for bit in range(1, bits_of(n)):
        joint = halve(joint, joint.ndim - 3, "dp", bit, n)
        if bit == 1:
            gtable, joint, *frame = tie((gtable, joint, *frame))
    returned = assemble(here, [a.reshape(frames // m, rows, width) for a in frame])
    returned = returned.reshape(frames // m, m * rows, width).transpose(1, 0, 2)
    late_sum = quarter_sum(joint[at:].reshape(m, block, width), m)
    dense = jnp.concatenate([joint[:at], late_sum], 0)
    squares = square_blocks(squares, dense, n * m)
    squares = lax.all_to_all(squares, ("dp", "seq"), 0, 0)

    gtable = gtable[:few]
    for i, bit in enumerate(reversed(range(bits_of(m)))):
        gtable = both_halves(gtable, i, "seq", bit, m)
    gtable = gtable.reshape(share, padded)
    dense = both_halves(dense, 0, "seq", 1, m)
    dense = both_halves(dense, 1, "seq", 0, m).reshape(m, -1, width)
    grad_norm, results = adam(
        squares, gtable, dense,
        [(a.T if i == 0 else a) for group in (masters, firsts, seconds) for i, a in enumerate(group)],
    )
    results = [(a.T if i < 5 else a) for i, a in enumerate(results)]
    return (block_out.reshape(rows, length, width), returned, grad_norm.reshape(()), *results)


def solution(mesh):
    n, m = mesh.shape["dp"], mesh.shape["seq"]
    state = (
        P(None, "dp"), P(None, "dp", None), P(None, "dp", None),
        P("dp", None), P("dp", None), P(None, "dp"),
    )
    flat = P(("dp", "seq"), None)
    deep = P(("dp", "seq"), None, None)
    in_specs = state * 3 + (P("dp", "seq", None), flat, flat, flat, deep)
    out_specs = (deep, P("dp", "seq", None), P()) + tuple(s for s in state for _ in range(5))
    return jax.shard_map(
        functools.partial(body, n, m), mesh=mesh, in_specs=in_specs, out_specs=out_specs, check_vma=False
    )
```

```python
import functools
import math

import jax
import jax.numpy as jnp
from jax import lax
from jax.experimental import pallas as pl
from jax.experimental.pallas import tpu as pltpu
from jax.sharding import PartitionSpec as P

HEADS = 4
STEP = 5
EPS = 1e-05
NEG = -1e30
CLIP = 300.0
RATE = 0.05
NORM_RATE = 0.3
BETA_ONE = 0.5
BETA_TWO = 0.5
DECAY = 0.01
ADAM_EPS = 1e-08
BF = jnp.bfloat16
F32 = jnp.float32
ROOMY = 56 * 1024 * 1024
TIGHT = 28 * 1024 * 1024
BASE = 256
LANES = 128
SPAN = 32


def dot(left, right):
    return jnp.dot(left, right, preferred_element_type=F32)


def dot_nt(left, right):
    return lax.dot_general(left, right, (((1,), (1,)), ((), ())), preferred_element_type=F32)


def dot_tn(left, right):
    return lax.dot_general(left, right, (((0,), (0,)), ((), ())), preferred_element_type=F32)


def norm_parts(stream):
    center = stream - jnp.mean(stream, -1, keepdims=True)
    inverse = lax.rsqrt(jnp.mean(center * center, -1, keepdims=True) + EPS)
    return center * inverse, inverse


def norm_back(upstream, unit, inverse, gain):
    scaled = upstream * gain
    grad = inverse * (
        scaled
        - jnp.mean(scaled, -1, keepdims=True)
        - unit * jnp.mean(scaled * unit, -1, keepdims=True)
    )
    both = jnp.concatenate(
        [jnp.sum(upstream * unit, 0, keepdims=True), jnp.sum(upstream, 0, keepdims=True)], 0
    )
    return grad, both


def head_columns(flipped):
    width, length = flipped.shape
    wide = jnp.concatenate([flipped] * HEADS, 1)
    row = lax.broadcasted_iota(jnp.int32, wide.shape, 0) // (width // HEADS)
    column = lax.broadcasted_iota(jnp.int32, wide.shape, 1) // length
    return jnp.where(row == column, wide, jnp.zeros_like(wide))


def head_rows(values):
    length, width = values.shape
    tall = jnp.concatenate([values] * HEADS, 0)
    row = lax.broadcasted_iota(jnp.int32, tall.shape, 0) // length
    column = lax.broadcasted_iota(jnp.int32, tall.shape, 1) // (width // HEADS)
    return jnp.where(row == column, tall, jnp.zeros_like(tall))


def own_blocks(wide, length):
    part = wide.shape[0] // HEADS
    return jnp.concatenate(
        [
            wide[h * part : (h + 1) * part, h * length : (h + 1) * length]
            for h in range(HEADS)
        ],
        0,
    )


def flip(values):
    return values.T


def scores_of(keys, columns, low, high):
    scores = dot(keys, columns)
    place = lax.broadcasted_iota(jnp.int32, scores.shape, 0)
    return jnp.where((place >= low) & (place < high), scores, NEG)


def spread(bounds):
    return jnp.concatenate([bounds] * HEADS, 1)


def counts(segments, tokens):
    low = jnp.zeros(tokens.shape, jnp.int32)
    high = jnp.zeros(tokens.shape, jnp.int32)
    values = segments.astype(F32)
    for s in range(4):
        below = jnp.sum((values < s).astype(F32), 1, keepdims=True).astype(jnp.int32)
        upto = jnp.sum((values < s + 1).astype(F32), 1, keepdims=True).astype(jnp.int32)
        low = jnp.where(tokens == s, below, low)
        high = jnp.where(tokens == s, upto, high)
    return low, high


def softmax_columns(scores):
    peak = jnp.max(scores, 0, keepdims=True)
    expo = jnp.exp(scores - peak)
    total = jnp.sum(expo, 0, keepdims=True)
    return expo * (1.0 / total), peak + jnp.log(total)


def attention_back(keys, values, query, dcontext, low, high, logsum):
    length = query.shape[0]
    query_columns = head_columns(flip(query))
    grad_rows = head_rows(dcontext)
    probs = jnp.exp(scores_of(keys, query_columns, low, high) - logsum)
    dvalues = dot(probs.astype(BF), grad_rows)
    dprobs = dot_nt(values, grad_rows)
    inner = jnp.sum(dprobs * probs, 0, keepdims=True)
    dscores = (probs * (dprobs - inner)).astype(BF)
    dkeys = dot(dscores, head_rows(query))
    dquery = flip(own_blocks(dot_tn(keys, dscores), length))
    return dquery, dkeys, dvalues


def matrix(ref, i):
    block = ref[:, i]
    return block.reshape(block.shape[0] * block.shape[1], block.shape[2])


def norm_rows(ref):
    return jnp.sum(ref[:, 0].astype(F32), 0)


def stack_spec(stack, count, at):
    groups, _, rows, width = stack.shape
    return pl.BlockSpec((groups, count, rows, width), lambda *_: (0, at // count, 0, 0))


def full_spec(shape):
    return pl.BlockSpec(shape, lambda *_: (0,) * len(shape))


def shape_of(shape, kind):
    return jax.ShapeDtypeStruct(shape, kind)


def params(limit):
    return pltpu.CompilerParams(vmem_limit_bytes=limit, dimension_semantics=("arbitrary",))


def cost(flops, data):
    return pl.CostEstimate(flops=int(flops), bytes_accessed=int(data), transcendentals=0)


def lookup_kernel(ids_ref, table_ref, out_ref, split_ref):
    width = table_ref.shape[0]
    blocks = split_ref.shape[0] // width

    @pl.when(pl.program_id(0) == 0)
    def _():
        for b in range(blocks):
            split_ref[b * width : (b + 1) * width, :] = table_ref[:, b * BASE : (b + 1) * BASE]

    ids = ids_ref[0]
    lead = ids >> 8
    rest = ids & (BASE - 1)
    onehot = (
        lax.broadcasted_iota(jnp.int32, (BASE, ids.shape[1]), 0) == rest
    ).astype(F32).astype(BF)
    found = dot(split_ref[...].astype(BF), onehot)
    total = jnp.zeros((width, ids.shape[1]), F32)
    for b in range(blocks):
        total = jnp.where(lead == b, found[b * width : (b + 1) * width, :], total)
    out_ref[0] = total.astype(BF)


def lookup(ids, table):
    count, _, tokens = ids.shape
    width, padded = table.shape
    blocks = padded // BASE
    return pl.pallas_call(
        lookup_kernel,
        grid=(count,),
        in_specs=[
            pl.BlockSpec((1, 1, tokens), lambda i: (i, 0, 0)),
            full_spec((width, padded)),
        ],
        out_specs=pl.BlockSpec((1, width, tokens), lambda i: (i, 0, 0)),
        out_shape=shape_of((count, width, tokens), BF),
        scratch_shapes=[pltpu.VMEM((blocks * width, BASE), F32)],
        compiler_params=params(TIGHT),
        cost_estimate=cost(
            2 * blocks * width * BASE * tokens * count, 4 * width * padded + 2 * count * width * tokens
        ),
        name="lookup",
    )(ids, table)


def table_grad_kernel(ids_ref, grads_ref, out_ref, square_ref, total_ref):
    count, width, _ = grads_ref.shape
    blocks = total_ref.shape[0] // width
    ids = jnp.concatenate([ids_ref[i] for i in range(count)], 1)
    grads = jnp.concatenate([grads_ref[i].astype(F32) for i in range(count)], 1)
    lead = ids >> 8
    rest = ids & (BASE - 1)
    onehot = (
        lax.broadcasted_iota(jnp.int32, (BASE, ids.shape[1]), 0) == rest
    ).astype(F32).astype(BF)
    spreads = jnp.concatenate(
        [jnp.where(lead == b, grads, 0.0) for b in range(blocks)], 0
    ).astype(BF)
    part = dot_nt(spreads, onehot)
    step = pl.program_id(0)

    @pl.when(step == 0)
    def _():
        total_ref[...] = part

    @pl.when(step > 0)
    def _():
        total_ref[...] += part

    @pl.when(step == pl.num_programs(0) - 1)
    def _():
        total = jnp.zeros(square_ref.shape, F32)
        for b in range(blocks):
            value = total_ref[b * width : (b + 1) * width, :]
            out_ref[:, b * BASE : (b + 1) * BASE] = value
            for i in range(0, width, 8):
                for j in range(0, BASE, LANES):
                    piece = value[i : i + 8, j : j + LANES]
                    total = total + piece * piece
        square_ref[...] = total


def table_grad(ids, grads, padded):
    count, width, tokens = grads.shape
    blocks = padded // BASE
    group = 4
    return pl.pallas_call(
        table_grad_kernel,
        grid=(count // group,),
        in_specs=[
            pl.BlockSpec((group, 1, tokens), lambda i: (i, 0, 0)),
            pl.BlockSpec((group, width, tokens), lambda i: (i, 0, 0)),
        ],
        out_specs=[full_spec((width, padded)), full_spec((8, LANES))],
        out_shape=[shape_of((width, padded), F32), shape_of((8, LANES), F32)],
        scratch_shapes=[pltpu.VMEM((blocks * width, BASE), F32)],
        compiler_params=params(TIGHT),
        cost_estimate=cost(
            2 * blocks * width * BASE * tokens * count, 4 * width * padded + 2 * count * width * tokens
        ),
        name="table_grad",
    )(ids, grads)


def self_forward_kernel(
    emb_ref, waves_ref, segments_ref, inward_ref, outward_ref, norms_ref,
    x0_ref, x1_ref, n1_ref, q_ref, k_ref, v_ref, c1_ref, n2_ref, qc_ref, lse_ref,
):
    rows, length = segments_ref.shape
    width = x0_ref.shape[1]
    scale = (width // HEADS) ** (-0.5)
    segments = segments_ref[...]
    low, _ = counts(segments, segments)
    index = lax.broadcasted_iota(jnp.int32, (1, length), 1)
    places = jnp.concatenate([index - low[r : r + 1, :] for r in range(rows)], 1)
    onehot = (
        lax.broadcasted_iota(jnp.int32, (length, rows * length), 0) == places
    ).astype(F32).astype(BF)
    rest = waves_ref[...]
    place = jnp.zeros(x0_ref.shape, F32)
    for _ in range(3):
        term = rest.astype(BF)
        rest = rest - term.astype(F32)
        place = place + dot_tn(onehot, term)
    x0 = math.sqrt(width) * flip(emb_ref[...].astype(F32)) + place
    x0_ref[...] = x0
    norms = norm_rows(norms_ref)
    unit, _ = norm_parts(x0)
    n1 = (unit * norms[0:1, :] + norms[1:2, :]).astype(BF)
    n1_ref[...] = n1
    q_ref[...] = (dot(n1, matrix(inward_ref, 0)) * scale).astype(BF)
    k_ref[...] = dot(n1, matrix(inward_ref, 1)).astype(BF)
    v_ref[...] = dot(n1, matrix(inward_ref, 2)).astype(BF)
    high = spread(lax.broadcasted_iota(jnp.int32, (1, length), 1) + 1)
    for r in range(rows):
        span = slice(r * length, (r + 1) * length)
        scores = scores_of(
            k_ref[span, :], head_columns(flip(q_ref[span, :])), spread(low[r : r + 1, :]), high
        )
        probs, logsum = softmax_columns(scores)
        lse_ref[r : r + 1, :] = logsum
        c1_ref[span, :] = flip(
            own_blocks(dot_tn(v_ref[span, :], probs.astype(BF)), length)
        ).astype(BF)
    x1 = x0 + dot(c1_ref[...], matrix(outward_ref, 0))
    x1_ref[...] = x1
    unit, _ = norm_parts(x1)
    n2 = (unit * norms[2:3, :] + norms[3:4, :]).astype(BF)
    n2_ref[...] = n2
    qc_ref[...] = (dot(n2, matrix(inward_ref, 3)) * scale).astype(BF)


def self_forward(emb, waves, segments, stack):
    rows, length = segments.shape
    width, tokens = emb.shape
    wide = shape_of((tokens, width), F32)
    thin = shape_of((tokens, width), BF)
    return pl.pallas_call(
        self_forward_kernel,
        in_specs=[
            full_spec(emb.shape), full_spec(waves.shape), full_spec(segments.shape),
            stack_spec(stack, 4, 0), stack_spec(stack, 1, 6), stack_spec(stack, 1, 8),
        ],
        grid=(1,),
        out_specs=[full_spec((tokens, width))] * 9 + [full_spec((rows, HEADS * length))],
        out_shape=[wide, wide, thin, thin, thin, thin, thin, thin, thin,
                   shape_of((rows, HEADS * length), F32)],
        compiler_params=params(ROOMY),
        cost_estimate=cost(2 * tokens * width * width * 8, 8 * tokens * width * 4),
        name="self_forward",
    )(emb, waves, segments, stack, stack, stack)


def pieces_of(part, count):
    early = part // 32 * 16
    return [
        piece
        for i in range(count)
        for piece in ([(i, 0, early), (i, early, part - early)] if i == 2 else [(i, 0, part)])
    ]


def frame_tiles(frames):
    return [(at, min(SPAN, frames - at)) for at in range(0, frames, SPAN)]


def interleave(rows, size, back):
    count = rows * size
    out = lax.broadcasted_iota(jnp.int32, (count, count), 0)
    source = lax.broadcasted_iota(jnp.int32, (count, count), 1)
    inner = rows if back else size
    return (source == (out % inner) * (count // inner) + out // inner).astype(F32).astype(BF)


def cross_forward_kernel(rows, pieces, here_ref, *refs):
    *memory_refs, inward_ref, qc_ref, tokens_ref, frames_ref = refs[:-5]
    c2_ref, held_ref, lse_ref, flat_ref, by_row_ref = refs[-5:]
    row = pl.program_id(0)
    part, width = memory_refs[0].shape
    frames = flat_ref.shape[0] // rows
    length = qc_ref.shape[0]

    @pl.when(row == 0)
    def _():
        for (i, at, size), ref in zip(pieces, memory_refs):
            start = pl.multiple_of((here_ref[0] ^ i) * part + at, 16)
            flat_ref[pl.ds(start, size), :] = ref[...]
        turns = {size: interleave(rows, size, False) for _, size in frame_tiles(frames)}
        for at, size in frame_tiles(frames):
            block = dot(turns[size], flat_ref[at * rows : (at + size) * rows, :]).astype(BF)
            for r in range(rows):
                by_row_ref[r, at : at + size, :] = block[r * size : (r + 1) * size, :]

    memory = by_row_ref[row]
    held_ref[0] = memory
    keys = dot(memory, matrix(inward_ref, 0)).astype(BF)
    values = dot(memory, matrix(inward_ref, 1)).astype(BF)
    low, high = counts(frames_ref[pl.ds(row, 1), :], tokens_ref[pl.ds(row, 1), :])
    scores = scores_of(keys, head_columns(flip(qc_ref[...])), spread(low), spread(high))
    probs, logsum = softmax_columns(scores)
    lse_ref[0] = logsum
    c2_ref[...] = flip(own_blocks(dot_tn(values, probs.astype(BF)), length)).astype(BF)


def cross_forward(here, memory, stack, query, tokens, frame_segments):
    rows, length = tokens.shape
    part, width = memory[0].shape
    pieces = pieces_of(part, sum(a.shape[0] for a in memory) // part)
    total = sum(size for _, _, size in pieces)
    frames = total // rows
    block = pl.BlockSpec((length, width), lambda i: (i, 0))
    return pl.pallas_call(
        functools.partial(cross_forward_kernel, rows, pieces),
        grid=(rows,),
        in_specs=[
            pl.BlockSpec(memory_space=pltpu.SMEM), *[full_spec(a.shape) for a in memory],
            stack_spec(stack, 2, 4), block, full_spec(tokens.shape),
            full_spec(frame_segments.shape),
        ],
        out_specs=[
            block, pl.BlockSpec((1, frames, width), lambda i: (i, 0, 0)),
            pl.BlockSpec((1, 1, HEADS * length), lambda i: (i, 0, 0)),
        ],
        out_shape=[
            shape_of((rows * length, width), BF),
            shape_of((rows, frames, width), BF),
            shape_of((rows, 1, HEADS * length), F32),
        ],
        scratch_shapes=[
            pltpu.VMEM((total, width), BF), pltpu.VMEM((rows, frames, width), BF),
        ],
        compiler_params=params(TIGHT),
        cost_estimate=cost(
            2 * total * width * 2 * width + 4 * total * length * HEADS * width, 6 * total * width
        ),
        name="cross_forward",
    )(here, *memory, stack, query, tokens, frame_segments)


def feed_kernel(
    packed, x1_ref, c2_ref, outward_ref, norms_ref, expand_ref, shrink_ref, cot_ref,
    out_ref, dx2_ref, gff_ref, gnorm_ref, total_ref, dn_ref,
):
    parts, owners = gff_ref.shape[0], gff_ref.shape[1]
    blocks = expand_ref.shape[1] // parts
    groups = shrink_ref.shape[0] // parts
    norms = norm_rows(norms_ref)
    x2 = x1_ref[...] + dot(c2_ref[...], matrix(outward_ref, 0))
    width = x2.shape[1]
    unit, inverse = norm_parts(x2)
    gain = norms[4:5, :]
    n3 = (unit * gain + norms[5:6, :]).astype(BF)
    n3_flipped = flip(n3)
    cot = cot_ref[...]
    cot_flipped = flip(cot)
    total_ref[...] = x2
    first = math.sqrt(2.0 / math.pi)
    for j in range(parts):
        expand = jnp.concatenate([matrix(expand_ref, j * blocks + b) for b in range(blocks)], 1)
        shrink = shrink_ref[j * groups : (j + 1) * groups].reshape(-1, width)
        chunk = shrink.shape[0]
        before = dot(n3, expand)
        square = before * before
        tanh = jnp.tanh(before * (first + (first * 0.044715) * square))
        half = 0.5 * before
        wing = 0.5 + 0.5 * tanh
        active = (before * wing).astype(BF)
        slope = wing + half * (1.0 - tanh * tanh) * (first + (3.0 * first * 0.044715) * square)
        grad = (dot_nt(cot, shrink) * slope).astype(BF)
        total_ref[...] += dot(active, shrink)
        gexp = dot(n3_flipped, grad).astype(BF)
        gshr = flip(dot(cot_flipped, active)).astype(BF)
        share = chunk * parts // (parts * owners)
        if packed:
            rows = width // owners
            for o in range(chunk // (share * parts)):
                for q in range(parts):
                    at = (o * parts + q) * share
                    owner = j * (chunk // (share * parts)) + o
                    gff_ref[q, owner, 0:share, :] = gshr[at : at + share, :]
            for b in range(chunk // width):
                for o in range(owners):
                    gff_ref[j, o, share + b * rows : share + (b + 1) * rows, :] = gexp[
                        o * rows : (o + 1) * rows, b * width : (b + 1) * width
                    ]
        else:
            gff_ref[j, 0, 0:chunk, :] = gshr
            for b in range(chunk // width):
                gff_ref[j, 0, chunk + b * width : chunk + (b + 1) * width, :] = gexp[
                    :, b * width : (b + 1) * width
                ]
        back = dot_nt(grad, expand)
        if j == 0:
            dn_ref[...] = back
        else:
            dn_ref[...] += back
    out_ref[...] = total_ref[...].astype(BF)
    grad, both = norm_back(dn_ref[...], unit, inverse, gain)
    dx2_ref[...] = cot.astype(F32) + grad
    gnorm_ref[...] = both


def feed(x1, c2, stack, wide, cot, parts, owners):
    tokens, width = x1.shape
    groups, blocks, rows, _ = wide.shape
    blocks //= 2
    hidden = groups * blocks * rows
    packed = width // owners % 16 == 0 and hidden // (parts * owners) % 16 == 0
    shape = (parts, owners if packed else 1, 2 * hidden // (parts * (owners if packed else 1)), width)
    result = pl.pallas_call(
        functools.partial(feed_kernel, packed),
        grid=(1,),
        in_specs=[
            full_spec(x1.shape), full_spec(c2.shape), stack_spec(stack, 1, 7),
            stack_spec(stack, 1, 8), stack_spec(wide, blocks, 0), stack_spec(wide, blocks, blocks),
            full_spec(cot.shape),
        ],
        out_specs=[
            full_spec((tokens, width)), full_spec((tokens, width)), full_spec(shape),
            full_spec((2, width)),
        ],
        out_shape=[
            shape_of((tokens, width), BF), shape_of((tokens, width), F32), shape_of(shape, BF),
            shape_of((2, width), F32),
        ],
        scratch_shapes=[pltpu.VMEM((tokens, width), F32), pltpu.VMEM((tokens, width), F32)],
        compiler_params=params(TIGHT),
        cost_estimate=cost(12 * tokens * width * hidden, 12 * width * hidden),
        name="feed",
    )(x1, c2, stack, stack, wide, wide, cot)
    out, dx2, gff, gnorm = result
    if not packed:
        chunk = hidden // parts
        gshr = gff[:, 0, :chunk].reshape(owners, parts, hidden // (parts * owners), width)
        gexp = gff[:, 0, chunk:].reshape(parts, chunk // width, owners, width // owners, width)
        gff = jnp.concatenate(
            [
                gshr.transpose(1, 0, 2, 3),
                gexp.transpose(0, 2, 1, 3, 4).reshape(parts, owners, -1, width),
            ],
            2,
        )
    return out, dx2, gff, gnorm


def cross_backward_kernel(
    rows, pieces, here_ref, dx2_ref, c2_ref, outward_ref, qc_ref, held_ref, lse_ref, tokens_ref,
    frames_ref, n2_ref, x1_ref, inward_ref, norms_ref, *refs,
):
    frame_refs = refs[: len(pieces)]
    dx1_ref, gweight_ref, gnorm_ref, dc_ref, dq_ref, flat_ref, by_row_ref = refs[len(pieces) :]
    row = pl.program_id(0)
    part, width = frame_refs[0].shape
    frames = flat_ref.shape[0] // rows
    length = qc_ref.shape[0]
    scale = (width // HEADS) ** (-0.5)

    @pl.when(row == 0)
    def _():
        rounded = dx2_ref[...].astype(BF)
        gweight_ref[3] = dot_tn(c2_ref[...], rounded)
        dc_ref[...] = dot_nt(rounded, matrix(outward_ref, 0)).astype(BF)
        gweight_ref[1] = jnp.zeros((width, width), F32)
        gweight_ref[2] = jnp.zeros((width, width), F32)

    span = pl.ds(pl.multiple_of(row * length, length), length)
    low, high = counts(frames_ref[pl.ds(row, 1), :], tokens_ref[pl.ds(row, 1), :])
    key_weight, value_weight = matrix(inward_ref, 1), matrix(inward_ref, 2)
    memory = held_ref[0]
    keys = dot(memory, key_weight).astype(BF)
    values = dot(memory, value_weight).astype(BF)
    dquery, dkeys, dvalues = attention_back(
        keys, values, qc_ref[...], dc_ref[span, :], spread(low), spread(high), lse_ref[0]
    )
    dq_ref[span, :] = dquery.astype(BF)
    dkeys, dvalues = dkeys.astype(BF), dvalues.astype(BF)
    gweight_ref[1] += dot_tn(memory, dkeys)
    gweight_ref[2] += dot_tn(memory, dvalues)
    by_row_ref[row] = (dot_nt(dkeys, key_weight) + dot_nt(dvalues, value_weight)).astype(BF)

    @pl.when(row == rows - 1)
    def _():
        turns = {size: interleave(rows, size, True) for _, size in frame_tiles(frames)}
        for at, size in frame_tiles(frames):
            block = jnp.concatenate([by_row_ref[r, at : at + size, :] for r in range(rows)], 0)
            flat_ref[at * rows : (at + size) * rows, :] = dot(turns[size], block).astype(BF)
        for (i, at, size), ref in zip(pieces, frame_refs):
            start = pl.multiple_of((here_ref[0] ^ i) * part + at, 16)
            ref[...] = flat_ref[pl.ds(start, size), :]
        dq = dq_ref[...]
        gweight_ref[0] = dot_tn(n2_ref[...], dq) * scale
        unit, inverse = norm_parts(x1_ref[...])
        grad, both = norm_back(
            dot_nt(dq, matrix(inward_ref, 0)) * scale, unit, inverse, norm_rows(norms_ref)[2:3, :]
        )
        dx1_ref[...] = dx2_ref[...] + grad
        gnorm_ref[...] = both


def cross_backward(here, dx2, c2, query, held, logsum, segments, frame_segments, n2, x1, stack, count):
    rows, length = segments.shape
    _, frames, width = held.shape
    total = rows * frames
    tokens = rows * length
    pieces = pieces_of(total // count, count)
    block = pl.BlockSpec((length, width), lambda i: (i, 0))
    return pl.pallas_call(
        functools.partial(cross_backward_kernel, rows, pieces),
        grid=(rows,),
        in_specs=[
            pl.BlockSpec(memory_space=pltpu.SMEM), full_spec(dx2.shape), full_spec(c2.shape),
            stack_spec(stack, 1, 7), block, pl.BlockSpec((1, frames, width), lambda i: (i, 0, 0)),
            pl.BlockSpec((1, 1, HEADS * length), lambda i: (i, 0, 0)), full_spec(segments.shape),
            full_spec(frame_segments.shape), full_spec(n2.shape), full_spec(x1.shape),
            stack_spec(stack, 3, 3), stack_spec(stack, 1, 8),
        ],
        out_specs=[
            *[full_spec((size, width)) for _, _, size in pieces], full_spec((tokens, width)),
            full_spec((4, width, width)), full_spec((2, width)),
        ],
        out_shape=[
            *[shape_of((size, width), BF) for _, _, size in pieces], shape_of((tokens, width), F32),
            shape_of((4, width, width), F32), shape_of((2, width), F32),
        ],
        scratch_shapes=[
            pltpu.VMEM((tokens, width), BF), pltpu.VMEM((tokens, width), BF),
            pltpu.VMEM((total, width), BF), pltpu.VMEM((rows, frames, width), BF),
        ],
        compiler_params=params(TIGHT),
        cost_estimate=cost(
            2 * total * width * 4 * width + 10 * total * length * HEADS * width, 8 * total * width
        ),
        name="cross_backward",
    )(here, dx2, c2, stack, query, held, logsum, segments, frame_segments, n2, x1, stack, stack)


def self_backward_kernel(
    dx1_ref, c1_ref, outward_ref, q_ref, k_ref, v_ref, lse_ref, segments_ref, n1_ref, x0_ref,
    inward_ref, norms_ref, dt_ref, gweight_ref, gnorm_ref, dc_ref, dq_ref, dk_ref, dv_ref,
):
    rows, length = segments_ref.shape
    width = x0_ref.shape[1]
    scale = (width // HEADS) ** (-0.5)
    low, _ = counts(segments_ref[...], segments_ref[...])
    dx1 = dx1_ref[...]
    rounded = dx1.astype(BF)
    gweight_ref[3] = dot_tn(c1_ref[...], rounded)
    dc_ref[...] = dot_nt(rounded, matrix(outward_ref, 0)).astype(BF)
    high = spread(lax.broadcasted_iota(jnp.int32, (1, length), 1) + 1)
    for r in range(rows):
        span = slice(r * length, (r + 1) * length)
        dquery, dkeys, dvalues = attention_back(
            k_ref[span, :], v_ref[span, :], q_ref[span, :], dc_ref[span, :],
            spread(low[r : r + 1, :]), high, lse_ref[r : r + 1, :],
        )
        dq_ref[span, :] = dquery.astype(BF)
        dk_ref[span, :] = dkeys.astype(BF)
        dv_ref[span, :] = dvalues.astype(BF)
    flipped = flip(n1_ref[...])
    gweight_ref[0] = dot(flipped, dq_ref[...]) * scale
    gweight_ref[1] = dot(flipped, dk_ref[...])
    gweight_ref[2] = dot(flipped, dv_ref[...])
    upstream = (
        dot_nt(dq_ref[...], matrix(inward_ref, 0)) * scale
        + dot_nt(dk_ref[...], matrix(inward_ref, 1))
        + dot_nt(dv_ref[...], matrix(inward_ref, 2))
    )
    unit, inverse = norm_parts(x0_ref[...])
    grad, both = norm_back(upstream, unit, inverse, norm_rows(norms_ref)[0:1, :])
    gnorm_ref[...] = both
    dt_ref[...] = flip(math.sqrt(width) * (dx1 + grad)).astype(BF)


def self_backward(dx1, c1, query, keys, values, logsum, segments, n1, x0, stack):
    tokens, width = dx1.shape
    ins = (dx1, c1, query, keys, values, logsum, segments, n1, x0)
    specs = [full_spec(a.shape) for a in ins]
    return pl.pallas_call(
        self_backward_kernel,
        grid=(1,),
        in_specs=specs[:2] + [stack_spec(stack, 1, 6)] + specs[2:]
        + [stack_spec(stack, 3, 0), stack_spec(stack, 1, 8)],
        out_specs=[full_spec((width, tokens)), full_spec((4, width, width)), full_spec((2, width))],
        out_shape=[
            shape_of((width, tokens), BF), shape_of((4, width, width), F32),
            shape_of((2, width), F32),
        ],
        scratch_shapes=[pltpu.VMEM((tokens, width), BF)] * 4,
        compiler_params=params(ROOMY),
        cost_estimate=cost(2 * tokens * width * width * 12, 8 * tokens * width * 4),
        name="self_backward",
    )(*ins[:2], stack, *ins[2:], stack, stack)


def bits_of(count):
    return count.bit_length() - 1


def swap(values, axis, bit, count):
    return lax.ppermute(values, axis, [(i, i ^ (1 << bit)) for i in range(count)])


def side(axis, bit):
    return (lax.axis_index(axis) >> bit) & 1


def halve(values, dim, axis, bit, count):
    mine = side(axis, bit)
    keep = lax.dynamic_index_in_dim(values, mine, dim, keepdims=False)
    send = lax.dynamic_index_in_dim(values, 1 - mine, dim, keepdims=False).astype(BF)
    return keep.astype(F32) + swap(send, axis, bit, count).astype(F32)


def halve_send(values, dim, axis, bit, count):
    mine = side(axis, bit)
    keep = lax.dynamic_index_in_dim(values, mine, dim, keepdims=False)
    send = lax.dynamic_index_in_dim(values, 1 - mine, dim, keepdims=False).astype(BF)
    return keep, swap(send, axis, bit, count)


def both_halves(values, dim, axis, bit, count):
    other = swap(values, axis, bit, count)
    mine = side(axis, bit) == 0
    return jnp.stack([jnp.where(mine, values, other), jnp.where(mine, other, values)], dim)


def quarter_sum(values, m):
    here = lax.axis_index("seq")
    pieces = [lax.dynamic_index_in_dim(values, here ^ i, 0, keepdims=False) for i in range(m)]
    pieces = [
        (lax.ppermute(a.astype(BF), "seq", [(p, p ^ i) for p in range(m)]) if i else a).astype(F32)
        for i, a in enumerate(pieces)
    ]
    return functools.reduce(jnp.add, pieces)


def gather_all(values, axis, bits, count):
    size, low_bit = 1 << len(bits), bits[0]
    mine = (lax.axis_index(axis) >> low_bit) & (size - 1)
    pieces = jnp.stack(
        [values]
        + [
            lax.ppermute(values, axis, [(p, p ^ (i << low_bit)) for p in range(count)])
            for i in range(1, size)
        ]
    )
    return jnp.stack(
        [lax.dynamic_index_in_dim(pieces, mine ^ i, 0, keepdims=False) for i in range(size)]
    )


tie = lax.optimization_barrier


def mark_kernel(source_ref, small_ref, out_ref):
    del source_ref
    out_ref[...] = small_ref[...]


def mark(source, small, *later):
    small = pl.pallas_call(
        mark_kernel,
        in_specs=[pl.BlockSpec(memory_space=pl.ANY), pl.BlockSpec(memory_space=pltpu.VMEM)],
        out_specs=pl.BlockSpec(memory_space=pltpu.VMEM),
        out_shape=shape_of(small.shape, small.dtype),
        compiler_params=pltpu.CompilerParams(vmem_limit_bytes=1024 * 1024),
        cost_estimate=cost(0, 100e6),
        name="mark",
    )(source, small)
    return tie((small, *later))


def regroup(values, rows):
    groups, count, part, width = values.shape
    return (
        values.transpose(1, 0, 2, 3).reshape(count, groups * part // rows, rows, width)
        .transpose(1, 0, 2, 3)
    )


def own_half(values, dim):
    half = values.shape[dim] // 2
    return lax.dynamic_slice_in_dim(values, side("seq", 0) * half, half, dim)


def encode(place, width):
    halves = jnp.arange(width // 2, dtype=F32)
    freq = jnp.exp(halves * (-2.0 * math.log(10000.0) / width))
    angle = place[..., None] * freq
    return jnp.stack([jnp.sin(angle), jnp.cos(angle)], -1).reshape(place.shape + (width,))


def assemble_kernel(pieces, here_ref, *refs):
    out_ref = refs[-1]
    for (i, at, size), ref in zip(pieces, refs):
        out_ref[pl.ds(at, size), pl.ds(here_ref[0] ^ i, 1)] = ref[...][:, None]


def assemble(here, pieces, count):
    frames, rows, width = pieces[0].shape
    places = [(i, at // rows, size // rows) for i, at, size in pieces_of(frames * rows, count)]
    return pl.pallas_call(
        functools.partial(assemble_kernel, places),
        grid=(1,),
        in_specs=[pl.BlockSpec(memory_space=pltpu.SMEM)] + [full_spec(a.shape) for a in pieces],
        out_specs=full_spec((frames, count, rows, width)),
        out_shape=shape_of((frames, count, rows, width), pieces[0].dtype),
        compiler_params=params(TIGHT),
        cost_estimate=cost(0, 4 * count * frames * rows * width),
        name="assemble",
    )(here, *pieces)


def square_kernel(part_ref, dense_ref, out_ref):
    dense = dense_ref[...]
    dense = dense * dense
    total = part_ref[...]
    for i in range(dense.shape[0] // 8):
        for j in range(dense.shape[1] // LANES):
            total = total + dense[i * 8 : (i + 1) * 8, j * LANES : (j + 1) * LANES]
    for i in range(out_ref.shape[0]):
        out_ref[i] = total


def square_blocks(part, dense, count):
    return pl.pallas_call(
        square_kernel,
        grid=(1,),
        in_specs=[full_spec(part.shape), full_spec(dense.shape)],
        out_specs=full_spec((count, 8, LANES)),
        out_shape=shape_of((count, 8, LANES), F32),
        compiler_params=params(TIGHT),
        cost_estimate=cost(dense.size, 4 * dense.size),
        name="square_blocks",
    )(part, dense)


def adam_kernel(squares_ref, gtable_ref, dense_ref, *refs):
    masters, firsts, seconds = refs[0:6], refs[6:12], refs[12:18]
    norm_ref, outs = refs[18], refs[19:]
    total = jnp.sum(jnp.sum(squares_ref[...], 0), keepdims=True)
    norm = jnp.sqrt(total)
    norm_ref[...] = norm
    factor = CLIP / jnp.maximum(norm, CLIP)
    parts, _, width = dense_ref.shape
    share = masters[5].shape[1]
    part = masters[1].shape[1]
    hidden = masters[3].shape[1]
    cut = masters[4].shape[0] // parts
    late = dense_ref.shape[1] - 2 * part - 8

    def update(i, at, gradient, rate):
        first_m = 1.0 / (1 - BETA_ONE**STEP)
        first_s = 1.0 / (1 - BETA_TWO**STEP)
        clipped = gradient * factor
        moment = BETA_ONE * firsts[i][at] + (1 - BETA_ONE) * clipped
        square = BETA_TWO * seconds[i][at] + (1 - BETA_TWO) * clipped * clipped
        master = masters[i][at]
        weight = master - rate * (
            (moment * first_m) / (jnp.sqrt(square * first_s) + ADAM_EPS) + DECAY * master
        )
        for ref, value in zip(outs[5 * i : 5 * i + 5], (clipped, moment, square, weight, weight)):
            ref[at] = value.astype(ref.dtype)

    everything = (slice(None), slice(None))
    update(0, everything, gtable_ref[:, 0 : masters[0].shape[1]], RATE)
    for i in range(parts):
        for a in range(2):
            gradient = dense_ref[i, late + a * part : late + (a + 1) * part, :]
            if i < 3:
                update(1, (3 - 3 * a + i, slice(None), slice(None)), gradient, RATE)
            else:
                update(2, (1 - a, slice(None), slice(None)), gradient, RATE)
        blocks = hidden // (parts * width)
        for b in range(blocks):
            at = (i * blocks + b) * width
            update(
                3, (slice(None), slice(at, at + width)),
                dense_ref[i, cut + b * part : cut + (b + 1) * part, :], RATE,
            )
        update(4, (slice(i * cut, (i + 1) * cut), slice(None)), dense_ref[i, 0:cut, :], RATE)
    update(5, everything, dense_ref[0, late + 2 * part : late + 2 * part + 6, 0:share], NORM_RATE)


def adam(squares, gtable, dense, state):
    shapes = [shape_of((1, 1), F32)] + [
        shape_of(a.shape, kind) for a in state[:6] for kind in (F32, F32, F32, F32, BF)
    ]
    ins = (squares, gtable, dense, *state)
    norm, *results = pl.pallas_call(
        adam_kernel,
        grid=(1,),
        in_specs=[full_spec(a.shape) for a in ins],
        out_specs=[full_spec(a.shape) for a in shapes],
        out_shape=shapes,
        compiler_params=params(ROOMY),
        cost_estimate=cost(0, 34 * sum(a.size for a in state[:6])),
        name="adam",
    )(*ins)
    return norm, results


def body(n, m, *args):
    masters, firsts, seconds = args[0:6], args[6:12], args[12:18]
    memory, token_ids, dec_segments, mem_segments, cotangent = args[18:23]
    table_master, inward_master, outward_master, expand_master, shrink_master, norms_master = masters
    rates = (RATE, RATE, RATE, RATE, RATE, NORM_RATE)
    rows, length = token_ids.shape
    tokens = rows * length
    vocab, share = table_master.shape
    width = inward_master.shape[2]
    hidden = expand_master.shape[1]
    part = inward_master.shape[1]
    frames = mem_segments.shape[1]
    padded = -(-vocab // (2 * BASE)) * 2 * BASE

    copies = jnp.broadcast_to(token_ids[None], (n * m, rows, length))
    ids = lax.all_to_all(copies, ("dp", "seq"), 0, 0).reshape(n * m, 1, tokens)
    norms_now, inward_now, outward_now, memory = mark(
        copies, norms_master, inward_master, outward_master, memory
    )

    here = lax.axis_index("seq")
    flipped = memory.transpose(1, 0, 2).reshape(frames // m, m, rows, width)
    routes = pieces_of(frames // m * rows, m)

    def frames_from(source, route):
        i, at, size = route
        own = lax.dynamic_index_in_dim(source, here ^ i, 1, keepdims=False)
        own = own.reshape(-1, width)[at : at + size]
        return lax.ppermute(own, "seq", [(p, p ^ i) for p in range(m)]) if i else own

    first_piece = frames_from(flipped, routes[2])
    line_ids = lax.dynamic_index_in_dim(
        ids.reshape(n, m, 1, tokens), here, 1, keepdims=False
    )

    norm_block = lax.dynamic_update_slice(
        jnp.zeros((1, max(part, 16), width), F32), norms_now[None],
        (0, 0, lax.axis_index("dp") * share),
    )
    blocks = own_half(jnp.concatenate([inward_now, outward_now], 0), 1)
    if part == 32:
        blocks = jnp.concatenate([blocks, own_half(norm_block, 1)], 0)
    upper = list(range(1, bits_of(n)))
    narrow = gather_all(blocks.astype(BF), "dp", upper[:2], n)
    table_flipped = jnp.pad(table_master.T, ((0, -share % 8), (0, padded - vocab)))

    found = lookup(line_ids, table_flipped)[:, :share]
    narrow = both_halves(narrow, 1, "dp", 0, n)
    found, narrow, first_piece, flipped, expand_now, shrink_now = tie(
        (found, narrow, first_piece, flipped, expand_master, shrink_master)
    )
    emb = lax.all_to_all(found, "dp", 0, 0).reshape(width, tokens)
    mem_rows = [first_piece if j == 2 else frames_from(flipped, r) for j, r in enumerate(routes)]
    here = here.reshape(1).astype(jnp.int32)
    if upper[2:]:
        narrow = gather_all(narrow, "dp", upper[2:], n)
        narrow = narrow.reshape((-1,) + narrow.shape[2:])
    narrow = both_halves(narrow, 2, "seq", 0, m)

    wide = jnp.concatenate(
        [
            own_half(expand_now, 0).reshape(part // 2, hidden // width, width).transpose(1, 0, 2),
            own_half(shrink_now, 0).reshape(hidden // width, part // 2, width),
        ],
        0,
    )
    wide = gather_all(wide.astype(BF), "dp", upper[:2], n)
    if upper[2:]:
        wide = gather_all(wide, "dp", upper[2:], n)
        wide = wide.reshape((-1,) + wide.shape[2:])

    waves = encode(jnp.arange(length).astype(F32), width)
    emb, narrow, mem_rows[3] = tie((emb, narrow, mem_rows[3]))
    stack = narrow.reshape((2 * n,) + narrow.shape[3:])
    if part != 32:
        norms = lax.psum(norm_block[:, :16].astype(BF).astype(F32), "dp").astype(BF)
        stack = regroup(stack, 16)
        norms = jnp.pad(norms[None], ((0, stack.shape[0] - 1), (0, 0), (0, 0), (0, 0)))
        stack = jnp.concatenate([stack, norms], 1)

    x0, x1, n1, q, k, v, c1, n2, qc, lse1 = self_forward(emb, waves, dec_segments, stack)
    qc, wide = tie((qc, wide))
    wide = both_halves(wide, 1, "dp", 0, n)
    c2, held, lse2 = cross_forward(here, mem_rows, stack, qc, dec_segments, mem_segments)
    c2, wide = tie((c2, wide))
    wide = both_halves(wide, 2, "seq", 0, m)
    wide = wide.reshape((2 * n,) + wide.shape[3:])
    if part != 32:
        count = hidden // width
        shrink = wide[:, count:].reshape(width // 16, count, 16, width)
        wide = jnp.concatenate([regroup(wide[:, :count], 16), shrink], 1)
    block_out, dx2, gff, gnorm3 = feed(
        x1, c2, stack, wide, cotangent.reshape(tokens, width), m, n
    )
    *frame, dx1, gcross, gnorm2 = cross_backward(
        here, dx2, c2, qc, held, lse2, dec_segments, mem_segments, n2, x1, stack, m
    )
    gff = quarter_sum(gff, m)
    dx1, gff = tie((dx1, gff))
    frame = [
        lax.ppermute(a, "seq", [(p, p ^ i) for p in range(m)]) if i else a
        for (i, _, _), a in zip(routes, frame)
    ]
    dt, gself, gnorm1 = self_backward(dx1, c1, q, k, v, lse1, dec_segments, n1, x0, stack)
    cut = gff.shape[1]
    early = jnp.concatenate(
        [gff, gcross.reshape(m, n, part, width).transpose(1, 0, 2, 3).reshape(n, -1, width)], 1
    )
    early = early.reshape((2,) * bits_of(n) + early.shape[1:])
    kept, came = halve_send(early, bits_of(n) - 1, "dp", 0, n)
    dt, kept, came, frame[2] = tie((dt, kept, came, frame[2]))
    early = kept.astype(F32) + came.astype(F32)

    few = share // m
    arrived = lax.all_to_all(dt.reshape(n * m, few, tokens), ("dp", "seq"), 0, 0)
    arrived = jnp.pad(arrived, ((0, 0), (0, -few % 8), (0, 0)))

    gnorm = jnp.concatenate([gnorm1, gnorm2, gnorm3], 0)
    gnorm = jnp.pad(
        gnorm.reshape(6, n, share).transpose(1, 0, 2)[:, None],
        ((0, 0), (0, m - 1), (0, 2), (0, width - share)),
    )
    late = jnp.concatenate(
        [gself.reshape(m, n, part, width).transpose(1, 0, 2, 3), gnorm], 2
    )
    late = late.reshape((2,) * bits_of(n) + (-1, width))
    late = halve(late, bits_of(n) - 1, "dp", 0, n)
    early = halve(early, early.ndim - 3, "dp", 1, n)
    arrived, late, early = tie((arrived, late, early))
    gtable, squares = table_grad(ids, arrived, padded)
    late = halve(late, late.ndim - 3, "dp", 1, n)
    for bit in range(2, bits_of(n)):
        early = halve(early, early.ndim - 3, "dp", bit, n)
    gtable, late, early, *frame = tie((gtable, late, early, *frame))
    for bit in range(2, bits_of(n)):
        late = halve(late, late.ndim - 3, "dp", bit, n)
    returned = assemble(here, [a.reshape(-1, rows, width) for a in frame], m)
    returned = returned.reshape(frames // m, m * rows, width).transpose(1, 0, 2)
    late_sum = quarter_sum(
        jnp.concatenate(
            [early[cut:].reshape(m, part, width), late.reshape(m, -1, width)], 1
        ), m,
    )
    dense = jnp.concatenate([early[:cut], late_sum], 0)
    squares = square_blocks(squares, dense, n * m)
    squares = lax.all_to_all(squares, ("dp", "seq"), 0, 0)

    gtable = gtable[:few]
    for i, bit in enumerate(reversed(range(bits_of(m)))):
        gtable = both_halves(gtable, i, "seq", bit, m)
    gtable = gtable.reshape(share, padded)
    dense = both_halves(dense, 0, "seq", 1, m)
    dense = both_halves(dense, 1, "seq", 0, m).reshape(m, -1, width)
    grad_norm, results = adam(
        squares, gtable, dense,
        [(a.T if i == 0 else a) for group in (masters, firsts, seconds) for i, a in enumerate(group)],
    )
    results = [(a.T if i < 5 else a) for i, a in enumerate(results)]
    return (block_out.reshape(rows, length, width), returned, grad_norm.reshape(()), *results)


def solution(mesh):
    n, m = mesh.shape["dp"], mesh.shape["seq"]
    state = (
        P(None, "dp"), P(None, "dp", None), P(None, "dp", None),
        P("dp", None), P("dp", None), P(None, "dp"),
    )
    flat = P(("dp", "seq"), None)
    deep = P(("dp", "seq"), None, None)
    in_specs = state * 3 + (P("dp", "seq", None), flat, flat, flat, deep)
    out_specs = (deep, P("dp", "seq", None), P()) + tuple(s for s in state for _ in range(5))
    return jax.shard_map(
        functools.partial(body, n, m), mesh=mesh, in_specs=in_specs, out_specs=out_specs, check_vma=False
    )
```

```python
import functools
import math

import jax
import jax.numpy as jnp
from jax import lax
from jax.experimental import pallas as pl
from jax.experimental.pallas import tpu as pltpu
from jax.sharding import PartitionSpec as P

HEADS = 4
STEP = 5
EPS = 1e-05
NEG = -1e30
CLIP = 300.0
RATE = 0.05
NORM_RATE = 0.3
BETA_ONE = 0.5
BETA_TWO = 0.5
DECAY = 0.01
ADAM_EPS = 1e-08
BF = jnp.bfloat16
F32 = jnp.float32
ROOMY = 56 * 1024 * 1024
TIGHT = 28 * 1024 * 1024
BASE = 256
LANES = 128
SPAN = 32


def dot(left, right):
    return jnp.dot(left, right, preferred_element_type=F32)


def dot_nt(left, right):
    return lax.dot_general(left, right, (((1,), (1,)), ((), ())), preferred_element_type=F32)


def dot_tn(left, right):
    return lax.dot_general(left, right, (((0,), (0,)), ((), ())), preferred_element_type=F32)


def norm_parts(stream):
    center = stream - jnp.mean(stream, -1, keepdims=True)
    inverse = lax.rsqrt(jnp.mean(center * center, -1, keepdims=True) + EPS)
    return center * inverse, inverse


def norm_back(upstream, unit, inverse, gain):
    scaled = upstream * gain
    grad = inverse * (
        scaled
        - jnp.mean(scaled, -1, keepdims=True)
        - unit * jnp.mean(scaled * unit, -1, keepdims=True)
    )
    both = jnp.concatenate(
        [jnp.sum(upstream * unit, 0, keepdims=True), jnp.sum(upstream, 0, keepdims=True)], 0
    )
    return grad, both


def head_columns(flipped):
    width, length = flipped.shape
    wide = jnp.concatenate([flipped] * HEADS, 1)
    row = lax.broadcasted_iota(jnp.int32, wide.shape, 0) // (width // HEADS)
    column = lax.broadcasted_iota(jnp.int32, wide.shape, 1) // length
    return jnp.where(row == column, wide, jnp.zeros_like(wide))


def head_rows(values):
    length, width = values.shape
    tall = jnp.concatenate([values] * HEADS, 0)
    row = lax.broadcasted_iota(jnp.int32, tall.shape, 0) // length
    column = lax.broadcasted_iota(jnp.int32, tall.shape, 1) // (width // HEADS)
    return jnp.where(row == column, tall, jnp.zeros_like(tall))


def own_blocks(wide, length):
    part = wide.shape[0] // HEADS
    return jnp.concatenate(
        [
            wide[h * part : (h + 1) * part, h * length : (h + 1) * length]
            for h in range(HEADS)
        ],
        0,
    )


def flip(values):
    return values.T


def scores_of(keys, columns, low, high):
    scores = dot(keys, columns)
    place = lax.broadcasted_iota(jnp.int32, scores.shape, 0)
    return jnp.where((place >= low) & (place < high), scores, NEG)


def spread(bounds):
    return jnp.concatenate([bounds] * HEADS, 1)


def counts(segments, tokens):
    low = jnp.zeros(tokens.shape, jnp.int32)
    high = jnp.zeros(tokens.shape, jnp.int32)
    values = segments.astype(F32)
    for s in range(4):
        below = jnp.sum((values < s).astype(F32), 1, keepdims=True).astype(jnp.int32)
        upto = jnp.sum((values < s + 1).astype(F32), 1, keepdims=True).astype(jnp.int32)
        low = jnp.where(tokens == s, below, low)
        high = jnp.where(tokens == s, upto, high)
    return low, high


def softmax_columns(scores):
    peak = jnp.max(scores, 0, keepdims=True)
    expo = jnp.exp(scores - peak)
    total = jnp.sum(expo, 0, keepdims=True)
    return expo * (1.0 / total), peak + jnp.log(total)


def attention_back(keys, values, query, dcontext, low, high, logsum):
    length = query.shape[0]
    query_columns = head_columns(flip(query))
    grad_rows = head_rows(dcontext)
    probs = jnp.exp(scores_of(keys, query_columns, low, high) - logsum)
    dvalues = dot(probs.astype(BF), grad_rows)
    dprobs = dot_nt(values, grad_rows)
    inner = jnp.sum(dprobs * probs, 0, keepdims=True)
    dscores = (probs * (dprobs - inner)).astype(BF)
    dkeys = dot(dscores, head_rows(query))
    dquery = flip(own_blocks(dot_tn(keys, dscores), length))
    return dquery, dkeys, dvalues


def matrix(ref, i):
    block = ref[:, i]
    return block.reshape(block.shape[0] * block.shape[1], block.shape[2])


def norm_rows(ref):
    return jnp.sum(ref[:, 0].astype(F32), 0)


def stack_spec(stack, count, at):
    groups, _, rows, width = stack.shape
    return pl.BlockSpec((groups, count, rows, width), lambda *_: (0, at // count, 0, 0))


def full_spec(shape):
    return pl.BlockSpec(shape, lambda *_: (0,) * len(shape))


def shape_of(shape, kind):
    return jax.ShapeDtypeStruct(shape, kind)


def params(limit):
    return pltpu.CompilerParams(vmem_limit_bytes=limit, dimension_semantics=("arbitrary",))


def cost(flops, data):
    return pl.CostEstimate(flops=int(flops), bytes_accessed=int(data), transcendentals=0)


def one_hot(rest):
    place = lax.broadcasted_iota(jnp.int32, (BASE, rest.shape[1]), 0).astype(BF)
    return jnp.where(place == rest.astype(F32).astype(BF), jnp.ones((), BF), jnp.zeros((), BF))


def lookup_kernel(ids_ref, table_ref, out_ref, split_ref):
    width = table_ref.shape[0]
    blocks = split_ref.shape[0] // width

    @pl.when(pl.program_id(0) == 0)
    def _():
        for b in range(blocks):
            split_ref[b * width : (b + 1) * width, :] = table_ref[:, b * BASE : (b + 1) * BASE]

    ids = ids_ref[0]
    lead = ids >> 8
    rest = ids & (BASE - 1)
    onehot = one_hot(rest)
    found = dot(split_ref[...].astype(BF), onehot)
    total = jnp.zeros((width, ids.shape[1]), F32)
    for b in range(blocks):
        total = jnp.where(lead == b, found[b * width : (b + 1) * width, :], total)
    out_ref[0] = total.astype(BF)


def lookup(ids, table):
    count, _, tokens = ids.shape
    width, padded = table.shape
    blocks = padded // BASE
    return pl.pallas_call(
        lookup_kernel,
        grid=(count,),
        in_specs=[
            pl.BlockSpec((1, 1, tokens), lambda i: (i, 0, 0)),
            full_spec((width, padded)),
        ],
        out_specs=pl.BlockSpec((1, width, tokens), lambda i: (i, 0, 0)),
        out_shape=shape_of((count, width, tokens), BF),
        scratch_shapes=[pltpu.VMEM((blocks * width, BASE), F32)],
        compiler_params=params(TIGHT),
        cost_estimate=cost(
            2 * blocks * width * BASE * tokens * count, 4 * width * padded + 2 * count * width * tokens
        ),
        name="lookup",
    )(ids, table)


def table_grad_kernel(ids_ref, grads_ref, out_ref, square_ref, total_ref):
    count, width, _ = grads_ref.shape
    blocks = total_ref.shape[0] // width
    ids = jnp.concatenate([ids_ref[i] for i in range(count)], 1)
    grads = jnp.concatenate([grads_ref[i].astype(F32) for i in range(count)], 1)
    lead = ids >> 8
    rest = ids & (BASE - 1)
    onehot = one_hot(rest)
    spreads = jnp.concatenate(
        [jnp.where(lead == b, grads, 0.0) for b in range(blocks)], 0
    ).astype(BF)
    part = dot_nt(spreads, onehot)
    step = pl.program_id(0)

    @pl.when(step == 0)
    def _():
        total_ref[...] = part

    @pl.when(step > 0)
    def _():
        total_ref[...] += part

    @pl.when(step == pl.num_programs(0) - 1)
    def _():
        total = jnp.zeros(square_ref.shape, F32)
        for b in range(blocks):
            value = total_ref[b * width : (b + 1) * width, :]
            out_ref[:, b * BASE : (b + 1) * BASE] = value
            for i in range(0, width, 8):
                for j in range(0, BASE, LANES):
                    piece = value[i : i + 8, j : j + LANES]
                    total = total + piece * piece
        square_ref[...] = total


def table_grad(ids, grads, padded):
    count, width, tokens = grads.shape
    blocks = padded // BASE
    group = 8
    return pl.pallas_call(
        table_grad_kernel,
        grid=(count // group,),
        in_specs=[
            pl.BlockSpec((group, 1, tokens), lambda i: (i, 0, 0)),
            pl.BlockSpec((group, width, tokens), lambda i: (i, 0, 0)),
        ],
        out_specs=[full_spec((width, padded)), full_spec((8, LANES))],
        out_shape=[shape_of((width, padded), F32), shape_of((8, LANES), F32)],
        scratch_shapes=[pltpu.VMEM((blocks * width, BASE), F32)],
        compiler_params=params(TIGHT),
        cost_estimate=cost(
            2 * blocks * width * BASE * tokens * count, 4 * width * padded + 2 * count * width * tokens
        ),
        name="table_grad",
    )(ids, grads)


def embed(emb_ref, waves_ref, low):
    rows, length = low.shape
    width, tokens = emb_ref.shape
    index = lax.broadcasted_iota(jnp.int32, (1, length), 1)
    places = jnp.concatenate([index - low[r : r + 1, :] for r in range(rows)], 1)
    onehot = (
        lax.broadcasted_iota(jnp.int32, (length, tokens), 0) == places
    ).astype(F32).astype(BF)
    rest = waves_ref[...]
    place = jnp.zeros((tokens, width), F32)
    for _ in range(3):
        term = rest.astype(BF)
        rest = rest - term.astype(F32)
        place = place + dot_tn(onehot, term)
    return math.sqrt(width) * flip(emb_ref[...].astype(F32)) + place


def self_inputs(n1, inward_ref, scale, q_ref, k_ref, v_ref):
    q_ref[...] = (dot(n1, matrix(inward_ref, 0)) * scale).astype(BF)
    k_ref[...] = dot(n1, matrix(inward_ref, 1)).astype(BF)
    v_ref[...] = dot(n1, matrix(inward_ref, 2)).astype(BF)


def self_forward_kernel(
    emb_ref, waves_ref, segments_ref, inward_ref, outward_ref, norms_ref,
    x1_ref, c1_ref, n2_ref, qc_ref, lse_ref, q_ref, k_ref, v_ref,
):
    rows, length = segments_ref.shape
    width = x1_ref.shape[1]
    scale = (width // HEADS) ** (-0.5)
    segments = segments_ref[...]
    low, _ = counts(segments, segments)
    x0 = embed(emb_ref, waves_ref, low)
    norms = norm_rows(norms_ref)
    unit, _ = norm_parts(x0)
    n1 = (unit * norms[0:1, :] + norms[1:2, :]).astype(BF)
    self_inputs(n1, inward_ref, scale, q_ref, k_ref, v_ref)
    high = spread(lax.broadcasted_iota(jnp.int32, (1, length), 1) + 1)
    for r in range(rows):
        span = slice(r * length, (r + 1) * length)
        scores = scores_of(
            k_ref[span, :], head_columns(flip(q_ref[span, :])), spread(low[r : r + 1, :]), high
        )
        probs, logsum = softmax_columns(scores)
        lse_ref[r : r + 1, :] = logsum
        c1_ref[span, :] = flip(
            own_blocks(dot_tn(v_ref[span, :], probs.astype(BF)), length)
        ).astype(BF)
    x1 = x0 + dot(c1_ref[...], matrix(outward_ref, 0))
    x1_ref[...] = x1
    unit, _ = norm_parts(x1)
    n2 = (unit * norms[2:3, :] + norms[3:4, :]).astype(BF)
    n2_ref[...] = n2
    qc_ref[...] = (dot(n2, matrix(inward_ref, 3)) * scale).astype(BF)


def self_forward(emb, waves, segments, stack):
    rows, length = segments.shape
    width, tokens = emb.shape
    thin = shape_of((tokens, width), BF)
    return pl.pallas_call(
        self_forward_kernel,
        in_specs=[
            full_spec(emb.shape), full_spec(waves.shape), full_spec(segments.shape),
            stack_spec(stack, 4, 0), stack_spec(stack, 1, 6), stack_spec(stack, 1, 8),
        ],
        grid=(1,),
        out_specs=[full_spec((tokens, width))] * 4 + [full_spec((rows, HEADS * length))],
        out_shape=[shape_of((tokens, width), F32), thin, thin, thin,
                   shape_of((rows, HEADS * length), F32)],
        scratch_shapes=[pltpu.VMEM((tokens, width), BF)] * 3,
        compiler_params=params(TIGHT),
        cost_estimate=cost(2 * tokens * width * width * 8, 8 * tokens * width * 4),
        name="self_forward",
    )(emb, waves, segments, stack, stack, stack)


def pieces_of(part, count):
    early = part // 32 * 16
    return [
        piece
        for i in range(count)
        for piece in ([(i, 0, early), (i, early, part - early)] if i == 2 else [(i, 0, part)])
    ]


def frame_tiles(frames):
    return [(at, min(SPAN, frames - at)) for at in range(0, frames, SPAN)]


def interleave(rows, size, back):
    count = rows * size
    out = lax.broadcasted_iota(jnp.int32, (count, count), 0)
    source = lax.broadcasted_iota(jnp.int32, (count, count), 1)
    inner = rows if back else size
    return (source == (out % inner) * (count // inner) + out // inner).astype(F32).astype(BF)


def cross_forward_kernel(rows, pieces, here_ref, *refs):
    *memory_refs, inward_ref, qc_ref, tokens_ref, frames_ref = refs[:-6]
    c2_ref, held_ref, lse_ref, flat_ref, by_row_ref, sem = refs[-6:]
    row = pl.program_id(0)
    part, width = memory_refs[0].shape
    frames = flat_ref.shape[0] // rows
    length = qc_ref.shape[0]

    @pl.when(row == 0)
    def _():
        copies = []
        for j, ((i, at, size), ref) in enumerate(zip(pieces, memory_refs)):
            start = pl.multiple_of((here_ref[0] ^ i) * part + at, 16)
            copies.append(
                pltpu.make_async_copy(ref, flat_ref.at[pl.ds(start, size), :], sem.at[j])
            )
        for copy in copies:
            copy.start()
        for copy in copies:
            copy.wait()
        turns = {size: interleave(rows, size, False) for _, size in frame_tiles(frames)}
        for at, size in frame_tiles(frames):
            block = dot(turns[size], flat_ref[at * rows : (at + size) * rows, :]).astype(BF)
            for r in range(rows):
                by_row_ref[r, at : at + size, :] = block[r * size : (r + 1) * size, :]

    memory = by_row_ref[row]
    held_ref[0] = memory
    keys = dot(memory, matrix(inward_ref, 0)).astype(BF)
    values = dot(memory, matrix(inward_ref, 1)).astype(BF)
    low, high = counts(frames_ref[pl.ds(row, 1), :], tokens_ref[pl.ds(row, 1), :])
    scores = scores_of(keys, head_columns(flip(qc_ref[...])), spread(low), spread(high))
    probs, logsum = softmax_columns(scores)
    lse_ref[0] = logsum
    c2_ref[...] = flip(own_blocks(dot_tn(values, probs.astype(BF)), length)).astype(BF)


def cross_forward(here, memory, stack, query, tokens, frame_segments):
    rows, length = tokens.shape
    part, width = memory[0].shape
    pieces = pieces_of(part, sum(a.shape[0] for a in memory) // part)
    total = sum(size for _, _, size in pieces)
    frames = total // rows
    block = pl.BlockSpec((length, width), lambda i: (i, 0))
    return pl.pallas_call(
        functools.partial(cross_forward_kernel, rows, pieces),
        grid=(rows,),
        in_specs=[
            pl.BlockSpec(memory_space=pltpu.SMEM),
            *[pl.BlockSpec(memory_space=pl.ANY)] * len(memory),
            stack_spec(stack, 2, 4), block, full_spec(tokens.shape),
            full_spec(frame_segments.shape),
        ],
        out_specs=[
            block, pl.BlockSpec((1, frames, width), lambda i: (i, 0, 0)),
            pl.BlockSpec((1, 1, HEADS * length), lambda i: (i, 0, 0)),
        ],
        out_shape=[
            shape_of((rows * length, width), BF),
            shape_of((rows, frames, width), BF),
            shape_of((rows, 1, HEADS * length), F32),
        ],
        scratch_shapes=[
            pltpu.VMEM((total, width), BF), pltpu.VMEM((rows, frames, width), BF),
            pltpu.SemaphoreType.DMA((len(memory),)),
        ],
        compiler_params=params(TIGHT),
        cost_estimate=cost(
            2 * total * width * 2 * width + 4 * total * length * HEADS * width, 6 * total * width
        ),
        name="cross_forward",
    )(here, *memory, stack, query, tokens, frame_segments)


def feed_kernel(
    packed, x1_ref, c2_ref, outward_ref, norms_ref, expand_ref, shrink_ref, cot_ref,
    out_ref, dx2_ref, gff_ref, gnorm_ref, total_ref, dn_ref,
):
    parts, owners = gff_ref.shape[0], gff_ref.shape[1]
    blocks = expand_ref.shape[1] // parts
    groups = shrink_ref.shape[0] // parts
    norms = norm_rows(norms_ref)
    x2 = x1_ref[...] + dot(c2_ref[...], matrix(outward_ref, 0))
    width = x2.shape[1]
    unit, inverse = norm_parts(x2)
    gain = norms[4:5, :]
    n3 = (unit * gain + norms[5:6, :]).astype(BF)
    n3_flipped = flip(n3)
    cot = cot_ref[...]
    cot_flipped = flip(cot)
    total_ref[...] = x2
    first = math.sqrt(2.0 / math.pi)
    for j in range(parts):
        expand = jnp.concatenate([matrix(expand_ref, j * blocks + b) for b in range(blocks)], 1)
        shrink = shrink_ref[j * groups : (j + 1) * groups].reshape(-1, width)
        chunk = shrink.shape[0]
        before = dot(n3, expand)
        square = before * before
        tanh = jnp.tanh(before * (first + (first * 0.044715) * square))
        half = 0.5 * before
        wing = 0.5 + 0.5 * tanh
        active = (before * wing).astype(BF)
        slope = wing + half * (1.0 - tanh * tanh) * (first + (3.0 * first * 0.044715) * square)
        grad = (dot_nt(cot, shrink) * slope).astype(BF)
        total_ref[...] += dot(active, shrink)
        gexp = dot(n3_flipped, grad).astype(BF)
        gshr = flip(dot(cot_flipped, active)).astype(BF)
        share = chunk * parts // (parts * owners)
        if packed:
            rows = width // owners
            for o in range(chunk // (share * parts)):
                for q in range(parts):
                    at = (o * parts + q) * share
                    owner = j * (chunk // (share * parts)) + o
                    gff_ref[q, owner, 0:share, :] = gshr[at : at + share, :]
            for b in range(chunk // width):
                for o in range(owners):
                    gff_ref[j, o, share + b * rows : share + (b + 1) * rows, :] = gexp[
                        o * rows : (o + 1) * rows, b * width : (b + 1) * width
                    ]
        else:
            gff_ref[j, 0, 0:chunk, :] = gshr
            for b in range(chunk // width):
                gff_ref[j, 0, chunk + b * width : chunk + (b + 1) * width, :] = gexp[
                    :, b * width : (b + 1) * width
                ]
        back = dot_nt(grad, expand)
        if j == 0:
            dn_ref[...] = back
        else:
            dn_ref[...] += back
    out_ref[...] = total_ref[...].astype(BF)
    grad, both = norm_back(dn_ref[...], unit, inverse, gain)
    dx2_ref[...] = cot.astype(F32) + grad
    gnorm_ref[...] = both


def feed(x1, c2, stack, wide, cot, parts, owners):
    tokens, width = x1.shape
    groups, blocks, rows, _ = wide.shape
    blocks //= 2
    hidden = groups * blocks * rows
    packed = width // owners % 16 == 0 and hidden // (parts * owners) % 16 == 0
    shape = (parts, owners if packed else 1, 2 * hidden // (parts * (owners if packed else 1)), width)
    result = pl.pallas_call(
        functools.partial(feed_kernel, packed),
        grid=(1,),
        in_specs=[
            full_spec(x1.shape), full_spec(c2.shape), stack_spec(stack, 1, 7),
            stack_spec(stack, 1, 8), stack_spec(wide, blocks, 0), stack_spec(wide, blocks, blocks),
            full_spec(cot.shape),
        ],
        out_specs=[
            full_spec((tokens, width)), full_spec((tokens, width)), full_spec(shape),
            full_spec((2, width)),
        ],
        out_shape=[
            shape_of((tokens, width), BF), shape_of((tokens, width), F32), shape_of(shape, BF),
            shape_of((2, width), F32),
        ],
        scratch_shapes=[pltpu.VMEM((tokens, width), F32), pltpu.VMEM((tokens, width), F32)],
        compiler_params=params(TIGHT),
        cost_estimate=cost(12 * tokens * width * hidden, 12 * width * hidden),
        name="feed",
    )(x1, c2, stack, stack, wide, wide, cot)
    out, dx2, gff, gnorm = result
    if not packed:
        chunk = hidden // parts
        gshr = gff[:, 0, :chunk].reshape(owners, parts, hidden // (parts * owners), width)
        gexp = gff[:, 0, chunk:].reshape(parts, chunk // width, owners, width // owners, width)
        gff = jnp.concatenate(
            [
                gshr.transpose(1, 0, 2, 3),
                gexp.transpose(0, 2, 1, 3, 4).reshape(parts, owners, -1, width),
            ],
            2,
        )
    return out, dx2, gff, gnorm


def cross_backward_kernel(
    rows, pieces, here_ref, dx2_ref, c2_ref, outward_ref, qc_ref, held_ref, lse_ref, tokens_ref,
    frames_ref, n2_ref, x1_ref, inward_ref, norms_ref, *refs,
):
    frame_refs = refs[: len(pieces)]
    dx1_ref, gweight_ref, gnorm_ref, dc_ref, dq_ref, flat_ref, by_row_ref = refs[len(pieces) :]
    row = pl.program_id(0)
    part, width = frame_refs[0].shape
    frames = flat_ref.shape[0] // rows
    length = qc_ref.shape[0]
    scale = (width // HEADS) ** (-0.5)

    @pl.when(row == 0)
    def _():
        rounded = dx2_ref[...].astype(BF)
        gweight_ref[3] = dot_tn(c2_ref[...], rounded)
        dc_ref[...] = dot_nt(rounded, matrix(outward_ref, 0)).astype(BF)
        gweight_ref[1] = jnp.zeros((width, width), F32)
        gweight_ref[2] = jnp.zeros((width, width), F32)

    span = pl.ds(pl.multiple_of(row * length, length), length)
    low, high = counts(frames_ref[pl.ds(row, 1), :], tokens_ref[pl.ds(row, 1), :])
    key_weight, value_weight = matrix(inward_ref, 1), matrix(inward_ref, 2)
    memory = held_ref[0]
    keys = dot(memory, key_weight).astype(BF)
    values = dot(memory, value_weight).astype(BF)
    dquery, dkeys, dvalues = attention_back(
        keys, values, qc_ref[...], dc_ref[span, :], spread(low), spread(high), lse_ref[0]
    )
    dq_ref[span, :] = dquery.astype(BF)
    dkeys, dvalues = dkeys.astype(BF), dvalues.astype(BF)
    gweight_ref[1] += dot_tn(memory, dkeys)
    gweight_ref[2] += dot_tn(memory, dvalues)
    by_row_ref[row] = (dot_nt(dkeys, key_weight) + dot_nt(dvalues, value_weight)).astype(BF)

    @pl.when(row == rows - 1)
    def _():
        turns = {size: interleave(rows, size, True) for _, size in frame_tiles(frames)}
        for at, size in frame_tiles(frames):
            block = jnp.concatenate([by_row_ref[r, at : at + size, :] for r in range(rows)], 0)
            flat_ref[at * rows : (at + size) * rows, :] = dot(turns[size], block).astype(BF)
        for (i, at, size), ref in zip(pieces, frame_refs):
            start = pl.multiple_of((here_ref[0] ^ i) * part + at, 16)
            ref[...] = flat_ref[pl.ds(start, size), :]
        dq = dq_ref[...]
        gweight_ref[0] = dot_tn(n2_ref[...], dq) * scale
        unit, inverse = norm_parts(x1_ref[...])
        grad, both = norm_back(
            dot_nt(dq, matrix(inward_ref, 0)) * scale, unit, inverse, norm_rows(norms_ref)[2:3, :]
        )
        dx1_ref[...] = dx2_ref[...] + grad
        gnorm_ref[...] = both


def cross_backward(here, dx2, c2, query, held, logsum, segments, frame_segments, n2, x1, stack, count):
    rows, length = segments.shape
    _, frames, width = held.shape
    total = rows * frames
    tokens = rows * length
    pieces = pieces_of(total // count, count)
    block = pl.BlockSpec((length, width), lambda i: (i, 0))
    return pl.pallas_call(
        functools.partial(cross_backward_kernel, rows, pieces),
        grid=(rows,),
        in_specs=[
            pl.BlockSpec(memory_space=pltpu.SMEM), full_spec(dx2.shape), full_spec(c2.shape),
            stack_spec(stack, 1, 7), block, pl.BlockSpec((1, frames, width), lambda i: (i, 0, 0)),
            pl.BlockSpec((1, 1, HEADS * length), lambda i: (i, 0, 0)), full_spec(segments.shape),
            full_spec(frame_segments.shape), full_spec(n2.shape), full_spec(x1.shape),
            stack_spec(stack, 3, 3), stack_spec(stack, 1, 8),
        ],
        out_specs=[
            *[full_spec((size, width)) for _, _, size in pieces], full_spec((tokens, width)),
            full_spec((4, width, width)), full_spec((2, width)),
        ],
        out_shape=[
            *[shape_of((size, width), BF) for _, _, size in pieces], shape_of((tokens, width), F32),
            shape_of((4, width, width), F32), shape_of((2, width), F32),
        ],
        scratch_shapes=[
            pltpu.VMEM((tokens, width), BF), pltpu.VMEM((tokens, width), BF),
            pltpu.VMEM((total, width), BF), pltpu.VMEM((rows, frames, width), BF),
        ],
        compiler_params=params(TIGHT),
        cost_estimate=cost(
            2 * total * width * 4 * width + 10 * total * length * HEADS * width, 8 * total * width
        ),
        name="cross_backward",
    )(here, dx2, c2, stack, query, held, logsum, segments, frame_segments, n2, x1, stack, stack)


def self_backward_kernel(
    dx1_ref, c1_ref, outward_ref, lse_ref, segments_ref, emb_ref, waves_ref,
    inward_ref, norms_ref, dt_ref, gweight_ref, gnorm_ref,
    dc_ref, dq_ref, dk_ref, dv_ref, q_ref, k_ref, v_ref,
):
    rows, length = segments_ref.shape
    width = dx1_ref.shape[1]
    scale = (width // HEADS) ** (-0.5)
    low, _ = counts(segments_ref[...], segments_ref[...])
    x0 = embed(emb_ref, waves_ref, low)
    norms = norm_rows(norms_ref)
    unit, inverse = norm_parts(x0)
    n1 = (unit * norms[0:1, :] + norms[1:2, :]).astype(BF)
    self_inputs(n1, inward_ref, scale, q_ref, k_ref, v_ref)
    dx1 = dx1_ref[...]
    rounded = dx1.astype(BF)
    gweight_ref[3] = dot_tn(c1_ref[...], rounded)
    dc_ref[...] = dot_nt(rounded, matrix(outward_ref, 0)).astype(BF)
    high = spread(lax.broadcasted_iota(jnp.int32, (1, length), 1) + 1)
    for r in range(rows):
        span = slice(r * length, (r + 1) * length)
        dquery, dkeys, dvalues = attention_back(
            k_ref[span, :], v_ref[span, :], q_ref[span, :], dc_ref[span, :],
            spread(low[r : r + 1, :]), high, lse_ref[r : r + 1, :],
        )
        dq_ref[span, :] = dquery.astype(BF)
        dk_ref[span, :] = dkeys.astype(BF)
        dv_ref[span, :] = dvalues.astype(BF)
    flipped = flip(n1)
    gweight_ref[0] = dot(flipped, dq_ref[...]) * scale
    gweight_ref[1] = dot(flipped, dk_ref[...])
    gweight_ref[2] = dot(flipped, dv_ref[...])
    upstream = (
        dot_nt(dq_ref[...], matrix(inward_ref, 0)) * scale
        + dot_nt(dk_ref[...], matrix(inward_ref, 1))
        + dot_nt(dv_ref[...], matrix(inward_ref, 2))
    )
    grad, both = norm_back(upstream, unit, inverse, norms[0:1, :])
    gnorm_ref[...] = both
    dt_ref[...] = flip(math.sqrt(width) * (dx1 + grad)).astype(BF)


def self_backward(dx1, c1, logsum, segments, emb, waves, stack):
    tokens, width = dx1.shape
    ins = (dx1, c1, logsum, segments, emb, waves)
    specs = [full_spec(a.shape) for a in ins]
    return pl.pallas_call(
        self_backward_kernel,
        grid=(1,),
        in_specs=specs[:2] + [stack_spec(stack, 1, 6)] + specs[2:]
        + [stack_spec(stack, 3, 0), stack_spec(stack, 1, 8)],
        out_specs=[full_spec((width, tokens)), full_spec((4, width, width)), full_spec((2, width))],
        out_shape=[
            shape_of((width, tokens), BF), shape_of((4, width, width), F32),
            shape_of((2, width), F32),
        ],
        scratch_shapes=[pltpu.VMEM((tokens, width), BF)] * 7,
        compiler_params=params(ROOMY),
        cost_estimate=cost(2 * tokens * width * width * 12, 8 * tokens * width * 4),
        name="self_backward",
    )(*ins[:2], stack, *ins[2:], stack, stack)


def bits_of(count):
    return count.bit_length() - 1


def swap(values, axis, bit, count):
    return lax.ppermute(values, axis, [(i, i ^ (1 << bit)) for i in range(count)])


def side(axis, bit):
    return (lax.axis_index(axis) >> bit) & 1


def halve(values, dim, axis, bit, count):
    mine = side(axis, bit)
    keep = lax.dynamic_index_in_dim(values, mine, dim, keepdims=False)
    send = lax.dynamic_index_in_dim(values, 1 - mine, dim, keepdims=False).astype(BF)
    return keep.astype(F32) + swap(send, axis, bit, count).astype(F32)


def halve_send(values, dim, axis, bit, count):
    mine = side(axis, bit)
    keep = lax.dynamic_index_in_dim(values, mine, dim, keepdims=False)
    send = lax.dynamic_index_in_dim(values, 1 - mine, dim, keepdims=False).astype(BF)
    return keep, swap(send, axis, bit, count)


def both_halves(values, dim, axis, bit, count):
    return in_order(values, swap(values, axis, bit, count), dim, axis, bit)


def in_order(values, other, dim, axis, bit):
    mine = side(axis, bit) == 0
    return jnp.stack([jnp.where(mine, values, other), jnp.where(mine, other, values)], dim)


def quarter_sum(values, m):
    here = lax.axis_index("seq")
    pieces = [lax.dynamic_index_in_dim(values, here ^ i, 0, keepdims=False) for i in range(m)]
    pieces = [
        (lax.ppermute(a.astype(BF), "seq", [(p, p ^ i) for p in range(m)]) if i else a).astype(F32)
        for i, a in enumerate(pieces)
    ]
    return functools.reduce(jnp.add, pieces)


def gather_all(values, axis, bits, count, beside=None):
    size, low_bit = 1 << len(bits), bits[0]
    mine = (lax.axis_index(axis) >> low_bit) & (size - 1)
    pieces = [values] + [
        lax.ppermute(values, axis, [(p, p ^ (i << low_bit)) for p in range(count)])
        for i in range(1, size)
    ]
    if beside is not None:
        beside, *pieces = tie((beside, *pieces))
    pieces = jnp.stack(pieces)
    ordered = jnp.stack(
        [lax.dynamic_index_in_dim(pieces, mine ^ i, 0, keepdims=False) for i in range(size)]
    )
    return ordered if beside is None else (ordered, beside)


tie = lax.optimization_barrier


def mark_kernel(source_ref, small_ref, out_ref):
    del source_ref
    out_ref[...] = small_ref[...]


def mark(source, small, *later):
    small = pl.pallas_call(
        mark_kernel,
        in_specs=[pl.BlockSpec(memory_space=pl.ANY), pl.BlockSpec(memory_space=pltpu.VMEM)],
        out_specs=pl.BlockSpec(memory_space=pltpu.VMEM),
        out_shape=shape_of(small.shape, small.dtype),
        compiler_params=pltpu.CompilerParams(vmem_limit_bytes=1024 * 1024),
        cost_estimate=cost(0, 100e6),
        name="mark",
    )(source, small)
    return tie((small, *later))


def regroup(values, rows):
    groups, count, part, width = values.shape
    return (
        values.transpose(1, 0, 2, 3).reshape(count, groups * part // rows, rows, width)
        .transpose(1, 0, 2, 3)
    )


def own_half(values, dim):
    half = values.shape[dim] // 2
    return lax.dynamic_slice_in_dim(values, side("seq", 0) * half, half, dim)


def encode(place, width):
    halves = jnp.arange(width // 2, dtype=F32)
    freq = jnp.exp(halves * (-2.0 * math.log(10000.0) / width))
    angle = place[..., None] * freq
    return jnp.stack([jnp.sin(angle), jnp.cos(angle)], -1).reshape(place.shape + (width,))


def assemble_kernel(pieces, here_ref, *refs):
    out_ref = refs[-1]
    for (i, at, size), ref in zip(pieces, refs):
        out_ref[pl.ds(at, size), pl.ds(here_ref[0] ^ i, 1)] = ref[...][:, None]


def assemble(here, pieces, count):
    frames, rows, width = pieces[0].shape
    places = [(i, at // rows, size // rows) for i, at, size in pieces_of(frames * rows, count)]
    return pl.pallas_call(
        functools.partial(assemble_kernel, places),
        grid=(1,),
        in_specs=[pl.BlockSpec(memory_space=pltpu.SMEM)] + [full_spec(a.shape) for a in pieces],
        out_specs=full_spec((frames, count, rows, width)),
        out_shape=shape_of((frames, count, rows, width), pieces[0].dtype),
        compiler_params=params(TIGHT),
        cost_estimate=cost(0, 4 * count * frames * rows * width),
        name="assemble",
    )(here, *pieces)


def square_kernel(part_ref, dense_ref, out_ref):
    dense = dense_ref[...]
    dense = dense * dense
    total = part_ref[...]
    for i in range(dense.shape[0] // 8):
        for j in range(dense.shape[1] // LANES):
            total = total + dense[i * 8 : (i + 1) * 8, j * LANES : (j + 1) * LANES]
    for i in range(out_ref.shape[0]):
        out_ref[i] = total


def square_blocks(part, dense, count):
    return pl.pallas_call(
        square_kernel,
        grid=(1,),
        in_specs=[full_spec(part.shape), full_spec(dense.shape)],
        out_specs=full_spec((count, 8, LANES)),
        out_shape=shape_of((count, 8, LANES), F32),
        compiler_params=params(TIGHT),
        cost_estimate=cost(dense.size, 4 * dense.size),
        name="square_blocks",
    )(part, dense)


def adam_kernel(squares_ref, gtable_ref, dense_ref, *refs):
    masters, firsts, seconds = refs[0:6], refs[6:12], refs[12:18]
    norm_ref, outs = refs[18], refs[19:]
    total = jnp.sum(jnp.sum(squares_ref[...], 0), keepdims=True)
    norm = jnp.sqrt(total)
    norm_ref[...] = norm
    factor = CLIP / jnp.maximum(norm, CLIP)
    parts, _, width = dense_ref.shape
    share = masters[5].shape[1]
    part = masters[1].shape[1]
    hidden = masters[3].shape[1]
    cut = masters[4].shape[0] // parts
    late = dense_ref.shape[1] - 2 * part - 8

    def update(i, at, gradient, rate):
        first_m = 1.0 / (1 - BETA_ONE**STEP)
        first_s = 1.0 / (1 - BETA_TWO**STEP)
        clipped = gradient * factor
        moment = BETA_ONE * firsts[i][at] + (1 - BETA_ONE) * clipped
        square = BETA_TWO * seconds[i][at] + (1 - BETA_TWO) * clipped * clipped
        master = masters[i][at]
        weight = master - rate * (
            (moment * first_m) / (jnp.sqrt(square * first_s) + ADAM_EPS) + DECAY * master
        )
        for ref, value in zip(outs[5 * i : 5 * i + 5], (clipped, moment, square, weight, weight)):
            ref[at] = value.astype(ref.dtype)

    everything = (slice(None), slice(None))
    update(0, everything, gtable_ref[:, 0 : masters[0].shape[1]], RATE)
    for i in range(parts):
        for a in range(2):
            gradient = dense_ref[i, late + a * part : late + (a + 1) * part, :]
            if i < 3:
                update(1, (3 - 3 * a + i, slice(None), slice(None)), gradient, RATE)
            else:
                update(2, (1 - a, slice(None), slice(None)), gradient, RATE)
        blocks = hidden // (parts * width)
        for b in range(blocks):
            at = (i * blocks + b) * width
            update(
                3, (slice(None), slice(at, at + width)),
                dense_ref[i, cut + b * part : cut + (b + 1) * part, :], RATE,
            )
        update(4, (slice(i * cut, (i + 1) * cut), slice(None)), dense_ref[i, 0:cut, :], RATE)
    update(5, everything, dense_ref[0, late + 2 * part : late + 2 * part + 6, 0:share], NORM_RATE)


def adam(squares, gtable, dense, state):
    shapes = [shape_of((1, 1), F32)] + [
        shape_of(a.shape, kind) for a in state[:6] for kind in (F32, F32, F32, F32, BF)
    ]
    ins = (squares, gtable, dense, *state)
    norm, *results = pl.pallas_call(
        adam_kernel,
        grid=(1,),
        in_specs=[full_spec(a.shape) for a in ins],
        out_specs=[full_spec(a.shape) for a in shapes],
        out_shape=shapes,
        compiler_params=params(ROOMY),
        cost_estimate=cost(0, 34 * sum(a.size for a in state[:6])),
        name="adam",
    )(*ins)
    return norm, results


def body(n, m, *args):
    masters, firsts, seconds = args[0:6], args[6:12], args[12:18]
    memory, token_ids, dec_segments, mem_segments, cotangent = args[18:23]
    table_master, inward_master, outward_master, expand_master, shrink_master, norms_master = masters
    rates = (RATE, RATE, RATE, RATE, RATE, NORM_RATE)
    rows, length = token_ids.shape
    tokens = rows * length
    vocab, share = table_master.shape
    width = inward_master.shape[2]
    hidden = expand_master.shape[1]
    part = inward_master.shape[1]
    frames = mem_segments.shape[1]
    padded = -(-vocab // (2 * BASE)) * 2 * BASE

    copies = jnp.broadcast_to(token_ids[None], (n * m, rows, length))
    ids = lax.all_to_all(copies, ("dp", "seq"), 0, 0).reshape(n * m, 1, tokens)
    norms_now, inward_now, outward_now, memory = mark(
        copies, norms_master, inward_master, outward_master, memory
    )

    here = lax.axis_index("seq")
    flipped = memory.transpose(1, 0, 2).reshape(frames // m, m, rows, width)
    routes = pieces_of(frames // m * rows, m)

    def frames_from(source, route):
        i, at, size = route
        own = lax.dynamic_index_in_dim(source, here ^ i, 1, keepdims=False)
        own = own.reshape(-1, width)[at : at + size]
        return lax.ppermute(own, "seq", [(p, p ^ i) for p in range(m)]) if i else own

    first_piece, second_piece = frames_from(flipped, routes[2]), frames_from(flipped, routes[3])
    line_ids = lax.dynamic_index_in_dim(
        ids.reshape(n, m, 1, tokens), here, 1, keepdims=False
    )

    norm_block = lax.dynamic_update_slice(
        jnp.zeros((1, max(part, 16), width), F32), norms_now[None],
        (0, 0, lax.axis_index("dp") * share),
    )
    blocks = own_half(jnp.concatenate([inward_now, outward_now], 0), 1)
    if part == 32:
        blocks = jnp.concatenate([blocks, own_half(norm_block, 1)], 0)
    upper = list(range(1, bits_of(n)))
    narrow = gather_all(blocks.astype(BF), "dp", upper[:2], n)
    table_flipped = jnp.pad(table_master.T, ((0, -share % 8), (0, padded - vocab)))

    wide = jnp.concatenate(
        [
            own_half(expand_master, 0).reshape(part // 2, hidden // width, width).transpose(1, 0, 2),
            own_half(shrink_master, 0).reshape(hidden // width, part // 2, width),
        ],
        0,
    )
    wide = wide.astype(BF)
    found = lookup(line_ids, table_flipped)[:, :share]
    narrow = both_halves(narrow, 1, "dp", 0, n)
    wide, found = gather_all(wide, "dp", upper[:2], n, found)
    found, narrow, first_piece = tie((found, narrow, first_piece))
    emb = lax.all_to_all(found, "dp", 0, 0).reshape(width, tokens)
    if upper[2:]:
        narrow = gather_all(narrow, "dp", upper[2:], n)
        narrow = narrow.reshape((-1,) + narrow.shape[2:])
    other = swap(narrow, "seq", 0, m)
    narrow, other, second_piece, flipped = tie((narrow, other, second_piece, flipped))
    narrow = in_order(narrow, other, 2, "seq", 0)
    mem_rows = [
        (first_piece, second_piece)[j - 2] if j in (2, 3) else frames_from(flipped, r)
        for j, r in enumerate(routes)
    ]
    here = here.reshape(1).astype(jnp.int32)

    waves = encode(jnp.arange(length).astype(F32), width)
    emb, narrow = tie((emb, narrow))
    stack = narrow.reshape((2 * n,) + narrow.shape[3:])
    if part != 32:
        norms = lax.psum(norm_block[:, :16].astype(BF).astype(F32), "dp").astype(BF)
        stack = regroup(stack, 16)
        norms = jnp.pad(norms[None], ((0, stack.shape[0] - 1), (0, 0), (0, 0), (0, 0)))
        stack = jnp.concatenate([stack, norms], 1)

    x1, c1, n2, qc, lse1 = self_forward(emb, waves, dec_segments, stack)
    if upper[2:]:
        wide = gather_all(wide, "dp", upper[2:], n)
        wide = wide.reshape((-1,) + wide.shape[2:])
    along = swap(wide, "dp", 0, n)
    qc, along = tie((qc, along))
    wide = in_order(wide, along, 1, "dp", 0)
    across = swap(wide, "seq", 0, m)
    c2, held, lse2 = cross_forward(here, mem_rows, stack, qc, dec_segments, mem_segments)
    c2, across = tie((c2, across))
    wide = in_order(wide, across, 2, "seq", 0)
    wide = wide.reshape((2 * n,) + wide.shape[3:])
    if part != 32:
        count = hidden // width
        shrink = wide[:, count:].reshape(width // 16, count, 16, width)
        wide = jnp.concatenate([regroup(wide[:, :count], 16), shrink], 1)
    block_out, dx2, gff, gnorm3 = feed(
        x1, c2, stack, wide, cotangent.reshape(tokens, width), m, n
    )
    *frame, dx1, gcross, gnorm2 = cross_backward(
        here, dx2, c2, qc, held, lse2, dec_segments, mem_segments, n2, x1, stack, m
    )
    gff = quarter_sum(gff, m)
    dx1, gff = tie((dx1, gff))
    frame = [
        lax.ppermute(a, "seq", [(p, p ^ i) for p in range(m)]) if i else a
        for (i, _, _), a in zip(routes, frame)
    ]
    dt, gself, gnorm1 = self_backward(dx1, c1, lse1, dec_segments, emb, waves, stack)
    cut = gff.shape[1]
    early = jnp.concatenate(
        [gff, gcross.reshape(m, n, part, width).transpose(1, 0, 2, 3).reshape(n, -1, width)], 1
    )
    early = early.reshape((2,) * bits_of(n) + early.shape[1:])
    kept, came = halve_send(early, bits_of(n) - 1, "dp", 0, n)
    dt, came, frame[2], gself, gnorm1 = tie((dt, came, frame[2], gself, gnorm1))
    early = kept.astype(F32) + came.astype(F32)

    few = share // m
    arrived = lax.all_to_all(dt.reshape(n * m, few, tokens), ("dp", "seq"), 0, 0)
    arrived = jnp.pad(arrived, ((0, 0), (0, -few % 8), (0, 0)))

    gnorm = jnp.concatenate([gnorm1, gnorm2, gnorm3], 0)
    gnorm = jnp.pad(
        gnorm.reshape(6, n, share).transpose(1, 0, 2)[:, None],
        ((0, 0), (0, m - 1), (0, 2), (0, width - share)),
    )
    late = jnp.concatenate(
        [gself.reshape(m, n, part, width).transpose(1, 0, 2, 3), gnorm], 2
    )
    late = late.reshape((2,) * bits_of(n) + (-1, width))
    late = halve(late, bits_of(n) - 1, "dp", 0, n)
    early = halve(early, early.ndim - 3, "dp", 1, n)
    arrived, late, early = tie((arrived, late, early))
    gtable, squares = table_grad(ids, arrived, padded)
    late = halve(late, late.ndim - 3, "dp", 1, n)
    for bit in range(2, bits_of(n)):
        early = halve(early, early.ndim - 3, "dp", bit, n)
    gtable, late, early, *frame = tie((gtable, late, early, *frame))
    for bit in range(2, bits_of(n)):
        late = halve(late, late.ndim - 3, "dp", bit, n)
    returned = assemble(here, [a.reshape(-1, rows, width) for a in frame], m)
    returned = returned.reshape(frames // m, m * rows, width).transpose(1, 0, 2)
    late_sum = quarter_sum(
        jnp.concatenate(
            [early[cut:].reshape(m, part, width), late.reshape(m, -1, width)], 1
        ), m,
    )
    dense = jnp.concatenate([early[:cut], late_sum], 0)
    squares = square_blocks(squares, dense, n * m)
    squares = lax.all_to_all(squares, ("dp", "seq"), 0, 0)

    gtable = gtable[:few]
    for i, bit in enumerate(reversed(range(bits_of(m)))):
        gtable = both_halves(gtable, i, "seq", bit, m)
    gtable = gtable.reshape(share, padded)
    dense = both_halves(dense, 0, "seq", 1, m)
    dense = both_halves(dense, 1, "seq", 0, m).reshape(m, -1, width)
    grad_norm, results = adam(
        squares, gtable, dense,
        [(a.T if i == 0 else a) for group in (masters, firsts, seconds) for i, a in enumerate(group)],
    )
    results = [(a.T if i < 5 else a) for i, a in enumerate(results)]
    return (block_out.reshape(rows, length, width), returned, grad_norm.reshape(()), *results)


def solution(mesh):
    n, m = mesh.shape["dp"], mesh.shape["seq"]
    state = (
        P(None, "dp"), P(None, "dp", None), P(None, "dp", None),
        P("dp", None), P("dp", None), P(None, "dp"),
    )
    flat = P(("dp", "seq"), None)
    deep = P(("dp", "seq"), None, None)
    in_specs = state * 3 + (P("dp", "seq", None), flat, flat, flat, deep)
    out_specs = (deep, P("dp", "seq", None), P()) + tuple(s for s in state for _ in range(5))
    return jax.shard_map(
        functools.partial(body, n, m), mesh=mesh, in_specs=in_specs, out_specs=out_specs, check_vma=False
    )
```

```python
import functools
import math

import jax
import jax.numpy as jnp
from jax import lax
from jax.experimental import pallas as pl
from jax.experimental.pallas import tpu as pltpu
from jax.sharding import PartitionSpec as P

HEADS = 4
STEP = 5
EPS = 1e-05
NEG = -1e30
CLIP = 300.0
RATE = 0.05
NORM_RATE = 0.3
BETA_ONE = 0.5
BETA_TWO = 0.5
DECAY = 0.01
ADAM_EPS = 1e-08
BF = jnp.bfloat16
F32 = jnp.float32
ROOMY = 56 * 1024 * 1024
TIGHT = 28 * 1024 * 1024
SMALL = 18 * 1024 * 1024
BASE = 256
LANES = 128
SPAN = 32


def dot(left, right):
    return jnp.dot(left, right, preferred_element_type=F32)


def dot_nt(left, right):
    return lax.dot_general(left, right, (((1,), (1,)), ((), ())), preferred_element_type=F32)


def dot_tn(left, right):
    return lax.dot_general(left, right, (((0,), (0,)), ((), ())), preferred_element_type=F32)


def norm_parts(stream):
    center = stream - jnp.mean(stream, -1, keepdims=True)
    inverse = lax.rsqrt(jnp.mean(center * center, -1, keepdims=True) + EPS)
    return center * inverse, inverse


def norm_back(upstream, unit, inverse, gain):
    scaled = upstream * gain
    grad = inverse * (
        scaled
        - jnp.mean(scaled, -1, keepdims=True)
        - unit * jnp.mean(scaled * unit, -1, keepdims=True)
    )
    both = jnp.concatenate(
        [jnp.sum(upstream * unit, 0, keepdims=True), jnp.sum(upstream, 0, keepdims=True)], 0
    )
    return grad, both


def head_columns(flipped):
    width, length = flipped.shape
    wide = jnp.concatenate([flipped] * HEADS, 1)
    row = lax.broadcasted_iota(jnp.int32, wide.shape, 0) // (width // HEADS)
    column = lax.broadcasted_iota(jnp.int32, wide.shape, 1) // length
    return jnp.where(row == column, wide, jnp.zeros_like(wide))


def head_rows(values):
    length, width = values.shape
    tall = jnp.concatenate([values] * HEADS, 0)
    row = lax.broadcasted_iota(jnp.int32, tall.shape, 0) // length
    column = lax.broadcasted_iota(jnp.int32, tall.shape, 1) // (width // HEADS)
    return jnp.where(row == column, tall, jnp.zeros_like(tall))


def own_blocks(wide, length):
    part = wide.shape[0] // HEADS
    return jnp.concatenate(
        [
            wide[h * part : (h + 1) * part, h * length : (h + 1) * length]
            for h in range(HEADS)
        ],
        0,
    )


def flip(values):
    return values.T


def scores_of(keys, columns, low, high):
    scores = dot(keys, columns)
    place = lax.broadcasted_iota(jnp.int32, scores.shape, 0)
    return jnp.where((place >= low) & (place < high), scores, NEG)


def spread(bounds):
    return jnp.concatenate([bounds] * HEADS, 1)


def counts(segments, tokens):
    low = jnp.zeros(tokens.shape, jnp.int32)
    high = jnp.zeros(tokens.shape, jnp.int32)
    values = segments.astype(F32)
    for s in range(4):
        below = jnp.sum((values < s).astype(F32), 1, keepdims=True).astype(jnp.int32)
        upto = jnp.sum((values < s + 1).astype(F32), 1, keepdims=True).astype(jnp.int32)
        low = jnp.where(tokens == s, below, low)
        high = jnp.where(tokens == s, upto, high)
    return low, high


def softmax_columns(scores):
    peak = jnp.max(scores, 0, keepdims=True)
    expo = jnp.exp(scores - peak)
    total = jnp.sum(expo, 0, keepdims=True)
    return expo * (1.0 / total), peak + jnp.log(total)


def attention_back(keys, values, query, dcontext, low, high, logsum):
    length = query.shape[0]
    query_columns = head_columns(flip(query))
    grad_rows = head_rows(dcontext)
    probs = jnp.exp(scores_of(keys, query_columns, low, high) - logsum)
    dvalues = dot(probs.astype(BF), grad_rows)
    dprobs = dot_nt(values, grad_rows)
    inner = jnp.sum(dprobs * probs, 0, keepdims=True)
    dscores = (probs * (dprobs - inner)).astype(BF)
    dkeys = dot(dscores, head_rows(query))
    dquery = flip(own_blocks(dot_tn(keys, dscores), length))
    return dquery, dkeys, dvalues


def matrix(ref, i):
    block = ref[:, i]
    return block.reshape(block.shape[0] * block.shape[1], block.shape[2])


def norm_rows(ref):
    return jnp.sum(ref[:, 0].astype(F32), 0)


def stack_spec(stack, count, at):
    groups, _, rows, width = stack.shape
    return pl.BlockSpec((groups, count, rows, width), lambda *_: (0, at // count, 0, 0))


def full_spec(shape):
    return pl.BlockSpec(shape, lambda *_: (0,) * len(shape))


def shape_of(shape, kind):
    return jax.ShapeDtypeStruct(shape, kind)


def params(limit):
    return pltpu.CompilerParams(vmem_limit_bytes=limit, dimension_semantics=("arbitrary",))


def cost(flops, data):
    return pl.CostEstimate(flops=int(flops), bytes_accessed=int(data), transcendentals=0)


def one_hot(rest):
    place = lax.broadcasted_iota(jnp.int32, (BASE, rest.shape[1]), 0).astype(BF)
    return jnp.where(place == rest.astype(F32).astype(BF), jnp.ones((), BF), jnp.zeros((), BF))


def lookup_kernel(ids_ref, table_ref, out_ref, split_ref):
    width = table_ref.shape[0]
    blocks = split_ref.shape[0] // width

    @pl.when(pl.program_id(0) == 0)
    def _():
        for b in range(blocks):
            split_ref[b * width : (b + 1) * width, :] = table_ref[:, b * BASE : (b + 1) * BASE]

    ids = ids_ref[0]
    lead = ids >> 8
    rest = ids & (BASE - 1)
    onehot = one_hot(rest)
    found = dot(split_ref[...].astype(BF), onehot)
    total = jnp.zeros((width, ids.shape[1]), F32)
    for b in range(blocks):
        total = jnp.where(lead == b, found[b * width : (b + 1) * width, :], total)
    out_ref[0] = total.astype(BF)


def lookup(ids, table):
    count, _, tokens = ids.shape
    width, padded = table.shape
    blocks = padded // BASE
    return pl.pallas_call(
        lookup_kernel,
        grid=(count,),
        in_specs=[
            pl.BlockSpec((1, 1, tokens), lambda i: (i, 0, 0)),
            full_spec((width, padded)),
        ],
        out_specs=pl.BlockSpec((1, width, tokens), lambda i: (i, 0, 0)),
        out_shape=shape_of((count, width, tokens), BF),
        scratch_shapes=[pltpu.VMEM((blocks * width, BASE), F32)],
        compiler_params=params(SMALL),
        cost_estimate=cost(
            2 * blocks * width * BASE * tokens * count, 4 * width * padded + 2 * count * width * tokens
        ),
        name="lookup",
    )(ids, table)


def table_grad_kernel(ids_ref, grads_ref, out_ref, square_ref, total_ref):
    count, width, _ = grads_ref.shape
    blocks = total_ref.shape[0] // width
    ids = jnp.concatenate([ids_ref[i] for i in range(count)], 1)
    grads = jnp.concatenate([grads_ref[i].astype(F32) for i in range(count)], 1)
    lead = ids >> 8
    rest = ids & (BASE - 1)
    onehot = one_hot(rest)
    spreads = jnp.concatenate(
        [jnp.where(lead == b, grads, 0.0) for b in range(blocks)], 0
    ).astype(BF)
    part = dot_nt(spreads, onehot)
    step = pl.program_id(0)

    @pl.when(step == 0)
    def _():
        total_ref[...] = part

    @pl.when(step > 0)
    def _():
        total_ref[...] += part

    @pl.when(step == pl.num_programs(0) - 1)
    def _():
        total = jnp.zeros(square_ref.shape, F32)
        for b in range(blocks):
            value = total_ref[b * width : (b + 1) * width, :]
            out_ref[:, b * BASE : (b + 1) * BASE] = value
            for i in range(0, width, 8):
                for j in range(0, BASE, LANES):
                    piece = value[i : i + 8, j : j + LANES]
                    total = total + piece * piece
        square_ref[...] = total


def table_grad(ids, grads, padded):
    count, width, tokens = grads.shape
    blocks = padded // BASE
    group = 8
    return pl.pallas_call(
        table_grad_kernel,
        grid=(count // group,),
        in_specs=[
            pl.BlockSpec((group, 1, tokens), lambda i: (i, 0, 0)),
            pl.BlockSpec((group, width, tokens), lambda i: (i, 0, 0)),
        ],
        out_specs=[full_spec((width, padded)), full_spec((8, LANES))],
        out_shape=[shape_of((width, padded), F32), shape_of((8, LANES), F32)],
        scratch_shapes=[pltpu.VMEM((blocks * width, BASE), F32)],
        compiler_params=params(SMALL),
        cost_estimate=cost(
            2 * blocks * width * BASE * tokens * count, 4 * width * padded + 2 * count * width * tokens
        ),
        name="table_grad",
    )(ids, grads)


def embed(emb_ref, waves_ref, low):
    rows, length = low.shape
    width, tokens = emb_ref.shape
    index = lax.broadcasted_iota(jnp.int32, (1, length), 1)
    places = jnp.concatenate([index - low[r : r + 1, :] for r in range(rows)], 1)
    onehot = (
        lax.broadcasted_iota(jnp.int32, (length, tokens), 0) == places
    ).astype(F32).astype(BF)
    rest = waves_ref[...]
    place = jnp.zeros((tokens, width), F32)
    for _ in range(3):
        term = rest.astype(BF)
        rest = rest - term.astype(F32)
        place = place + dot_tn(onehot, term)
    return math.sqrt(width) * flip(emb_ref[...].astype(F32)) + place


def self_inputs(n1, inward_ref, scale, q_ref, k_ref, v_ref):
    q_ref[...] = (dot(n1, matrix(inward_ref, 0)) * scale).astype(BF)
    k_ref[...] = dot(n1, matrix(inward_ref, 1)).astype(BF)
    v_ref[...] = dot(n1, matrix(inward_ref, 2)).astype(BF)


def self_forward_kernel(
    emb_ref, waves_ref, segments_ref, inward_ref, outward_ref, norms_ref,
    x1_ref, c1_ref, n2_ref, qc_ref, lse_ref, q_ref, k_ref, v_ref,
):
    rows, length = segments_ref.shape
    width = x1_ref.shape[1]
    scale = (width // HEADS) ** (-0.5)
    segments = segments_ref[...]
    low, _ = counts(segments, segments)
    x0 = embed(emb_ref, waves_ref, low)
    norms = norm_rows(norms_ref)
    unit, _ = norm_parts(x0)
    n1 = (unit * norms[0:1, :] + norms[1:2, :]).astype(BF)
    self_inputs(n1, inward_ref, scale, q_ref, k_ref, v_ref)
    high = spread(lax.broadcasted_iota(jnp.int32, (1, length), 1) + 1)
    for r in range(rows):
        span = slice(r * length, (r + 1) * length)
        scores = scores_of(
            k_ref[span, :], head_columns(flip(q_ref[span, :])), spread(low[r : r + 1, :]), high
        )
        probs, logsum = softmax_columns(scores)
        lse_ref[r : r + 1, :] = logsum
        c1_ref[span, :] = flip(
            own_blocks(dot_tn(v_ref[span, :], probs.astype(BF)), length)
        ).astype(BF)
    x1 = x0 + dot(c1_ref[...], matrix(outward_ref, 0))
    x1_ref[...] = x1
    unit, _ = norm_parts(x1)
    n2 = (unit * norms[2:3, :] + norms[3:4, :]).astype(BF)
    n2_ref[...] = n2
    qc_ref[...] = (dot(n2, matrix(inward_ref, 3)) * scale).astype(BF)


def self_forward(emb, waves, segments, stack):
    rows, length = segments.shape
    width, tokens = emb.shape
    thin = shape_of((tokens, width), BF)
    return pl.pallas_call(
        self_forward_kernel,
        in_specs=[
            full_spec(emb.shape), full_spec(waves.shape), full_spec(segments.shape),
            stack_spec(stack, 4, 0), stack_spec(stack, 1, 6), stack_spec(stack, 1, 8),
        ],
        grid=(1,),
        out_specs=[full_spec((tokens, width))] * 4 + [full_spec((rows, HEADS * length))],
        out_shape=[shape_of((tokens, width), F32), thin, thin, thin,
                   shape_of((rows, HEADS * length), F32)],
        scratch_shapes=[pltpu.VMEM((tokens, width), BF)] * 3,
        compiler_params=params(SMALL),
        cost_estimate=cost(2 * tokens * width * width * 8, 8 * tokens * width * 4),
        name="self_forward",
    )(emb, waves, segments, stack, stack, stack)


def pieces_of(part, count):
    early = part // 32 * 16
    return [
        piece
        for i in range(count)
        for piece in ([(i, 0, early), (i, early, part - early)] if i == 2 else [(i, 0, part)])
    ]


def frame_tiles(frames):
    return [(at, min(SPAN, frames - at)) for at in range(0, frames, SPAN)]


def interleave(rows, size, back):
    count = rows * size
    out = lax.broadcasted_iota(jnp.int32, (count, count), 0)
    source = lax.broadcasted_iota(jnp.int32, (count, count), 1)
    inner = rows if back else size
    return (source == (out % inner) * (count // inner) + out // inner).astype(F32).astype(BF)


def cross_forward_kernel(rows, pieces, here_ref, *refs):
    *memory_refs, inward_ref, qc_ref, tokens_ref, frames_ref = refs[:-6]
    c2_ref, held_ref, lse_ref, flat_ref, by_row_ref, sem = refs[-6:]
    row = pl.program_id(0)
    part, width = memory_refs[0].shape
    frames = flat_ref.shape[0] // rows
    length = qc_ref.shape[0]

    @pl.when(row == 0)
    def _():
        copies = []
        for j, ((i, at, size), ref) in enumerate(zip(pieces, memory_refs)):
            start = pl.multiple_of((here_ref[0] ^ i) * part + at, 16)
            copies.append(
                pltpu.make_async_copy(ref, flat_ref.at[pl.ds(start, size), :], sem.at[j])
            )
        for copy in copies:
            copy.start()
        for copy in copies:
            copy.wait()
        turns = {size: interleave(rows, size, False) for _, size in frame_tiles(frames)}
        for at, size in frame_tiles(frames):
            block = dot(turns[size], flat_ref[at * rows : (at + size) * rows, :]).astype(BF)
            for r in range(rows):
                by_row_ref[r, at : at + size, :] = block[r * size : (r + 1) * size, :]

    memory = by_row_ref[row]
    held_ref[0] = memory
    keys = dot(memory, matrix(inward_ref, 0)).astype(BF)
    values = dot(memory, matrix(inward_ref, 1)).astype(BF)
    low, high = counts(frames_ref[pl.ds(row, 1), :], tokens_ref[pl.ds(row, 1), :])
    scores = scores_of(keys, head_columns(flip(qc_ref[...])), spread(low), spread(high))
    probs, logsum = softmax_columns(scores)
    lse_ref[0] = logsum
    c2_ref[...] = flip(own_blocks(dot_tn(values, probs.astype(BF)), length)).astype(BF)


def cross_forward(here, memory, stack, query, tokens, frame_segments):
    rows, length = tokens.shape
    part, width = memory[0].shape
    pieces = pieces_of(part, sum(a.shape[0] for a in memory) // part)
    total = sum(size for _, _, size in pieces)
    frames = total // rows
    block = pl.BlockSpec((length, width), lambda i: (i, 0))
    return pl.pallas_call(
        functools.partial(cross_forward_kernel, rows, pieces),
        grid=(rows,),
        in_specs=[
            pl.BlockSpec(memory_space=pltpu.SMEM),
            *[pl.BlockSpec(memory_space=pltpu.HBM)] * len(memory),
            stack_spec(stack, 2, 4), block, full_spec(tokens.shape),
            full_spec(frame_segments.shape),
        ],
        out_specs=[
            block, pl.BlockSpec((1, frames, width), lambda i: (i, 0, 0)),
            pl.BlockSpec((1, 1, HEADS * length), lambda i: (i, 0, 0)),
        ],
        out_shape=[
            shape_of((rows * length, width), BF),
            shape_of((rows, frames, width), BF),
            shape_of((rows, 1, HEADS * length), F32),
        ],
        scratch_shapes=[
            pltpu.VMEM((total, width), BF), pltpu.VMEM((rows, frames, width), BF),
            pltpu.SemaphoreType.DMA((len(memory),)),
        ],
        compiler_params=params(SMALL),
        cost_estimate=cost(
            2 * total * width * 2 * width + 4 * total * length * HEADS * width, 6 * total * width
        ),
        name="cross_forward",
    )(here, *memory, stack, query, tokens, frame_segments)


def feed_kernel(
    packed, x1_ref, c2_ref, outward_ref, norms_ref, expand_ref, shrink_ref, cot_ref,
    out_ref, dx2_ref, gff_ref, gnorm_ref, total_ref, dn_ref,
):
    parts, owners = gff_ref.shape[0], gff_ref.shape[1]
    blocks = expand_ref.shape[1] // parts
    groups = shrink_ref.shape[0] // parts
    norms = norm_rows(norms_ref)
    x2 = x1_ref[...] + dot(c2_ref[...], matrix(outward_ref, 0))
    width = x2.shape[1]
    unit, inverse = norm_parts(x2)
    gain = norms[4:5, :]
    n3 = (unit * gain + norms[5:6, :]).astype(BF)
    n3_flipped = flip(n3)
    cot = cot_ref[...]
    cot_flipped = flip(cot)
    total_ref[...] = x2
    first = math.sqrt(2.0 / math.pi)
    for j in range(parts):
        expand = jnp.concatenate([matrix(expand_ref, j * blocks + b) for b in range(blocks)], 1)
        shrink = shrink_ref[j * groups : (j + 1) * groups].reshape(-1, width)
        chunk = shrink.shape[0]
        before = dot(n3, expand)
        square = before * before
        tanh = jnp.tanh(before * (first + (first * 0.044715) * square))
        half = 0.5 * before
        wing = 0.5 + 0.5 * tanh
        active = (before * wing).astype(BF)
        slope = wing + half * (1.0 - tanh * tanh) * (first + (3.0 * first * 0.044715) * square)
        grad = (dot_nt(cot, shrink) * slope).astype(BF)
        total_ref[...] += dot(active, shrink)
        gexp = dot(n3_flipped, grad).astype(BF)
        gshr = flip(dot(cot_flipped, active)).astype(BF)
        share = chunk * parts // (parts * owners)
        if packed:
            rows = width // owners
            for o in range(chunk // (share * parts)):
                for q in range(parts):
                    at = (o * parts + q) * share
                    owner = j * (chunk // (share * parts)) + o
                    gff_ref[q, owner, 0:share, :] = gshr[at : at + share, :]
            for b in range(chunk // width):
                for o in range(owners):
                    gff_ref[j, o, share + b * rows : share + (b + 1) * rows, :] = gexp[
                        o * rows : (o + 1) * rows, b * width : (b + 1) * width
                    ]
        else:
            gff_ref[j, 0, 0:chunk, :] = gshr
            for b in range(chunk // width):
                gff_ref[j, 0, chunk + b * width : chunk + (b + 1) * width, :] = gexp[
                    :, b * width : (b + 1) * width
                ]
        back = dot_nt(grad, expand)
        if j == 0:
            dn_ref[...] = back
        else:
            dn_ref[...] += back
    out_ref[...] = total_ref[...].astype(BF)
    grad, both = norm_back(dn_ref[...], unit, inverse, gain)
    dx2_ref[...] = cot.astype(F32) + grad
    gnorm_ref[...] = both


def feed(x1, c2, stack, wide, cot, parts, owners):
    tokens, width = x1.shape
    groups, blocks, rows, _ = wide.shape
    blocks //= 2
    hidden = groups * blocks * rows
    packed = width // owners % 16 == 0 and hidden // (parts * owners) % 16 == 0
    shape = (parts, owners if packed else 1, 2 * hidden // (parts * (owners if packed else 1)), width)
    result = pl.pallas_call(
        functools.partial(feed_kernel, packed),
        grid=(1,),
        in_specs=[
            full_spec(x1.shape), full_spec(c2.shape), stack_spec(stack, 1, 7),
            stack_spec(stack, 1, 8), stack_spec(wide, blocks, 0), stack_spec(wide, blocks, blocks),
            full_spec(cot.shape),
        ],
        out_specs=[
            full_spec((tokens, width)), full_spec((tokens, width)), full_spec(shape),
            full_spec((2, width)),
        ],
        out_shape=[
            shape_of((tokens, width), BF), shape_of((tokens, width), F32), shape_of(shape, BF),
            shape_of((2, width), F32),
        ],
        scratch_shapes=[pltpu.VMEM((tokens, width), F32), pltpu.VMEM((tokens, width), F32)],
        compiler_params=params(TIGHT),
        cost_estimate=cost(12 * tokens * width * hidden, 12 * width * hidden),
        name="feed",
    )(x1, c2, stack, stack, wide, wide, cot)
    out, dx2, gff, gnorm = result
    if not packed:
        chunk = hidden // parts
        gshr = gff[:, 0, :chunk].reshape(owners, parts, hidden // (parts * owners), width)
        gexp = gff[:, 0, chunk:].reshape(parts, chunk // width, owners, width // owners, width)
        gff = jnp.concatenate(
            [
                gshr.transpose(1, 0, 2, 3),
                gexp.transpose(0, 2, 1, 3, 4).reshape(parts, owners, -1, width),
            ],
            2,
        )
    return out, dx2, gff, gnorm


def cross_backward_kernel(
    rows, pieces, here_ref, dx2_ref, c2_ref, outward_ref, qc_ref, held_ref, lse_ref, tokens_ref,
    frames_ref, n2_ref, x1_ref, inward_ref, norms_ref, *refs,
):
    frame_refs = refs[: len(pieces)]
    dx1_ref, gweight_ref, gnorm_ref, dc_ref, dq_ref, flat_ref, by_row_ref = refs[len(pieces) :]
    row = pl.program_id(0)
    part, width = frame_refs[0].shape
    frames = flat_ref.shape[0] // rows
    length = qc_ref.shape[0]
    scale = (width // HEADS) ** (-0.5)

    @pl.when(row == 0)
    def _():
        rounded = dx2_ref[...].astype(BF)
        gweight_ref[3] = dot_tn(c2_ref[...], rounded)
        dc_ref[...] = dot_nt(rounded, matrix(outward_ref, 0)).astype(BF)
        gweight_ref[1] = jnp.zeros((width, width), F32)
        gweight_ref[2] = jnp.zeros((width, width), F32)

    span = pl.ds(pl.multiple_of(row * length, length), length)
    low, high = counts(frames_ref[pl.ds(row, 1), :], tokens_ref[pl.ds(row, 1), :])
    key_weight, value_weight = matrix(inward_ref, 1), matrix(inward_ref, 2)
    memory = held_ref[0]
    keys = dot(memory, key_weight).astype(BF)
    values = dot(memory, value_weight).astype(BF)
    dquery, dkeys, dvalues = attention_back(
        keys, values, qc_ref[...], dc_ref[span, :], spread(low), spread(high), lse_ref[0]
    )
    dq_ref[span, :] = dquery.astype(BF)
    dkeys, dvalues = dkeys.astype(BF), dvalues.astype(BF)
    gweight_ref[1] += dot_tn(memory, dkeys)
    gweight_ref[2] += dot_tn(memory, dvalues)
    by_row_ref[row] = (dot_nt(dkeys, key_weight) + dot_nt(dvalues, value_weight)).astype(BF)

    @pl.when(row == rows - 1)
    def _():
        turns = {size: interleave(rows, size, True) for _, size in frame_tiles(frames)}
        for at, size in frame_tiles(frames):
            block = jnp.concatenate([by_row_ref[r, at : at + size, :] for r in range(rows)], 0)
            flat_ref[at * rows : (at + size) * rows, :] = dot(turns[size], block).astype(BF)
        for (i, at, size), ref in zip(pieces, frame_refs):
            start = pl.multiple_of((here_ref[0] ^ i) * part + at, 16)
            ref[...] = flat_ref[pl.ds(start, size), :]
        dq = dq_ref[...]
        gweight_ref[0] = dot_tn(n2_ref[...], dq) * scale
        unit, inverse = norm_parts(x1_ref[...])
        grad, both = norm_back(
            dot_nt(dq, matrix(inward_ref, 0)) * scale, unit, inverse, norm_rows(norms_ref)[2:3, :]
        )
        dx1_ref[...] = dx2_ref[...] + grad
        gnorm_ref[...] = both


def cross_backward(here, dx2, c2, query, held, logsum, segments, frame_segments, n2, x1, stack, count):
    rows, length = segments.shape
    _, frames, width = held.shape
    total = rows * frames
    tokens = rows * length
    pieces = pieces_of(total // count, count)
    block = pl.BlockSpec((length, width), lambda i: (i, 0))
    return pl.pallas_call(
        functools.partial(cross_backward_kernel, rows, pieces),
        grid=(rows,),
        in_specs=[
            pl.BlockSpec(memory_space=pltpu.SMEM), full_spec(dx2.shape), full_spec(c2.shape),
            stack_spec(stack, 1, 7), block, pl.BlockSpec((1, frames, width), lambda i: (i, 0, 0)),
            pl.BlockSpec((1, 1, HEADS * length), lambda i: (i, 0, 0)), full_spec(segments.shape),
            full_spec(frame_segments.shape), full_spec(n2.shape), full_spec(x1.shape),
            stack_spec(stack, 3, 3), stack_spec(stack, 1, 8),
        ],
        out_specs=[
            *[full_spec((size, width)) for _, _, size in pieces], full_spec((tokens, width)),
            full_spec((4, width, width)), full_spec((2, width)),
        ],
        out_shape=[
            *[shape_of((size, width), BF) for _, _, size in pieces], shape_of((tokens, width), F32),
            shape_of((4, width, width), F32), shape_of((2, width), F32),
        ],
        scratch_shapes=[
            pltpu.VMEM((tokens, width), BF), pltpu.VMEM((tokens, width), BF),
            pltpu.VMEM((total, width), BF), pltpu.VMEM((rows, frames, width), BF),
        ],
        compiler_params=params(TIGHT),
        cost_estimate=cost(
            2 * total * width * 4 * width + 10 * total * length * HEADS * width, 8 * total * width
        ),
        name="cross_backward",
    )(here, dx2, c2, stack, query, held, logsum, segments, frame_segments, n2, x1, stack, stack)


def self_backward_kernel(
    dx1_ref, c1_ref, outward_ref, lse_ref, segments_ref, emb_ref, waves_ref,
    inward_ref, norms_ref, dt_ref, gweight_ref, gnorm_ref,
    dc_ref, dq_ref, dk_ref, dv_ref, q_ref, k_ref, v_ref,
):
    rows, length = segments_ref.shape
    width = dx1_ref.shape[1]
    scale = (width // HEADS) ** (-0.5)
    low, _ = counts(segments_ref[...], segments_ref[...])
    x0 = embed(emb_ref, waves_ref, low)
    norms = norm_rows(norms_ref)
    unit, inverse = norm_parts(x0)
    n1 = (unit * norms[0:1, :] + norms[1:2, :]).astype(BF)
    self_inputs(n1, inward_ref, scale, q_ref, k_ref, v_ref)
    dx1 = dx1_ref[...]
    rounded = dx1.astype(BF)
    gweight_ref[3] = dot_tn(c1_ref[...], rounded)
    dc_ref[...] = dot_nt(rounded, matrix(outward_ref, 0)).astype(BF)
    high = spread(lax.broadcasted_iota(jnp.int32, (1, length), 1) + 1)
    for r in range(rows):
        span = slice(r * length, (r + 1) * length)
        dquery, dkeys, dvalues = attention_back(
            k_ref[span, :], v_ref[span, :], q_ref[span, :], dc_ref[span, :],
            spread(low[r : r + 1, :]), high, lse_ref[r : r + 1, :],
        )
        dq_ref[span, :] = dquery.astype(BF)
        dk_ref[span, :] = dkeys.astype(BF)
        dv_ref[span, :] = dvalues.astype(BF)
    flipped = flip(n1)
    gweight_ref[0] = dot(flipped, dq_ref[...]) * scale
    gweight_ref[1] = dot(flipped, dk_ref[...])
    gweight_ref[2] = dot(flipped, dv_ref[...])
    upstream = (
        dot_nt(dq_ref[...], matrix(inward_ref, 0)) * scale
        + dot_nt(dk_ref[...], matrix(inward_ref, 1))
        + dot_nt(dv_ref[...], matrix(inward_ref, 2))
    )
    grad, both = norm_back(upstream, unit, inverse, norms[0:1, :])
    gnorm_ref[...] = both
    dt_ref[...] = flip(math.sqrt(width) * (dx1 + grad)).astype(BF)


def self_backward(dx1, c1, logsum, segments, emb, waves, stack):
    tokens, width = dx1.shape
    ins = (dx1, c1, logsum, segments, emb, waves)
    specs = [full_spec(a.shape) for a in ins]
    return pl.pallas_call(
        self_backward_kernel,
        grid=(1,),
        in_specs=specs[:2] + [stack_spec(stack, 1, 6)] + specs[2:]
        + [stack_spec(stack, 3, 0), stack_spec(stack, 1, 8)],
        out_specs=[full_spec((width, tokens)), full_spec((4, width, width)), full_spec((2, width))],
        out_shape=[
            shape_of((width, tokens), BF), shape_of((4, width, width), F32),
            shape_of((2, width), F32),
        ],
        scratch_shapes=[pltpu.VMEM((tokens, width), BF)] * 7,
        compiler_params=params(ROOMY),
        cost_estimate=cost(2 * tokens * width * width * 12, 8 * tokens * width * 4),
        name="self_backward",
    )(*ins[:2], stack, *ins[2:], stack, stack)


def bits_of(count):
    return count.bit_length() - 1


def swap(values, axis, bit, count):
    return lax.ppermute(values, axis, [(i, i ^ (1 << bit)) for i in range(count)])


def side(axis, bit):
    return (lax.axis_index(axis) >> bit) & 1


def halve(values, dim, axis, bit, count):
    mine = side(axis, bit)
    keep = lax.dynamic_index_in_dim(values, mine, dim, keepdims=False)
    send = lax.dynamic_index_in_dim(values, 1 - mine, dim, keepdims=False).astype(BF)
    return keep.astype(F32) + swap(send, axis, bit, count).astype(F32)


def halve_send(values, dim, axis, bit, count):
    mine = side(axis, bit)
    keep = lax.dynamic_index_in_dim(values, mine, dim, keepdims=False)
    send = lax.dynamic_index_in_dim(values, 1 - mine, dim, keepdims=False).astype(BF)
    return keep, swap(send, axis, bit, count)


def both_halves(values, dim, axis, bit, count):
    return in_order(values, swap(values, axis, bit, count), dim, axis, bit)


def in_order(values, other, dim, axis, bit):
    mine = side(axis, bit) == 0
    return jnp.stack([jnp.where(mine, values, other), jnp.where(mine, other, values)], dim)


def quarter_sum(values, m):
    here = lax.axis_index("seq")
    pieces = [lax.dynamic_index_in_dim(values, here ^ i, 0, keepdims=False) for i in range(m)]
    pieces = [
        (lax.ppermute(a.astype(BF), "seq", [(p, p ^ i) for p in range(m)]) if i else a).astype(F32)
        for i, a in enumerate(pieces)
    ]
    return functools.reduce(jnp.add, pieces)


def gather_all(values, axis, bits, count, beside=None):
    size, low_bit = 1 << len(bits), bits[0]
    mine = (lax.axis_index(axis) >> low_bit) & (size - 1)
    pieces = [values] + [
        lax.ppermute(values, axis, [(p, p ^ (i << low_bit)) for p in range(count)])
        for i in range(1, size)
    ]
    if beside is not None:
        beside, *pieces = tie((beside, *pieces))
    pieces = jnp.stack(pieces)
    ordered = jnp.stack(
        [lax.dynamic_index_in_dim(pieces, mine ^ i, 0, keepdims=False) for i in range(size)]
    )
    return ordered if beside is None else (ordered, beside)


tie = lax.optimization_barrier


def mark_kernel(source_ref, small_ref, out_ref):
    del source_ref
    out_ref[...] = small_ref[...]


def mark(source, small, *later):
    small = pl.pallas_call(
        mark_kernel,
        in_specs=[pl.BlockSpec(memory_space=pl.ANY), pl.BlockSpec(memory_space=pltpu.VMEM)],
        out_specs=pl.BlockSpec(memory_space=pltpu.VMEM),
        out_shape=shape_of(small.shape, small.dtype),
        compiler_params=pltpu.CompilerParams(vmem_limit_bytes=1024 * 1024),
        cost_estimate=cost(0, 100e6),
        name="mark",
    )(source, small)
    return tie((small, *later))


def regroup(values, rows):
    groups, count, part, width = values.shape
    return (
        values.transpose(1, 0, 2, 3).reshape(count, groups * part // rows, rows, width)
        .transpose(1, 0, 2, 3)
    )


def own_half(values, dim):
    half = values.shape[dim] // 2
    return lax.dynamic_slice_in_dim(values, side("seq", 0) * half, half, dim)


def encode(place, width):
    halves = jnp.arange(width // 2, dtype=F32)
    freq = jnp.exp(halves * (-2.0 * math.log(10000.0) / width))
    angle = place[..., None] * freq
    return jnp.stack([jnp.sin(angle), jnp.cos(angle)], -1).reshape(place.shape + (width,))


def assemble_kernel(pieces, here_ref, *refs):
    out_ref = refs[-1]
    for (i, at, size), ref in zip(pieces, refs):
        out_ref[pl.ds(at, size), pl.ds(here_ref[0] ^ i, 1)] = ref[...][:, None]


def assemble(here, pieces, count):
    frames, rows, width = pieces[0].shape
    places = [(i, at // rows, size // rows) for i, at, size in pieces_of(frames * rows, count)]
    return pl.pallas_call(
        functools.partial(assemble_kernel, places),
        grid=(1,),
        in_specs=[pl.BlockSpec(memory_space=pltpu.SMEM)] + [full_spec(a.shape) for a in pieces],
        out_specs=full_spec((frames, count, rows, width)),
        out_shape=shape_of((frames, count, rows, width), pieces[0].dtype),
        compiler_params=params(TIGHT),
        cost_estimate=cost(0, 4 * count * frames * rows * width),
        name="assemble",
    )(here, *pieces)


def square_kernel(part_ref, dense_ref, out_ref):
    dense = dense_ref[...]
    dense = dense * dense
    total = part_ref[...]
    for i in range(dense.shape[0] // 8):
        for j in range(dense.shape[1] // LANES):
            total = total + dense[i * 8 : (i + 1) * 8, j * LANES : (j + 1) * LANES]
    for i in range(out_ref.shape[0]):
        out_ref[i] = total


def square_blocks(part, dense, count):
    return pl.pallas_call(
        square_kernel,
        grid=(1,),
        in_specs=[full_spec(part.shape), full_spec(dense.shape)],
        out_specs=full_spec((count, 8, LANES)),
        out_shape=shape_of((count, 8, LANES), F32),
        compiler_params=params(TIGHT),
        cost_estimate=cost(dense.size, 4 * dense.size),
        name="square_blocks",
    )(part, dense)


def adam_kernel(squares_ref, gtable_ref, dense_ref, *refs):
    masters, firsts, seconds = refs[0:6], refs[6:12], refs[12:18]
    norm_ref, outs = refs[18], refs[19:]
    total = jnp.sum(jnp.sum(squares_ref[...], 0), keepdims=True)
    norm = jnp.sqrt(total)
    norm_ref[...] = norm
    factor = CLIP / jnp.maximum(norm, CLIP)
    parts, _, width = dense_ref.shape
    share = masters[5].shape[1]
    part = masters[1].shape[1]
    hidden = masters[3].shape[1]
    cut = masters[4].shape[0] // parts
    late = dense_ref.shape[1] - 2 * part - 8

    def update(i, at, gradient, rate):
        first_m = 1.0 / (1 - BETA_ONE**STEP)
        first_s = 1.0 / (1 - BETA_TWO**STEP)
        clipped = gradient * factor
        moment = BETA_ONE * firsts[i][at] + (1 - BETA_ONE) * clipped
        square = BETA_TWO * seconds[i][at] + (1 - BETA_TWO) * clipped * clipped
        master = masters[i][at]
        weight = master - rate * (
            (moment * first_m) / (jnp.sqrt(square * first_s) + ADAM_EPS) + DECAY * master
        )
        for ref, value in zip(outs[5 * i : 5 * i + 5], (clipped, moment, square, weight, weight)):
            ref[at] = value.astype(ref.dtype)

    everything = (slice(None), slice(None))
    update(0, everything, gtable_ref[:, 0 : masters[0].shape[1]], RATE)
    for i in range(parts):
        for a in range(2):
            gradient = dense_ref[i, late + a * part : late + (a + 1) * part, :]
            if i < 3:
                update(1, (3 - 3 * a + i, slice(None), slice(None)), gradient, RATE)
            else:
                update(2, (1 - a, slice(None), slice(None)), gradient, RATE)
        blocks = hidden // (parts * width)
        for b in range(blocks):
            at = (i * blocks + b) * width
            update(
                3, (slice(None), slice(at, at + width)),
                dense_ref[i, cut + b * part : cut + (b + 1) * part, :], RATE,
            )
        update(4, (slice(i * cut, (i + 1) * cut), slice(None)), dense_ref[i, 0:cut, :], RATE)
    update(5, everything, dense_ref[0, late + 2 * part : late + 2 * part + 6, 0:share], NORM_RATE)


def adam(squares, gtable, dense, state):
    shapes = [shape_of((1, 1), F32)] + [
        shape_of(a.shape, kind) for a in state[:6] for kind in (F32, F32, F32, F32, BF)
    ]
    ins = (squares, gtable, dense, *state)
    norm, *results = pl.pallas_call(
        adam_kernel,
        grid=(1,),
        in_specs=[full_spec(a.shape) for a in ins],
        out_specs=[full_spec(a.shape) for a in shapes],
        out_shape=shapes,
        compiler_params=params(ROOMY),
        cost_estimate=cost(0, 34 * sum(a.size for a in state[:6])),
        name="adam",
    )(*ins)
    return norm, results


def body(n, m, *args):
    masters, firsts, seconds = args[0:6], args[6:12], args[12:18]
    memory, token_ids, dec_segments, mem_segments, cotangent = args[18:23]
    table_master, inward_master, outward_master, expand_master, shrink_master, norms_master = masters
    rates = (RATE, RATE, RATE, RATE, RATE, NORM_RATE)
    rows, length = token_ids.shape
    tokens = rows * length
    vocab, share = table_master.shape
    width = inward_master.shape[2]
    hidden = expand_master.shape[1]
    part = inward_master.shape[1]
    frames = mem_segments.shape[1]
    padded = -(-vocab // (2 * BASE)) * 2 * BASE

    copies = jnp.broadcast_to(token_ids[None], (n * m, rows, length))
    ids = lax.all_to_all(copies, ("dp", "seq"), 0, 0).reshape(n * m, 1, tokens)
    norms_now, inward_now, outward_now, memory = mark(
        copies, norms_master, inward_master, outward_master, memory
    )

    here = lax.axis_index("seq")
    flipped = memory.transpose(1, 0, 2).reshape(frames // m, m, rows, width)
    routes = pieces_of(frames // m * rows, m)

    def frames_from(source, route):
        i, at, size = route
        own = lax.dynamic_index_in_dim(source, here ^ i, 1, keepdims=False)
        own = own.reshape(-1, width)[at : at + size]
        return lax.ppermute(own, "seq", [(p, p ^ i) for p in range(m)]) if i else own

    first_piece, second_piece = frames_from(flipped, routes[2]), frames_from(flipped, routes[3])
    line_ids = lax.dynamic_index_in_dim(
        ids.reshape(n, m, 1, tokens), here, 1, keepdims=False
    )

    norm_block = lax.dynamic_update_slice(
        jnp.zeros((1, max(part, 16), width), F32), norms_now[None],
        (0, 0, lax.axis_index("dp") * share),
    )
    blocks = own_half(jnp.concatenate([inward_now, outward_now], 0), 1)
    if part == 32:
        blocks = jnp.concatenate([blocks, own_half(norm_block, 1)], 0)
    upper = list(range(1, bits_of(n)))
    narrow = gather_all(blocks.astype(BF), "dp", upper[:2], n)
    table_flipped = jnp.pad(table_master.T, ((0, -share % 8), (0, padded - vocab)))

    wide = jnp.concatenate(
        [
            own_half(expand_master, 0).reshape(part // 2, hidden // width, width).transpose(1, 0, 2),
            own_half(shrink_master, 0).reshape(hidden // width, part // 2, width),
        ],
        0,
    )
    wide = wide.astype(BF)
    found = lookup(line_ids, table_flipped)[:, :share]
    narrow = both_halves(narrow, 1, "dp", 0, n)
    wide, found = gather_all(wide, "dp", upper[:2], n, found)
    found, narrow, first_piece = tie((found, narrow, first_piece))
    emb = lax.all_to_all(found, "dp", 0, 0).reshape(width, tokens)
    if upper[2:]:
        narrow = gather_all(narrow, "dp", upper[2:], n)
        narrow = narrow.reshape((-1,) + narrow.shape[2:])
    other = swap(narrow, "seq", 0, m)
    narrow, other, second_piece, flipped = tie((narrow, other, second_piece, flipped))
    narrow = in_order(narrow, other, 2, "seq", 0)
    mem_rows = [
        (first_piece, second_piece)[j - 2] if j in (2, 3) else frames_from(flipped, r)
        for j, r in enumerate(routes)
    ]
    here = here.reshape(1).astype(jnp.int32)

    waves = encode(jnp.arange(length).astype(F32), width)
    stack = narrow.reshape((2 * n,) + narrow.shape[3:])
    if part != 32:
        norms = lax.psum(norm_block[:, :16].astype(BF).astype(F32), "dp").astype(BF)
        stack = regroup(stack, 16)
        norms = jnp.pad(norms[None], ((0, stack.shape[0] - 1), (0, 0), (0, 0), (0, 0)))
        stack = jnp.concatenate([stack, norms], 1)

    x1, c1, n2, qc, lse1 = self_forward(emb, waves, dec_segments, stack)
    if upper[2:]:
        wide = gather_all(wide, "dp", upper[2:], n)
        wide = wide.reshape((-1,) + wide.shape[2:])
    along = swap(wide, "dp", 0, n)
    lse1, along, dec_segments = tie((lse1, along, dec_segments))
    wide = in_order(wide, along, 1, "dp", 0)
    across = swap(wide, "seq", 0, m)
    c2, held, lse2 = cross_forward(here, mem_rows, stack, qc, dec_segments, mem_segments)
    lse2, across = tie((lse2, across))
    wide = in_order(wide, across, 2, "seq", 0)
    wide = wide.reshape((2 * n,) + wide.shape[3:])
    if part != 32:
        count = hidden // width
        shrink = wide[:, count:].reshape(width // 16, count, 16, width)
        wide = jnp.concatenate([regroup(wide[:, :count], 16), shrink], 1)
    block_out, dx2, gff, gnorm3 = feed(
        x1, c2, stack, wide, cotangent.reshape(tokens, width), m, n
    )
    *frame, dx1, gcross, gnorm2 = cross_backward(
        here, dx2, c2, qc, held, lse2, dec_segments, mem_segments, n2, x1, stack, m
    )
    gff = quarter_sum(gff, m)
    dx1, gff = tie((dx1, gff))
    frame = [
        lax.ppermute(a, "seq", [(p, p ^ i) for p in range(m)]) if i else a
        for (i, _, _), a in zip(routes, frame)
    ]
    dt, gself, gnorm1 = self_backward(dx1, c1, lse1, dec_segments, emb, waves, stack)
    cut = gff.shape[1]
    early = jnp.concatenate(
        [gff, gcross.reshape(m, n, part, width).transpose(1, 0, 2, 3).reshape(n, -1, width)], 1
    )
    early = early.reshape((2,) * bits_of(n) + early.shape[1:])
    kept, came = halve_send(early, bits_of(n) - 1, "dp", 0, n)
    dt, came, frame[2], gself, gnorm1 = tie((dt, came, frame[2], gself, gnorm1))
    early = kept.astype(F32) + came.astype(F32)

    few = share // m
    arrived = lax.all_to_all(dt.reshape(n * m, few, tokens), ("dp", "seq"), 0, 0)
    arrived = jnp.pad(arrived, ((0, 0), (0, -few % 8), (0, 0)))

    gnorm = jnp.concatenate([gnorm1, gnorm2, gnorm3], 0)
    gnorm = jnp.pad(
        gnorm.reshape(6, n, share).transpose(1, 0, 2)[:, None],
        ((0, 0), (0, m - 1), (0, 2), (0, width - share)),
    )
    late = jnp.concatenate(
        [gself.reshape(m, n, part, width).transpose(1, 0, 2, 3), gnorm], 2
    )
    late = late.reshape((2,) * bits_of(n) + (-1, width))
    late = halve(late, bits_of(n) - 1, "dp", 0, n)
    early = halve(early, early.ndim - 3, "dp", 1, n)
    arrived, late, early = tie((arrived, late, early))
    gtable, squares = table_grad(ids, arrived, padded)
    late = halve(late, late.ndim - 3, "dp", 1, n)
    for bit in range(2, bits_of(n)):
        early = halve(early, early.ndim - 3, "dp", bit, n)
    gtable, late, early, *frame = tie((gtable, late, early, *frame))
    for bit in range(2, bits_of(n)):
        late = halve(late, late.ndim - 3, "dp", bit, n)
    returned = assemble(here, [a.reshape(-1, rows, width) for a in frame], m)
    returned = returned.reshape(frames // m, m * rows, width).transpose(1, 0, 2)
    late_sum = quarter_sum(
        jnp.concatenate(
            [early[cut:].reshape(m, part, width), late.reshape(m, -1, width)], 1
        ), m,
    )
    dense = jnp.concatenate([early[:cut], late_sum], 0)
    squares = square_blocks(squares, dense, n * m)
    squares = lax.all_to_all(squares, ("dp", "seq"), 0, 0)

    gtable = gtable[:few]
    for i, bit in enumerate(reversed(range(bits_of(m)))):
        gtable = both_halves(gtable, i, "seq", bit, m)
    gtable = gtable.reshape(share, padded)
    dense = both_halves(dense, 0, "seq", 1, m)
    dense = both_halves(dense, 1, "seq", 0, m).reshape(m, -1, width)
    grad_norm, results = adam(
        squares, gtable, dense,
        [(a.T if i == 0 else a) for group in (masters, firsts, seconds) for i, a in enumerate(group)],
    )
    results = [(a.T if i < 5 else a) for i, a in enumerate(results)]
    return (block_out.reshape(rows, length, width), returned, grad_norm.reshape(()), *results)


def solution(mesh):
    n, m = mesh.shape["dp"], mesh.shape["seq"]
    state = (
        P(None, "dp"), P(None, "dp", None), P(None, "dp", None),
        P("dp", None), P("dp", None), P(None, "dp"),
    )
    flat = P(("dp", "seq"), None)
    deep = P(("dp", "seq"), None, None)
    in_specs = state * 3 + (P("dp", "seq", None), flat, flat, flat, deep)
    out_specs = (deep, P("dp", "seq", None), P()) + tuple(s for s in state for _ in range(5))
    return jax.shard_map(
        functools.partial(body, n, m), mesh=mesh, in_specs=in_specs, out_specs=out_specs, check_vma=False
    )
```
